128 devices in a mesh: rows: 8 (over x_hi, y), cols: 16 (over z, x_lo, core).
Axes of the slice: x: 4 (x_hi: 2, x_lo: 2; x = x_hi * 2 + x_lo), y: 4, z: 4, core: 2. Of those that a mesh axis runs over, the one named last changes fastest.
Arguments:
- features: bfloat16 [2048, 512], P(('rows', 'cols')), may hold values from -6 to 6
- tower_weight: bfloat16 [2, 3, 512, 512], replicated, may hold values from -0.15625 to 0.15625
- tower_bias: float32 [2, 512], replicated, may hold values from -0.5 to 0.5
- pair_proj: bfloat16 [512, 64], replicated, may hold values from -0.25 to 0.25
- dist_gain: float32 [32], replicated, may hold values from -1 to 1
- map_weight: bfloat16 [3, 3, 3, 32, 32], replicated, may hold values from -0.375 to 0.375
- map_bias: float32 [3, 32], replicated, may hold values from -0.5 to 0.5
- dilations: int32 [5], replicated, may hold values from 1 to 16, as said below
- start_bin: int32 [1], replicated, may hold values from 0 to 99999
Outputs:
- pair_map: bfloat16 [32, 2048, 2048], P(None, 'rows', 'cols')
The draws below stay inside these ranges and needn't reach their ends.
Inputs may be any that keep to these rules, and one draw needn't show every extreme that they name: `dilations`: the first 2 entries lie in 1 to 16 and at least one equals 16; the last 3 lie in 1 to 16 and at least one equals 16.
All inputs are finite; a program needn't handle non-finite values.
Results may differ from the reference program's by a relative error of at most 0.013.
Values may be sent and summed in bfloat16 or wider, within the bound.
No kernel may reach another device: no remote copies, remote signals or barrier semaphores. Data moves between devices by JAX's collectives and lax.ppermute only.
A program may use at most 192 MiB of HBM per device.

```python
import math
import jax
import jax.numpy as jnp
from jax import lax

C1 = 512
C2 = 32
K1 = 2
K2 = 3
DMAX1 = 16
DMAX2 = 16
L = 2048
TILE_R = 256


def draw_dilations(key, part):
    key = jax.random.fold_in(key, 7)
    keys = jax.random.split(key, 4)
    first = jax.random.randint(keys[0], (K1,), 1, DMAX1 + 1)
    chosen = jax.random.randint(keys[1], (), 0, K1)
    first = jnp.where(jnp.arange(K1) == chosen, DMAX1, first)
    second = jax.random.randint(keys[2], (K2,), 1, DMAX2 + 1)
    picked = jax.random.randint(keys[3], (), 0, K2)
    second = jnp.where(jnp.arange(K2) == picked, DMAX2, second)
    return jnp.concatenate([first, second]).astype(jnp.int32)


def level_of(rng, extent, pieces, smallest, high):
    def one(dim, blocks):
        draws = jax.random.uniform(jax.random.fold_in(jax.random.fold_in(rng, 6), dim), (blocks,), jnp.float32, smallest / len(pieces), high / len(pieces))
        return jnp.repeat(jnp.exp(draws), extent[dim] // blocks).reshape((-1,) + (1,) * (len(extent) - dim - 1))

    factor_of = one(*pieces[0])
    for cut in pieces[1:]:
        factor_of = factor_of * one(*cut)
    return factor_of


def gaussian(stream_key, extent, spread, limit, cuts=(), held_as=jnp.bfloat16):
    result = spread * jax.random.normal(stream_key, extent, jnp.float32)
    if cuts:
        result = result * level_of(stream_key, extent, cuts, -0.22, 0.18)
    return jnp.clip(result, -limit, limit).astype(held_as)


def setup_inputs(seed: int = 0) -> dict:
    arg_keys = jax.random.split(jax.random.key(seed), 10)
    return {
        "features": gaussian(arg_keys[0], (L, C1), 1.0, 6.0, ((0, 128),)),
        "tower_weight": gaussian(arg_keys[1], (K1, 3, C1, C1), (3 * C1) ** -0.5, 0.15625),
        "tower_bias": jnp.clip(jax.random.uniform(arg_keys[2], (K1, C1), jnp.float32, -0.5, 0.5), -0.5, 0.5),
        "pair_proj": gaussian(arg_keys[3], (C1, 2 * C2), C1 ** -0.5, 0.25),
        "dist_gain": jnp.clip(jax.random.uniform(arg_keys[4], (C2,), jnp.float32, -1.0, 1.0), -1.0, 1.0),
        "map_weight": gaussian(arg_keys[5], (K2, 3, 3, C2, C2), (9 * C2) ** -0.5, 0.375),
        "map_bias": jnp.clip(jax.random.uniform(arg_keys[6], (K2, C2), jnp.float32, -0.5, 0.5), -0.5, 0.5),
        "dilations": draw_dilations(jax.random.fold_in(arg_keys[9], 71), 0),
        "start_bin": jax.random.randint(arg_keys[8], (1,), 0, 100000).astype(jnp.int32),
    }


def position_code(bin_index, start_pos, map_width):
    half_width = map_width // 2
    position = ((start_pos + bin_index) % 8192).astype(jnp.float32)
    rates = jnp.exp(-jnp.arange(half_width).astype(jnp.float32) * (math.log(1000.0) / half_width))
    phase_angle = position[:, None] * rates[None, :]
    return jnp.concatenate([jnp.cos(phase_angle), jnp.sin(phase_angle)], axis=1)


def tower_layer(widened, hidden, weight_set, bias_set, dilation, margin):
    count = hidden.shape[0]
    running = jnp.zeros((count, weight_set.shape[2]), jnp.float32)
    for tap in range(3):
        offset = (margin + (tap - 1) * dilation).astype(jnp.int32)
        tap_slice = lax.dynamic_slice_in_dim(widened, offset, count, 0)
        running = running + jnp.dot(tap_slice, weight_set[tap], preferred_element_type=jnp.float32)
    return (hidden.astype(jnp.float32) + jax.nn.relu(running + bias_set[None, :])).astype(jnp.bfloat16)


def build_pair(row_code, col_code, row_first, col_first, dist_gain):
    row_glob = row_first + jnp.arange(row_code.shape[0]).astype(jnp.int32)
    col_glob = col_first + jnp.arange(col_code.shape[0]).astype(jnp.int32)
    distance = jnp.log(1.0 + jnp.abs(row_glob[:, None] - col_glob[None, :]).astype(jnp.float32)) * 0.125
    summed = (row_code.T.astype(jnp.float32)[:, :, None] + col_code.T.astype(jnp.float32)[:, None, :]
              + dist_gain[:, None, None] * distance[None, :, :])
    return jax.nn.relu(summed).astype(jnp.bfloat16)


def conv_step(padded, center, weight_set, bias_set, dilation, margin):
    chans, nrow, ncol = center.shape
    running = jnp.zeros((weight_set.shape[2], nrow * ncol), jnp.float32)
    zero_index = jnp.zeros((), jnp.int32)
    for tap_row in range(3):
        for tap_col in range(3):
            row_start = (margin + (tap_row - 1) * dilation).astype(jnp.int32)
            col_start = (margin + (tap_col - 1) * dilation).astype(jnp.int32)
            tap_slice = lax.dynamic_slice(padded, (zero_index, row_start, col_start), (chans, nrow, ncol))
            running = running + jnp.dot(weight_set[tap_row, tap_col], tap_slice.reshape(chans, nrow * ncol), preferred_element_type=jnp.float32)
    running = running.reshape(weight_set.shape[2], nrow, ncol) + bias_set[:, None, None]
    return (center.astype(jnp.float32) + jax.nn.relu(running)).astype(jnp.bfloat16)


def reference(features, tower_weight, tower_bias, pair_proj, dist_gain, map_weight, map_bias, dilations, start_bin):
    hidden = features
    for layer in range(K1):
        widened = jnp.pad(hidden, ((DMAX1, DMAX1), (0, 0)))
        hidden = tower_layer(widened, hidden, tower_weight[layer], tower_bias[layer], dilations[layer], DMAX1)
    projected = jnp.dot(hidden, pair_proj, preferred_element_type=jnp.float32)
    bin_index = jnp.arange(L).astype(jnp.int32)
    row_code = (projected[:, :C2] + position_code(bin_index, start_bin[0], C2)).astype(jnp.bfloat16)
    col_code = projected[:, C2:].astype(jnp.bfloat16)
    block_count = L // TILE_R

    def first_block(which):
        row_first = (which * TILE_R).astype(jnp.int32)
        rows_here = lax.dynamic_slice_in_dim(row_code, row_first, TILE_R, 0)
        return build_pair(rows_here, col_code, row_first, jnp.int32(0), dist_gain)

    blocks = lax.map(first_block, jnp.arange(block_count).astype(jnp.int32))
    pair_map = jnp.transpose(blocks, (1, 0, 2, 3)).reshape(C2, L, L)
    for layer in range(K2):
        padded = jnp.pad(pair_map, ((0, 0), (DMAX2, DMAX2), (DMAX2, DMAX2)))
        dilation = dilations[K1 + layer]

        def conv_block(which, padded=padded, current=pair_map, dilation=dilation, layer=layer):
            start_row = (which * TILE_R).astype(jnp.int32)
            band = lax.dynamic_slice_in_dim(padded, start_row, TILE_R + 2 * DMAX2, 1)
            center = lax.dynamic_slice_in_dim(current, start_row, TILE_R, 1)
            return conv_step(band, center, map_weight[layer], map_bias[layer], dilation, DMAX2)

        blocks = lax.map(conv_block, jnp.arange(block_count).astype(jnp.int32))
        pair_map = jnp.transpose(blocks, (1, 0, 2, 3)).reshape(C2, L, L)
    return pair_map
```

```python
import functools
import math

import jax
import jax.numpy as jnp
from jax import lax
from jax.experimental import pallas as pl
from jax.experimental.pallas import tpu as pltpu
from jax.sharding import PartitionSpec as P

DMAX1 = 16
DMAX2 = 16
GROUP = 6
LANES = 256
AXES = ("rows", "cols")


def position_code(bin_index, start_pos, map_width):
    half_width = map_width // 2
    position = ((start_pos + bin_index) % 8192).astype(jnp.float32)
    rates = jnp.exp(-jnp.arange(half_width).astype(jnp.float32) * (math.log(1000.0) / half_width))
    phase_angle = position[:, None] * rates[None, :]
    return jnp.concatenate([jnp.cos(phase_angle), jnp.sin(phase_angle)], axis=1)


def encode_kernel(
    total, dil, place, up2, up1, here, down1, down2, weight, bias, proj, code, out, wide, mid
):
    count = here.shape[0]
    chunks = wide.shape[0]

    def keep(ref, first, value):
        for k in range(chunks):
            ref[k, first : first + value.shape[0], :] = value[:, k * 128 : (k + 1) * 128]

    def run(ref, first, span):
        return jnp.concatenate([ref[k, pl.ds(first, span), :] for k in range(chunks)], axis=1)

    def layer(which, ref, span):
        running = jnp.zeros((span, chunks * 128), jnp.float32)
        for tap in range(3):
            rows = run(ref, count + (tap - 1) * dil[which], span).astype(jnp.bfloat16)
            running += jnp.dot(rows, weight[which, tap], preferred_element_type=jnp.float32)
        return run(ref, count, span) + jnp.maximum(running + bias[which : which + 1, :], 0.0)

    for piece, ref in enumerate((up2, up1, here, down1, down2)):
        keep(wide, piece * count, ref[...].astype(jnp.float32))
    value = layer(0, wide, 3 * count).astype(jnp.bfloat16).astype(jnp.float32)
    index = (place[0] - 1) * count + lax.broadcasted_iota(jnp.int32, value.shape, 0)
    keep(mid, 0, jnp.where((index >= 0) & (index < total), value, 0.0))
    value = layer(1, mid, count)
    parts = jnp.dot(value.astype(jnp.bfloat16), proj[...], preferred_element_type=jnp.float32)
    parts = (parts + code[...]).astype(jnp.bfloat16)
    out[...] = jnp.broadcast_to(parts[None], out.shape)


def shifted(low, high, amount, lane):
    if amount[0] == "right":
        step = amount[1]
        low, high = pltpu.roll(low, step, 1), pltpu.roll(high, step, 1)
        edge = lane < step
    else:
        step = 128 - amount[1]
        low, high = pltpu.roll(low, step, 1), pltpu.roll(high, step, 1)
        edge = lane >= step
    return jnp.where(edge, high, low), jnp.where(edge, low, high)


def pair_kernel(
    total_shards, first_dil, dil, place, parts, gain, weight, bias, out,
    row_turned, distance, field0, field1, field2, final,
):
    shard = parts.shape[1]
    chans = gain.shape[0]
    tile_rows = out.shape[1]
    margin = 3 * DMAX2
    reach = margin // shard
    row_place, col_place = place[1], place[2]
    last_row, last_col = place[3] - 1, place[4] - 1
    row_first = row_place * tile_rows
    col_first = col_place * 128
    dils = [dil[first_dil + k] for k in range(3)]

    def pieces(first, count, wrap):
        taken = []
        for k in range(count):
            step = k - count if k >= wrap else k
            taken.append(parts[jnp.clip(first + step, 0, total_shards - 1)])
        return jnp.concatenate(taken, axis=0).astype(jnp.float32)

    cols = pieces(col_first // shard, LANES // shard, LANES // shard - reach)
    col_turned = jnp.transpose(cols)[chans : 2 * chans, :]
    span0 = tile_rows + 2 * margin
    blocks = -(-span0 // 128)
    rows = pieces(row_first // shard - reach, blocks * 128 // shard, blocks * 128)
    rows = jnp.transpose(rows)[:chans, :]
    for k in range(blocks):
        row_turned[k] = rows[:, k * 128 : (k + 1) * 128]

    lane = lax.broadcasted_iota(jnp.int32, (1, LANES), 1)
    col_local = jnp.where(lane < LANES - margin - 8, lane, lane - LANES)
    row_local = lax.broadcasted_iota(jnp.int32, (span0, LANES), 0) - margin
    apart = jnp.abs(row_first + row_local - (col_first + col_local))
    distance[...] = jnp.log(1.0 + apart.astype(jnp.float32)) * 0.125

    col_glob = col_first + col_local
    inside = (col_glob >= 0) & (col_glob < total_shards * shard)
    inside_high = jnp.where(inside[:, 128:], 1.0, 0.0)
    gain_wide = jnp.broadcast_to(gain[...], (chans, LANES))

    def first_row(i, carry):
        turned = row_turned[i // 128]
        pick = jnp.full((chans, 128), i % 128, jnp.int32)
        row_term = jnp.take_along_axis(turned, pick, axis=1)
        row_term = jnp.concatenate([row_term, row_term], axis=1)
        value = row_term + col_turned + gain_wide * distance[pl.ds(i, 1), :]
        value = jnp.maximum(value, 0.0)
        field0[i, :, :128] = value[:, :128].astype(jnp.bfloat16)
        field0[i, :, 128:] = (value[:, 128:] * inside_high).astype(jnp.bfloat16)
        return carry

    def clear(field, extra):
        @pl.when(row_place == 0)
        def _():
            @pl.loop(0, extra)
            def _(i):
                field[i] = jnp.zeros(field.shape[1:], field.dtype)

        @pl.when(row_place == last_row)
        def _():
            @pl.loop(0, extra)
            def _(i):
                field[extra + tile_rows + i] = jnp.zeros(field.shape[1:], field.dtype)

    need = dils[0] + dils[1] + dils[2]
    lax.fori_loop(margin - need, margin + tile_rows + need, first_row, 0)
    clear(field0, margin)

    lane128 = lax.broadcasted_iota(jnp.int32, (GROUP * chans, 128), 1)

    def tower(layer, source, extra, need, store):
        d = dils[layer]
        span = GROUP * d
        first = extra - need
        count = tile_rows + 2 * need
        bias_wide = jnp.broadcast_to(bias[layer], (chans, 128))

        def group(start, phase):
            base = start + phase
            taps = [source[base + DMAX2 + (k - 1) * d] for k in range(GROUP + 2)]
            stack = jnp.concatenate(taps, axis=0)
            sums = jnp.dot(weight[layer], stack, preferred_element_type=jnp.float32)
            size = GROUP * chans
            left, middle, right = (sums[b * size : (b + 1) * size] for b in range(3))
            left_low, left_high = shifted(left[:, :128], left[:, 128:], ("right", d), lane128)
            right_low, right_high = shifted(right[:, :128], right[:, 128:], ("left", d), lane128)
            low = left_low + middle[:, :128] + right_low
            high = left_high + middle[:, 128:] + right_high
            for k in range(GROUP):
                at = slice(k * chans, (k + 1) * chans)
                center = taps[k + 1].astype(jnp.float32)
                one = center[:, :128] + jnp.maximum(low[at] + bias_wide, 0.0)
                two = center[:, 128:] + jnp.maximum(high[at] + bias_wide, 0.0)
                store(base + k * d, one, two)

        @pl.loop(0, (count + span - 1) // span)
        def _(block):
            start = first + jnp.minimum(block * span, count - span)

            @pl.loop(0, d)
            def _(phase):
                group(start, phase)

    def keep(field):
        def store(i, low, high):
            field[i, :, :128] = low.astype(jnp.bfloat16)
            field[i, :, 128:] = (high * inside_high).astype(jnp.bfloat16)

        return store

    def keep_last(i, low, high):
        final[pl.ds(pl.multiple_of(i * chans, chans), chans), :] = low

    tower(0, field0, 2 * DMAX2, dils[1] + dils[2], keep(field1))
    clear(field1, 2 * DMAX2)
    tower(1, field1, DMAX2, dils[2], keep(field2))
    clear(field2, DMAX2)
    tower(2, field2, 0, 0, keep_last)

    @pl.loop(0, tile_rows // 16)
    def _(block):
        first = pl.multiple_of(block * 16, 16)
        for c in range(chans):
            taken = final[pl.ds(first * chans + c, 16, stride=chans), :]
            out[c, pl.ds(first, 16), :] = taken.astype(jnp.bfloat16)


def banded(map_weight):
    layers, _, _, outs, ins = map_weight.shape
    turned = jnp.transpose(map_weight, (0, 2, 3, 1, 4)).reshape(layers, 3, outs, 3 * ins)
    rows = [
        jnp.pad(turned, ((0, 0), (0, 0), (0, 0), (k * ins, (GROUP - 1 - k) * ins)))
        for k in range(GROUP)
    ]
    return jnp.stack(rows, axis=2).reshape(layers, 3 * GROUP * outs, (GROUP + 2) * ins)


def pair_call(dilations, place, gathered, dist_gain, bands, map_bias, tile_rows, tile_cols):
    chans = dist_gain.shape[0]
    smem = pl.BlockSpec(memory_space=pltpu.SMEM)
    vmem = pl.BlockSpec(memory_space=pltpu.VMEM)
    span = tile_rows + 6 * DMAX2
    return pl.pallas_call(
        functools.partial(pair_kernel, gathered.shape[0], dilations.shape[0] - 3),
        out_shape=jax.ShapeDtypeStruct((chans, tile_rows, tile_cols), jnp.bfloat16),
        in_specs=[smem] * 2 + [vmem] * 4,
        out_specs=vmem,
        scratch_shapes=[
            pltpu.VMEM((-(-span // 128), chans, 128), jnp.float32),
            pltpu.VMEM((span, LANES), jnp.float32),
            pltpu.VMEM((span, chans, LANES), jnp.bfloat16),
            pltpu.VMEM((span - 2 * DMAX2, chans, LANES), jnp.bfloat16),
            pltpu.VMEM((span - 4 * DMAX2, chans, LANES), jnp.bfloat16),
            pltpu.VMEM((tile_rows * chans, 128), jnp.float32),
        ],
        compiler_params=pltpu.CompilerParams(vmem_limit_bytes=48 * 2**20),
        cost_estimate=pl.CostEstimate(
            flops=3 * 2 * tile_rows * 9 * chans * chans * LANES,
            bytes_accessed=tile_rows * tile_cols * chans * 2,
            transcendentals=0,
        ),
        name="pair_tower",
    )(
        dilations, place, gathered, dist_gain.reshape(chans, 1), bands,
        map_bias.reshape(-1, chans, 1),
    )


def on_device(
    features,
    tower_weight,
    tower_bias,
    pair_proj,
    dist_gain,
    map_weight,
    map_bias,
    dilations,
    start_bin,
):
    row_count = lax.axis_size("rows")
    col_count = lax.axis_size("cols")
    shards = row_count * col_count
    shard, width = features.shape
    total = shard * shards
    tile_rows = total // row_count
    tile_cols = total // col_count
    chans = map_weight.shape[-1]
    row_place = lax.axis_index("rows")
    col_place = lax.axis_index("cols")
    mine = row_place * col_count + col_place
    place = jnp.stack(
        [mine, row_place, col_place, jnp.int32(row_count), jnp.int32(col_count)]
    ).astype(jnp.int32)

    def moved(step):
        pairs = [(i, i + step) for i in range(shards) if 0 <= i + step < shards]
        return lax.ppermute(features, AXES, pairs)

    up2, up1, down1, down2 = moved(2), moved(1), moved(-1), moved(-2)
    code = position_code(mine * shard + jnp.arange(shard), start_bin[0], chans)
    code = jnp.pad(code, ((0, 0), (0, chans)))
    bands = banded(map_weight)

    smem = pl.BlockSpec(memory_space=pltpu.SMEM)
    vmem = pl.BlockSpec(memory_space=pltpu.VMEM)
    parts = pl.pallas_call(
        functools.partial(encode_kernel, total),
        out_shape=jax.ShapeDtypeStruct((shards, shard, 2 * chans), jnp.bfloat16),
        in_specs=[smem] * 2 + [vmem] * 9,
        out_specs=vmem,
        scratch_shapes=[
            pltpu.VMEM((width // 128, 5 * shard, 128), jnp.float32),
            pltpu.VMEM((width // 128, 3 * shard, 128), jnp.float32),
        ],
        compiler_params=pltpu.CompilerParams(vmem_limit_bytes=24 * 2**20),
        cost_estimate=pl.CostEstimate(
            flops=2 * 4 * shard * 3 * width * width,
            bytes_accessed=6 * width * width * 2,
            transcendentals=0,
        ),
        name="encode",
    )(
        dilations, place, up2, up1, features, down1, down2,
        tower_weight, tower_bias, pair_proj, code,
    )

    gathered = lax.all_to_all(parts, AXES, split_axis=0, concat_axis=0, tiled=True)

    return pair_call(
        dilations, place, gathered, dist_gain, bands, map_bias, tile_rows, tile_cols
    )


def solution(mesh):
    placed = (P(AXES, None), P(), P(), P(), P(), P(), P(), P(), P())
    return jax.shard_map(
        on_device, mesh=mesh, in_specs=placed, out_specs=P(None, "rows", "cols"), check_vma=False
    )
```

```python
import functools
import math

import jax
import jax.numpy as jnp
from jax import lax
from jax.experimental import pallas as pl
from jax.experimental.pallas import tpu as pltpu
from jax.sharding import PartitionSpec as P

DMAX1 = 16
DMAX2 = 16
GROUP = 3
TAIL = 32
WIDE = 2
UNROLL = 2
LANES = 256
AXES = ("rows", "cols")


def position_code(bin_index, start_pos, map_width):
    half_width = map_width // 2
    position = ((start_pos + bin_index) % 8192).astype(jnp.float32)
    rates = jnp.exp(-jnp.arange(half_width).astype(jnp.float32) * (math.log(1000.0) / half_width))
    phase_angle = position[:, None] * rates[None, :]
    return jnp.concatenate([jnp.cos(phase_angle), jnp.sin(phase_angle)], axis=1)


def encode_kernel(
    total, place, up2, up1, down1, down2, code, near, weight_far, out,
    weight, wide, mid, arrived,
):
    count = up1.shape[0]
    bias = near[count : count + 2, :]
    proj = near[count + 2 :, :].astype(jnp.bfloat16)
    fetch = [
        [
            pltpu.make_async_copy(
                weight_far.at[which, tap], weight.at[which, tap], arrived.at[which, tap]
            )
            for tap in range(3)
        ]
        for which in range(2)
    ]
    for copy in fetch[0] + fetch[1]:
        copy.start()
    chunks = wide.shape[0]

    def keep(ref, first, value):
        for k in range(chunks):
            ref[k, first : first + value.shape[0], :] = value[:, k * 128 : (k + 1) * 128]

    def run(ref, first, span):
        return jnp.concatenate([ref[k, pl.ds(first, span), :] for k in range(chunks)], axis=1)

    def layer(which, ref, span):
        running = jnp.zeros((span, chunks * 128), jnp.float32)
        for tap in range(3):
            rows = run(ref, count + (tap - 1) * place[5 + which], span).astype(jnp.bfloat16)
            fetch[which][tap].wait()
            running += jnp.dot(rows, weight[which, tap], preferred_element_type=jnp.float32)
        return run(ref, count, span) + jnp.maximum(running + bias[which : which + 1, :], 0.0)

    for piece, ref in enumerate((up2, up1, near, down1, down2)):
        keep(wide, piece * count, ref[:count, :].astype(jnp.float32))
    value = layer(0, wide, 3 * count).astype(jnp.bfloat16).astype(jnp.float32)
    index = (place[0] - 1) * count + lax.broadcasted_iota(jnp.int32, value.shape, 0)
    keep(mid, 0, jnp.where((index >= 0) & (index < total), value, 0.0))
    value = layer(1, mid, count)
    parts = lax.dot_general(
        value.astype(jnp.bfloat16),
        proj,
        (((1,), (1,)), ((), ())),
        preferred_element_type=jnp.float32,
    )
    parts = (parts + code[...]).astype(jnp.bfloat16)
    parts = jnp.concatenate([parts[: count // 2], parts[count // 2 :]], axis=1)
    out[...] = jnp.broadcast_to(parts[None], out.shape)


def pair_kernel(
    total_shards, first_dil, place, parts, gain, weight, out,
    row_turned, distance, field_a, field_b, final,
):
    shard = 2 * parts.shape[1]
    chans = gain.shape[0]
    tile_rows = out.shape[1]
    margin = 3 * DMAX2
    reach = margin // shard
    row_place, col_place = place[1], place[2]
    last_row = place[3] - 1
    row_first = row_place * tile_rows
    col_first = col_place * 128
    dils = [place[first_dil + k] for k in range(3)]

    def pieces(first, count, wrap):
        taken = []
        for k in range(count):
            step = k - count if k >= wrap else k
            both = parts[jnp.clip(first + step, 0, total_shards - 1)]
            taken += [both[:, : 2 * chans], both[:, 2 * chans :]]
        return jnp.concatenate(taken, axis=0).astype(jnp.float32)

    cols = pieces(col_first // shard, LANES // shard, LANES // shard - reach)
    col_turned = jnp.transpose(cols)[chans : 2 * chans, :]
    span0 = tile_rows + 2 * margin
    blocks = -(-span0 // 128)
    rows = pieces(row_first // shard - reach, blocks * 128 // shard, blocks * 128)
    rows = jnp.transpose(rows)[:chans, :]
    for k in range(blocks):
        row_turned[k] = rows[:, k * 128 : (k + 1) * 128]

    lane = lax.broadcasted_iota(jnp.int32, (1, LANES), 1)
    col_local = jnp.where(lane < LANES - margin - 8, lane, lane - LANES)
    row_local = lax.broadcasted_iota(jnp.int32, (span0, LANES), 0) - margin
    apart = jnp.abs(row_first + row_local - (col_first + col_local))
    distance[...] = jnp.log(1.0 + apart.astype(jnp.float32)) * 0.125

    col_glob = col_first + col_local
    inside = (col_glob >= 0) & (col_glob < total_shards * shard)
    inside_high = jnp.where(inside[:, 128:], 1.0, 0.0)
    inside_high = jnp.broadcast_to(inside_high, (chans, 128)).astype(jnp.bfloat16)
    gain_wide = jnp.broadcast_to(gain[...], (chans, LANES))
    lane16 = lax.broadcasted_iota(jnp.int16, (chans, 128), 1)

    def keep(field, d):
        back = 128 - d
        at_left = lane16 < d.astype(jnp.int16)
        at_right = lane16 >= back.astype(jnp.int16)

        def store(i, low, high):
            low = low.astype(jnp.bfloat16)
            high = high.astype(jnp.bfloat16) * inside_high
            field[i, chans : 2 * chans, :128] = low
            field[i, chans : 2 * chans, 128:] = high
            turned_low, turned_high = pltpu.roll(low, d, 1), pltpu.roll(high, d, 1)
            field[i, :chans, :128] = jnp.where(at_left, turned_high, turned_low)
            field[i, :chans, 128:] = jnp.where(at_left, turned_low, turned_high)
            turned_low, turned_high = pltpu.roll(low, back, 1), pltpu.roll(high, back, 1)
            field[i, 2 * chans :, :128] = jnp.where(at_right, turned_high, turned_low)
            field[i, 2 * chans :, 128:] = jnp.where(at_right, turned_low, turned_high)

        return store

    def clear(field, extra):
        @pl.when(row_place == 0)
        def _():
            @pl.loop(0, extra)
            def _(i):
                field[i] = jnp.zeros(field.shape[1:], field.dtype)

        @pl.when(row_place == last_row)
        def _():
            @pl.loop(0, extra)
            def _(i):
                field[extra + tile_rows + i] = jnp.zeros(field.shape[1:], field.dtype)

    need = dils[0] + dils[1] + dils[2]
    store_first = keep(field_a, dils[0])
    first, last = margin - need, margin + tile_rows + need

    @pl.loop(0, (last - first + 3) // 4)
    def _(block):
        for k in range(4):
            i = jnp.minimum(first + block * 4 + k, last - 1)
            pick = jnp.full((chans, 128), i % 128, jnp.int32)
            row_term = jnp.take_along_axis(row_turned[i // 128], pick, axis=1)
            row_term = jnp.concatenate([row_term, row_term], axis=1)
            value = row_term + col_turned + gain_wide * distance[pl.ds(i, 1), :]
            value = jnp.maximum(value, 0.0)
            store_first(i, value[:, :128], value[:, 128:])

    clear(field_a, margin)

    tail = jnp.ones((TAIL, WIDE * LANES), jnp.bfloat16)

    def tower(layer, source, extra, need, store):
        d = dils[layer]
        span = GROUP * d
        first = extra - need
        count = tile_rows + 2 * need
        final_layer = layer == 2

        def groups(bases):
            width = 128 if final_layer else LANES
            taps = []
            for k in range(GROUP + 2):
                at = [base + DMAX2 + (k - 1) * d for base in bases]
                taps.append(jnp.concatenate([source[i, :, :width] for i in at], axis=1))
            stack = jnp.concatenate(taps + [tail], axis=0)
            sums = jnp.dot(weight[layer], stack, preferred_element_type=jnp.float32)
            for n, base in enumerate(bases):
                for k in range(GROUP):
                    at = slice(n * width, (n + 1) * width)
                    center = taps[k + 1][chans : 2 * chans, at].astype(jnp.float32)
                    value = center + jnp.maximum(sums[k * chans : (k + 1) * chans, at], 0.0)
                    if final_layer:
                        store(base + k * d, value)
                    else:
                        store(base + k * d, value[:, :128], value[:, 128:])

        each = WIDE * (2 if final_layer else 1)
        total = (count + span - 1) // span * d

        @functools.partial(
            lax.fori_loop, 0, (total + UNROLL * each - 1) // (UNROLL * each),
            init_val=(jnp.int32(0), jnp.int32(0)),
        )
        def _(step, carry):
            start, phase = carry
            bases = []
            for _ in range(UNROLL * each):
                bases.append(first + jnp.minimum(start, count - span) + phase)
                wrap = phase + 1 >= d
                start = jnp.where(wrap, start + span, start)
                phase = jnp.where(wrap, 0, phase + 1)
            for k in range(UNROLL):
                groups(bases[k * each : (k + 1) * each])
            return start, phase

    def keep_last(i, low):
        final[pl.ds(pl.multiple_of(i * chans, chans), chans), :] = low

    tower(0, field_a, 2 * DMAX2, dils[1] + dils[2], keep(field_b, dils[1]))
    clear(field_b, 2 * DMAX2)
    tower(1, field_b, DMAX2, dils[2], keep(field_a, dils[2]))
    clear(field_a, DMAX2)
    tower(2, field_a, 0, 0, keep_last)

    @pl.loop(0, tile_rows // 16)
    def _(block):
        first = pl.multiple_of(block * 16, 16)
        for c in range(chans):
            taken = final[pl.ds(first * chans + c, 16, stride=chans), :]
            out[c, pl.ds(first, 16), :] = taken.astype(jnp.bfloat16)


def banded(map_weight, map_bias):
    layers, _, _, outs, ins = map_weight.shape
    taps = jnp.transpose(map_weight, (0, 3, 1, 2, 4)).reshape(layers, outs, 9 * ins)
    left = map_bias
    split = []
    for _ in range(3):
        split.append(lax.reduce_precision(left, 8, 7))
        left = left - split[-1]
    split = jnp.stack(split, axis=2).astype(jnp.bfloat16)
    rows = []
    for k in range(GROUP):
        before, after = k * 3 * ins, (GROUP - 1 - k) * 3 * ins
        row = jnp.pad(taps, ((0, 0), (0, 0), (before, after)))
        rows.append(jnp.concatenate([row, jnp.pad(split, ((0, 0), (0, 0), (0, TAIL - 3)))], axis=2))
    return jnp.concatenate(rows, axis=1)


def pair_call(place, gathered, dist_gain, bands, tile_rows, tile_cols):
    chans = dist_gain.shape[0]
    smem = pl.BlockSpec(memory_space=pltpu.SMEM)
    vmem = pl.BlockSpec(memory_space=pltpu.VMEM)
    span = tile_rows + 6 * DMAX2
    return pl.pallas_call(
        functools.partial(pair_kernel, gathered.shape[0], place.shape[0] - 3),
        out_shape=jax.ShapeDtypeStruct((chans, tile_rows, tile_cols), jnp.bfloat16),
        in_specs=[smem] + [vmem] * 3,
        out_specs=vmem,
        scratch_shapes=[
            pltpu.VMEM((-(-span // 128), chans, 128), jnp.float32),
            pltpu.VMEM((span, LANES), jnp.float32),
            pltpu.VMEM((span, 3 * chans, LANES), jnp.bfloat16),
            pltpu.VMEM((span - 2 * DMAX2, 3 * chans, LANES), jnp.bfloat16),
            pltpu.VMEM((tile_rows * chans, 128), jnp.float32),
        ],
        compiler_params=pltpu.CompilerParams(vmem_limit_bytes=48 * 2**20),
        cost_estimate=pl.CostEstimate(
            flops=3 * 2 * tile_rows * 9 * chans * chans * LANES,
            bytes_accessed=tile_rows * tile_cols * chans * 2,
            transcendentals=0,
        ),
        name="pair_tower",
    )(
        place, gathered, dist_gain.reshape(chans, 1), bands,
    )


def on_device(
    features,
    tower_weight,
    tower_bias,
    pair_proj,
    dist_gain,
    map_weight,
    map_bias,
    dilations,
    start_bin,
):
    row_count = lax.axis_size("rows")
    col_count = lax.axis_size("cols")
    shards = row_count * col_count
    shard, width = features.shape
    total = shard * shards
    tile_rows = total // row_count
    tile_cols = total // col_count
    chans = map_weight.shape[-1]
    row_place = lax.axis_index("rows")
    col_place = lax.axis_index("cols")
    mine = row_place * col_count + col_place
    place = jnp.stack([mine, row_place, col_place, row_count, col_count]).astype(jnp.int32)
    place = jnp.concatenate([place, dilations])

    def moved(step):
        pairs = [(i, i + step) for i in range(shards) if 0 <= i + step < shards]
        return lax.ppermute(features, AXES, pairs)

    up2, up1, down1, down2 = moved(2), moved(1), moved(-1), moved(-2)
    code = position_code(mine * shard + jnp.arange(shard), start_bin[0], chans)
    code = jnp.pad(code, ((0, 0), (0, chans)))
    near = [features.astype(jnp.float32), tower_bias, pair_proj.T.astype(jnp.float32)]
    near = jnp.concatenate(near, axis=0)
    bands = banded(map_weight, map_bias)

    smem = pl.BlockSpec(memory_space=pltpu.SMEM)
    vmem = pl.BlockSpec(memory_space=pltpu.VMEM)
    parts = pl.pallas_call(
        functools.partial(encode_kernel, total),
        out_shape=jax.ShapeDtypeStruct((shards, shard // 2, 4 * chans), jnp.bfloat16),
        in_specs=[smem] + [vmem] * 6 + [pl.BlockSpec(memory_space=pltpu.HBM)],
        out_specs=vmem,
        scratch_shapes=[
            pltpu.VMEM(tower_weight.shape, tower_weight.dtype),
            pltpu.VMEM((width // 128, 5 * shard, 128), jnp.float32),
            pltpu.VMEM((width // 128, 3 * shard, 128), jnp.float32),
            pltpu.SemaphoreType.DMA(tower_weight.shape[:2]),
        ],
        compiler_params=pltpu.CompilerParams(vmem_limit_bytes=52 * 2**20),
        cost_estimate=pl.CostEstimate(
            flops=2 * 4 * shard * 3 * width * width,
            bytes_accessed=6 * width * width * 2,
            transcendentals=0,
        ),
        name="encode",
    )(
        place, up2, up1, down1, down2, code, near, tower_weight,
    )

    gathered = lax.all_to_all(parts, AXES, split_axis=0, concat_axis=0, tiled=True)
    return pair_call(
        place, gathered, dist_gain, bands, tile_rows, tile_cols
    )


def solution(mesh):
    placed = (P(AXES, None), P(), P(), P(), P(), P(), P(), P(), P())
    return jax.shard_map(
        on_device, mesh=mesh, in_specs=placed, out_specs=P(None, "rows", "cols"), check_vma=False
    )
```

```python
import functools
import math

import jax
import jax.numpy as jnp
from jax import lax
from jax.experimental import pallas as pl
from jax.experimental.pallas import tpu as pltpu
from jax.sharding import PartitionSpec as P

DMAX1 = 16
DMAX2 = 16
GROUP = 3
TAIL = 32
WIDE = 4
UNROLL = 1
LANES = 256
AXES = ("rows", "cols")


def position_code(bin_index, start_pos, map_width):
    half_width = map_width // 2
    position = ((start_pos + bin_index) % 8192).astype(jnp.float32)
    rates = jnp.exp(-jnp.arange(half_width).astype(jnp.float32) * (math.log(1000.0) / half_width))
    phase_angle = position[:, None] * rates[None, :]
    return jnp.concatenate([jnp.cos(phase_angle), jnp.sin(phase_angle)], axis=1)


def encode_kernel(
    total, place, up2, up1, down1, down2, code, near, weight_far, out,
    weight, wide, mid, arrived,
):
    count = up1.shape[0]
    bias = near[count : count + 2, :]
    proj = near[count + 2 :, :].astype(jnp.bfloat16)
    fetch = [
        [
            pltpu.make_async_copy(
                weight_far.at[which, tap], weight.at[which, tap], arrived.at[which, tap]
            )
            for tap in range(3)
        ]
        for which in range(2)
    ]
    for copy in fetch[0] + fetch[1]:
        copy.start()
    chunks = wide.shape[0]

    def keep(ref, first, value):
        for k in range(chunks):
            ref[k, first : first + value.shape[0], :] = value[:, k * 128 : (k + 1) * 128]

    def run(ref, first, span):
        return jnp.concatenate([ref[k, pl.ds(first, span), :] for k in range(chunks)], axis=1)

    def layer(which, ref, span):
        running = jnp.zeros((span, chunks * 128), jnp.float32)
        for tap in range(3):
            rows = run(ref, count + (tap - 1) * place[5 + which], span).astype(jnp.bfloat16)
            fetch[which][tap].wait()
            running += jnp.dot(rows, weight[which, tap], preferred_element_type=jnp.float32)
        return run(ref, count, span) + jnp.maximum(running + bias[which : which + 1, :], 0.0)

    for piece, ref in enumerate((up2, up1, near, down1, down2)):
        keep(wide, piece * count, ref[:count, :].astype(jnp.float32))
    value = layer(0, wide, 3 * count).astype(jnp.bfloat16).astype(jnp.float32)
    index = (place[0] - 1) * count + lax.broadcasted_iota(jnp.int32, value.shape, 0)
    keep(mid, 0, jnp.where((index >= 0) & (index < total), value, 0.0))
    value = layer(1, mid, count)
    parts = lax.dot_general(
        value.astype(jnp.bfloat16),
        proj,
        (((1,), (1,)), ((), ())),
        preferred_element_type=jnp.float32,
    )
    parts = (parts + code[...]).astype(jnp.bfloat16)
    parts = jnp.concatenate([parts[: count // 2], parts[count // 2 :]], axis=1)
    out[...] = jnp.broadcast_to(parts[None], out.shape)


def pair_kernel(
    total_shards, first_dil, place, parts, gain, weight, out,
    row_turned, distance, field_a, field_b, final,
):
    shard = 2 * parts.shape[1]
    chans = gain.shape[0]
    tile_rows = out.shape[1]
    margin = 3 * DMAX2
    reach = margin // shard
    row_place, col_place = place[1], place[2]
    last_row = place[3] - 1
    row_first = row_place * tile_rows
    col_first = col_place * 128
    dils = [place[first_dil + k] for k in range(3)]

    def pieces(first, count, wrap):
        taken = []
        for k in range(count):
            step = k - count if k >= wrap else k
            both = parts[jnp.clip(first + step, 0, total_shards - 1)]
            taken += [both[:, : 2 * chans], both[:, 2 * chans :]]
        return jnp.concatenate(taken, axis=0).astype(jnp.float32)

    cols = pieces(col_first // shard, LANES // shard, LANES // shard - reach)
    col_turned = jnp.transpose(cols)[chans : 2 * chans, :]
    span0 = tile_rows + 2 * margin
    blocks = -(-span0 // 128)
    rows = pieces(row_first // shard - reach, blocks * 128 // shard, blocks * 128)
    rows = jnp.transpose(rows)[:chans, :]
    for k in range(blocks):
        row_turned[k] = rows[:, k * 128 : (k + 1) * 128]

    lane = lax.broadcasted_iota(jnp.int32, (1, LANES), 1)
    col_local = jnp.where(lane < LANES - margin - 8, lane, lane - LANES)
    row_local = lax.broadcasted_iota(jnp.int32, (span0, LANES), 0) - margin
    apart = jnp.abs(row_first + row_local - (col_first + col_local))
    distance[...] = jnp.log(1.0 + apart.astype(jnp.float32)) * 0.125

    col_glob = col_first + col_local
    inside = (col_glob >= 0) & (col_glob < total_shards * shard)
    inside_high = jnp.where(inside[:, 128:], 1.0, 0.0)
    inside_high = jnp.broadcast_to(inside_high, (chans, 128)).astype(jnp.bfloat16)
    gain_wide = jnp.broadcast_to(gain[...], (chans, LANES))
    lane16 = lax.broadcasted_iota(jnp.int16, (chans, 128), 1)

    def keep(field, d):
        back = 128 - d
        at_left = lane16 < d.astype(jnp.int16)
        at_right = lane16 >= back.astype(jnp.int16)

        def store(i, low, high):
            low = low.astype(jnp.bfloat16)
            high = high.astype(jnp.bfloat16) * inside_high
            field[i, chans : 2 * chans, :128] = low
            field[i, chans : 2 * chans, 128:] = high
            turned_low, turned_high = pltpu.roll(low, d, 1), pltpu.roll(high, d, 1)
            field[i, :chans, :128] = jnp.where(at_left, turned_high, turned_low)
            field[i, :chans, 128:] = jnp.where(at_left, turned_low, turned_high)
            turned_low, turned_high = pltpu.roll(low, back, 1), pltpu.roll(high, back, 1)
            field[i, 2 * chans :, :128] = jnp.where(at_right, turned_high, turned_low)
            field[i, 2 * chans :, 128:] = jnp.where(at_right, turned_low, turned_high)

        return store

    def clear(field, extra):
        @pl.when(row_place == 0)
        def _():
            @pl.loop(0, extra)
            def _(i):
                field[i] = jnp.zeros(field.shape[1:], field.dtype)

        @pl.when(row_place == last_row)
        def _():
            @pl.loop(0, extra)
            def _(i):
                field[extra + tile_rows + i] = jnp.zeros(field.shape[1:], field.dtype)

    need = dils[0] + dils[1] + dils[2]
    store_first = keep(field_a, dils[0])
    first, last = margin - need, margin + tile_rows + need

    @pl.loop(0, (last - first + 3) // 4)
    def _(block):
        for k in range(4):
            i = jnp.minimum(first + block * 4 + k, last - 1)
            pick = jnp.full((chans, 128), i % 128, jnp.int32)
            row_term = jnp.take_along_axis(row_turned[i // 128], pick, axis=1)
            row_term = jnp.concatenate([row_term, row_term], axis=1)
            value = row_term + col_turned + gain_wide * distance[pl.ds(i, 1), :]
            value = jnp.maximum(value, 0.0)
            store_first(i, value[:, :128], value[:, 128:])

    clear(field_a, margin)

    tail = jnp.ones((TAIL, WIDE * LANES), jnp.bfloat16)

    def tower(layer, source, extra, need, store):
        d = dils[layer]
        span = GROUP * d
        first = extra - need
        count = tile_rows + 2 * need
        final_layer = layer == 2

        def groups(bases):
            width = 128 if final_layer else LANES
            taps = []
            for k in range(GROUP + 2):
                at = [base + DMAX2 + (k - 1) * d for base in bases]
                taps.append(jnp.concatenate([source[i, :, :width] for i in at], axis=1))
            stack = jnp.concatenate(taps + [tail], axis=0)
            sums = jnp.dot(weight[layer], stack, preferred_element_type=jnp.float32)
            for n, base in enumerate(bases):
                for k in range(GROUP):
                    at = slice(n * width, (n + 1) * width)
                    center = taps[k + 1][chans : 2 * chans, at].astype(jnp.float32)
                    value = center + jnp.maximum(sums[k * chans : (k + 1) * chans, at], 0.0)
                    if final_layer:
                        store(base + k * d, value)
                    else:
                        store(base + k * d, value[:, :128], value[:, 128:])

        each = WIDE * (2 if final_layer else 1)
        total = (count + span - 1) // span * d

        @functools.partial(
            lax.fori_loop, 0, (total + UNROLL * each - 1) // (UNROLL * each),
            init_val=(jnp.int32(0), jnp.int32(0)),
        )
        def _(step, carry):
            start, phase = carry
            bases = []
            for _ in range(UNROLL * each):
                bases.append(first + jnp.minimum(start, count - span) + phase)
                wrap = phase + 1 >= d
                start = jnp.where(wrap, start + span, start)
                phase = jnp.where(wrap, 0, phase + 1)
            for k in range(UNROLL):
                groups(bases[k * each : (k + 1) * each])
            return start, phase

    def keep_last(i, low):
        final[pl.ds(pl.multiple_of(i * chans, chans), chans), :] = low

    tower(0, field_a, 2 * DMAX2, dils[1] + dils[2], keep(field_b, dils[1]))
    clear(field_b, 2 * DMAX2)
    tower(1, field_b, DMAX2, dils[2], keep(field_a, dils[2]))
    clear(field_a, DMAX2)
    tower(2, field_a, 0, 0, keep_last)

    @pl.loop(0, tile_rows // 16)
    def _(block):
        first = pl.multiple_of(block * 16, 16)
        for c in range(chans):
            taken = final[pl.ds(first * chans + c, 16, stride=chans), :]
            out[c, pl.ds(first, 16), :] = taken.astype(jnp.bfloat16)


def banded(map_weight, map_bias):
    layers, _, _, outs, ins = map_weight.shape
    taps = jnp.transpose(map_weight, (0, 3, 1, 2, 4)).reshape(layers, outs, 9 * ins)
    left = map_bias
    split = []
    for _ in range(3):
        split.append(lax.reduce_precision(left, 8, 7))
        left = left - split[-1]
    split = jnp.stack(split, axis=2).astype(jnp.bfloat16)
    rows = []
    for k in range(GROUP):
        before, after = k * 3 * ins, (GROUP - 1 - k) * 3 * ins
        row = jnp.pad(taps, ((0, 0), (0, 0), (before, after)))
        rows.append(jnp.concatenate([row, jnp.pad(split, ((0, 0), (0, 0), (0, TAIL - 3)))], axis=2))
    return jnp.concatenate(rows, axis=1)


def pair_call(place, gathered, dist_gain, bands, tile_rows, tile_cols):
    chans = dist_gain.shape[0]
    smem = pl.BlockSpec(memory_space=pltpu.SMEM)
    vmem = pl.BlockSpec(memory_space=pltpu.VMEM)
    span = tile_rows + 6 * DMAX2
    return pl.pallas_call(
        functools.partial(pair_kernel, gathered.shape[0], place.shape[0] - 3),
        out_shape=jax.ShapeDtypeStruct((chans, tile_rows, tile_cols), jnp.bfloat16),
        in_specs=[smem] + [vmem] * 3,
        out_specs=vmem,
        scratch_shapes=[
            pltpu.VMEM((-(-span // 128), chans, 128), jnp.float32),
            pltpu.VMEM((span, LANES), jnp.float32),
            pltpu.VMEM((span, 3 * chans, LANES), jnp.bfloat16),
            pltpu.VMEM((span - 2 * DMAX2, 3 * chans, LANES), jnp.bfloat16),
            pltpu.VMEM((tile_rows * chans, 128), jnp.float32),
        ],
        compiler_params=pltpu.CompilerParams(vmem_limit_bytes=48 * 2**20),
        cost_estimate=pl.CostEstimate(
            flops=3 * 2 * tile_rows * 9 * chans * chans * LANES,
            bytes_accessed=tile_rows * tile_cols * chans * 2,
            transcendentals=0,
        ),
        name="pair_tower",
    )(
        place, gathered, dist_gain.reshape(chans, 1), bands,
    )


def on_device(
    features,
    tower_weight,
    tower_bias,
    pair_proj,
    dist_gain,
    map_weight,
    map_bias,
    dilations,
    start_bin,
):
    row_count = lax.axis_size("rows")
    col_count = lax.axis_size("cols")
    shards = row_count * col_count
    shard, width = features.shape
    total = shard * shards
    tile_rows = total // row_count
    tile_cols = total // col_count
    chans = map_weight.shape[-1]
    row_place = lax.axis_index("rows")
    col_place = lax.axis_index("cols")
    mine = row_place * col_count + col_place
    place = jnp.stack([mine, row_place, col_place, row_count, col_count]).astype(jnp.int32)
    place = jnp.concatenate([place, dilations])

    def moved(step):
        pairs = [(i, i + step) for i in range(shards) if 0 <= i + step < shards]
        return lax.ppermute(features, AXES, pairs)

    up2, up1, down1, down2 = moved(2), moved(1), moved(-1), moved(-2)
    code = position_code(mine * shard + jnp.arange(shard), start_bin[0], chans)
    code = jnp.pad(code, ((0, 0), (0, chans)))
    near = [features.astype(jnp.float32), tower_bias, pair_proj.T.astype(jnp.float32)]
    near = jnp.concatenate(near, axis=0)
    bands = banded(map_weight, map_bias)

    smem = pl.BlockSpec(memory_space=pltpu.SMEM)
    vmem = pl.BlockSpec(memory_space=pltpu.VMEM)
    parts = pl.pallas_call(
        functools.partial(encode_kernel, total),
        out_shape=jax.ShapeDtypeStruct((shards, shard // 2, 4 * chans), jnp.bfloat16),
        in_specs=[smem] + [vmem] * 6 + [pl.BlockSpec(memory_space=pltpu.HBM)],
        out_specs=vmem,
        scratch_shapes=[
            pltpu.VMEM(tower_weight.shape, tower_weight.dtype),
            pltpu.VMEM((width // 128, 5 * shard, 128), jnp.float32),
            pltpu.VMEM((width // 128, 3 * shard, 128), jnp.float32),
            pltpu.SemaphoreType.DMA(tower_weight.shape[:2]),
        ],
        compiler_params=pltpu.CompilerParams(vmem_limit_bytes=52 * 2**20),
        cost_estimate=pl.CostEstimate(
            flops=2 * 4 * shard * 3 * width * width,
            bytes_accessed=6 * width * width * 2,
            transcendentals=0,
        ),
        name="encode",
    )(
        place, up2, up1, down1, down2, code, near, tower_weight,
    )

    gathered = lax.all_to_all(parts, AXES, split_axis=0, concat_axis=0, tiled=True)
    return pair_call(
        place, gathered, dist_gain, bands, tile_rows, tile_cols
    )


def solution(mesh):
    placed = (P(AXES, None), P(), P(), P(), P(), P(), P(), P(), P())
    return jax.shard_map(
        on_device, mesh=mesh, in_specs=placed, out_specs=P(None, "rows", "cols"), check_vma=False
    )
```

```python
import functools
import math

import jax
import jax.numpy as jnp
from jax import lax
from jax.experimental import pallas as pl
from jax.experimental.pallas import tpu as pltpu
from jax.sharding import PartitionSpec as P

DMAX1 = 16
DMAX2 = 16
GROUP = 3
TAIL = 32
WIDE = 2
UNROLL = 4
LANES = 256
AXES = ("rows", "cols")


def position_code(bin_index, start_pos, map_width):
    half_width = map_width // 2
    position = ((start_pos + bin_index) % 8192).astype(jnp.float32)
    rates = jnp.exp(-jnp.arange(half_width).astype(jnp.float32) * (math.log(1000.0) / half_width))
    phase_angle = position[:, None] * rates[None, :]
    return jnp.concatenate([jnp.cos(phase_angle), jnp.sin(phase_angle)], axis=1)


def encode_kernel(
    total, place, up2, up1, down1, down2, code, near, weight_far, out,
    weight, wide, mid, arrived,
):
    count = up1.shape[0]
    bias = near[count : count + 2, :]
    proj = near[count + 2 :, :].astype(jnp.bfloat16)
    fetch = [
        [
            pltpu.make_async_copy(
                weight_far.at[which, tap], weight.at[which, tap], arrived.at[which, tap]
            )
            for tap in range(3)
        ]
        for which in range(2)
    ]
    for copy in fetch[0] + fetch[1]:
        copy.start()
    chunks = wide.shape[0]

    def keep(ref, first, value):
        for k in range(chunks):
            ref[k, first : first + value.shape[0], :] = value[:, k * 128 : (k + 1) * 128]

    def run(ref, first, span):
        return jnp.concatenate([ref[k, pl.ds(first, span), :] for k in range(chunks)], axis=1)

    def layer(which, ref, span):
        running = jnp.zeros((span, chunks * 128), jnp.float32)
        for tap in range(3):
            rows = run(ref, count + (tap - 1) * place[5 + which], span).astype(jnp.bfloat16)
            fetch[which][tap].wait()
            running += jnp.dot(rows, weight[which, tap], preferred_element_type=jnp.float32)
        return run(ref, count, span) + jnp.maximum(running + bias[which : which + 1, :], 0.0)

    for piece, ref in enumerate((up2, up1, near, down1, down2)):
        keep(wide, piece * count, ref[:count, :].astype(jnp.float32))
    value = layer(0, wide, 3 * count).astype(jnp.bfloat16).astype(jnp.float32)
    index = (place[0] - 1) * count + lax.broadcasted_iota(jnp.int32, value.shape, 0)
    keep(mid, 0, jnp.where((index >= 0) & (index < total), value, 0.0))
    value = layer(1, mid, count)
    parts = lax.dot_general(
        value.astype(jnp.bfloat16),
        proj,
        (((1,), (1,)), ((), ())),
        preferred_element_type=jnp.float32,
    )
    parts = (parts + code[...]).astype(jnp.bfloat16)
    parts = jnp.concatenate([parts[: count // 2], parts[count // 2 :]], axis=1)
    out[...] = jnp.broadcast_to(parts[None], out.shape)


def pair_kernel(
    total_shards, first_dil, place, parts, gain, weight, out,
    row_turned, distance, field_a, field_b, final,
):
    shard = 2 * parts.shape[1]
    chans = gain.shape[0]
    tile_rows = out.shape[1]
    margin = 3 * DMAX2
    reach = margin // shard
    row_place, col_place = place[1], place[2]
    last_row = place[3] - 1
    row_first = row_place * tile_rows
    col_first = col_place * 128
    dils = [place[first_dil + k] for k in range(3)]

    def pieces(first, count, wrap):
        taken = []
        for k in range(count):
            step = k - count if k >= wrap else k
            both = parts[jnp.clip(first + step, 0, total_shards - 1)]
            taken += [both[:, : 2 * chans], both[:, 2 * chans :]]
        return jnp.concatenate(taken, axis=0).astype(jnp.float32)

    cols = pieces(col_first // shard, LANES // shard, LANES // shard - reach)
    col_turned = jnp.transpose(cols)[chans : 2 * chans, :]
    span0 = tile_rows + 2 * margin
    blocks = -(-span0 // 128)
    rows = pieces(row_first // shard - reach, blocks * 128 // shard, blocks * 128)
    rows = jnp.transpose(rows)[:chans, :]
    for k in range(blocks):
        row_turned[k] = rows[:, k * 128 : (k + 1) * 128]

    lane = lax.broadcasted_iota(jnp.int32, (1, LANES), 1)
    col_local = jnp.where(lane < LANES - margin - 8, lane, lane - LANES)
    row_local = lax.broadcasted_iota(jnp.int32, (span0, LANES), 0) - margin
    apart = jnp.abs(row_first + row_local - (col_first + col_local))
    distance[...] = jnp.log(1.0 + apart.astype(jnp.float32)) * 0.125

    col_glob = col_first + col_local
    inside = (col_glob >= 0) & (col_glob < total_shards * shard)
    inside_high = jnp.where(inside[:, 128:], 1.0, 0.0)
    inside_high = jnp.broadcast_to(inside_high, (chans, 128)).astype(jnp.bfloat16)
    gain_wide = jnp.broadcast_to(gain[...], (chans, LANES))
    lane16 = lax.broadcasted_iota(jnp.int16, (chans, 128), 1)

    def keep(field, d):
        back = 128 - d
        at_left = lane16 < d.astype(jnp.int16)
        at_right = lane16 >= back.astype(jnp.int16)

        def store(i, low, high):
            low = low.astype(jnp.bfloat16)
            high = high.astype(jnp.bfloat16) * inside_high
            field[i, chans : 2 * chans, :128] = low
            field[i, chans : 2 * chans, 128:] = high
            turned_low, turned_high = pltpu.roll(low, d, 1), pltpu.roll(high, d, 1)
            field[i, :chans, :128] = jnp.where(at_left, turned_high, turned_low)
            field[i, :chans, 128:] = jnp.where(at_left, turned_low, turned_high)
            turned_low, turned_high = pltpu.roll(low, back, 1), pltpu.roll(high, back, 1)
            field[i, 2 * chans :, :128] = jnp.where(at_right, turned_high, turned_low)
            field[i, 2 * chans :, 128:] = jnp.where(at_right, turned_low, turned_high)

        return store

    def clear(field, extra):
        @pl.when(row_place == 0)
        def _():
            @pl.loop(0, extra)
            def _(i):
                field[i] = jnp.zeros(field.shape[1:], field.dtype)

        @pl.when(row_place == last_row)
        def _():
            @pl.loop(0, extra)
            def _(i):
                field[extra + tile_rows + i] = jnp.zeros(field.shape[1:], field.dtype)

    need = dils[0] + dils[1] + dils[2]
    store_first = keep(field_a, dils[0])
    first, last = margin - need, margin + tile_rows + need

    @pl.loop(0, (last - first + 3) // 4)
    def _(block):
        for k in range(4):
            i = jnp.minimum(first + block * 4 + k, last - 1)
            pick = jnp.full((chans, 128), i % 128, jnp.int32)
            row_term = jnp.take_along_axis(row_turned[i // 128], pick, axis=1)
            row_term = jnp.concatenate([row_term, row_term], axis=1)
            value = row_term + col_turned + gain_wide * distance[pl.ds(i, 1), :]
            value = jnp.maximum(value, 0.0)
            store_first(i, value[:, :128], value[:, 128:])

    clear(field_a, margin)

    tail = jnp.ones((TAIL, WIDE * LANES), jnp.bfloat16)

    def tower(layer, source, extra, need, store):
        d = dils[layer]
        span = GROUP * d
        first = extra - need
        count = tile_rows + 2 * need
        final_layer = layer == 2

        def groups(bases):
            width = 128 if final_layer else LANES
            taps = []
            for k in range(GROUP + 2):
                at = [base + DMAX2 + (k - 1) * d for base in bases]
                taps.append(jnp.concatenate([source[i, :, :width] for i in at], axis=1))
            stack = jnp.concatenate(taps + [tail], axis=0)
            sums = jnp.dot(weight[layer], stack, preferred_element_type=jnp.float32)
            for n, base in enumerate(bases):
                for k in range(GROUP):
                    at = slice(n * width, (n + 1) * width)
                    center = taps[k + 1][chans : 2 * chans, at].astype(jnp.float32)
                    value = center + jnp.maximum(sums[k * chans : (k + 1) * chans, at], 0.0)
                    if final_layer:
                        store(base + k * d, value)
                    else:
                        store(base + k * d, value[:, :128], value[:, 128:])

        each = WIDE * (2 if final_layer else 1)
        total = (count + span - 1) // span * d

        @functools.partial(
            lax.fori_loop, 0, (total + UNROLL * each - 1) // (UNROLL * each),
            init_val=(jnp.int32(0), jnp.int32(0)),
        )
        def _(step, carry):
            start, phase = carry
            bases = []
            for _ in range(UNROLL * each):
                bases.append(first + jnp.minimum(start, count - span) + phase)
                wrap = phase + 1 >= d
                start = jnp.where(wrap, start + span, start)
                phase = jnp.where(wrap, 0, phase + 1)
            for k in range(UNROLL):
                groups(bases[k * each : (k + 1) * each])
            return start, phase

    def keep_last(i, low):
        final[pl.ds(pl.multiple_of(i * chans, chans), chans), :] = low

    tower(0, field_a, 2 * DMAX2, dils[1] + dils[2], keep(field_b, dils[1]))
    clear(field_b, 2 * DMAX2)
    tower(1, field_b, DMAX2, dils[2], keep(field_a, dils[2]))
    clear(field_a, DMAX2)
    tower(2, field_a, 0, 0, keep_last)

    @pl.loop(0, tile_rows // 16)
    def _(block):
        first = pl.multiple_of(block * 16, 16)
        for c in range(chans):
            taken = final[pl.ds(first * chans + c, 16, stride=chans), :]
            out[c, pl.ds(first, 16), :] = taken.astype(jnp.bfloat16)


def banded(map_weight, map_bias):
    layers, _, _, outs, ins = map_weight.shape
    taps = jnp.transpose(map_weight, (0, 3, 1, 2, 4)).reshape(layers, outs, 9 * ins)
    left = map_bias
    split = []
    for _ in range(3):
        split.append(lax.reduce_precision(left, 8, 7))
        left = left - split[-1]
    split = jnp.stack(split, axis=2).astype(jnp.bfloat16)
    rows = []
    for k in range(GROUP):
        before, after = k * 3 * ins, (GROUP - 1 - k) * 3 * ins
        row = jnp.pad(taps, ((0, 0), (0, 0), (before, after)))
        rows.append(jnp.concatenate([row, jnp.pad(split, ((0, 0), (0, 0), (0, TAIL - 3)))], axis=2))
    return jnp.concatenate(rows, axis=1)


def pair_call(place, gathered, dist_gain, bands, tile_rows, tile_cols):
    chans = dist_gain.shape[0]
    smem = pl.BlockSpec(memory_space=pltpu.SMEM)
    vmem = pl.BlockSpec(memory_space=pltpu.VMEM)
    span = tile_rows + 6 * DMAX2
    return pl.pallas_call(
        functools.partial(pair_kernel, gathered.shape[0], place.shape[0] - 3),
        out_shape=jax.ShapeDtypeStruct((chans, tile_rows, tile_cols), jnp.bfloat16),
        in_specs=[smem] + [vmem] * 3,
        out_specs=vmem,
        scratch_shapes=[
            pltpu.VMEM((-(-span // 128), chans, 128), jnp.float32),
            pltpu.VMEM((span, LANES), jnp.float32),
            pltpu.VMEM((span, 3 * chans, LANES), jnp.bfloat16),
            pltpu.VMEM((span - 2 * DMAX2, 3 * chans, LANES), jnp.bfloat16),
            pltpu.VMEM((tile_rows * chans, 128), jnp.float32),
        ],
        compiler_params=pltpu.CompilerParams(vmem_limit_bytes=48 * 2**20),
        cost_estimate=pl.CostEstimate(
            flops=3 * 2 * tile_rows * 9 * chans * chans * LANES,
            bytes_accessed=tile_rows * tile_cols * chans * 2,
            transcendentals=0,
        ),
        name="pair_tower",
    )(
        place, gathered, dist_gain.reshape(chans, 1), bands,
    )


def on_device(
    features,
    tower_weight,
    tower_bias,
    pair_proj,
    dist_gain,
    map_weight,
    map_bias,
    dilations,
    start_bin,
):
    row_count = lax.axis_size("rows")
    col_count = lax.axis_size("cols")
    shards = row_count * col_count
    shard, width = features.shape
    total = shard * shards
    tile_rows = total // row_count
    tile_cols = total // col_count
    chans = map_weight.shape[-1]
    row_place = lax.axis_index("rows")
    col_place = lax.axis_index("cols")
    mine = row_place * col_count + col_place
    place = jnp.stack([mine, row_place, col_place, row_count, col_count]).astype(jnp.int32)
    place = jnp.concatenate([place, dilations])

    def moved(step):
        pairs = [(i, i + step) for i in range(shards) if 0 <= i + step < shards]
        return lax.ppermute(features, AXES, pairs)

    up2, up1, down1, down2 = moved(2), moved(1), moved(-1), moved(-2)
    code = position_code(mine * shard + jnp.arange(shard), start_bin[0], chans)
    code = jnp.pad(code, ((0, 0), (0, chans)))
    near = [features.astype(jnp.float32), tower_bias, pair_proj.T.astype(jnp.float32)]
    near = jnp.concatenate(near, axis=0)
    bands = banded(map_weight, map_bias)

    smem = pl.BlockSpec(memory_space=pltpu.SMEM)
    vmem = pl.BlockSpec(memory_space=pltpu.VMEM)
    parts = pl.pallas_call(
        functools.partial(encode_kernel, total),
        out_shape=jax.ShapeDtypeStruct((shards, shard // 2, 4 * chans), jnp.bfloat16),
        in_specs=[smem] + [vmem] * 6 + [pl.BlockSpec(memory_space=pltpu.HBM)],
        out_specs=vmem,
        scratch_shapes=[
            pltpu.VMEM(tower_weight.shape, tower_weight.dtype),
            pltpu.VMEM((width // 128, 5 * shard, 128), jnp.float32),
            pltpu.VMEM((width // 128, 3 * shard, 128), jnp.float32),
            pltpu.SemaphoreType.DMA(tower_weight.shape[:2]),
        ],
        compiler_params=pltpu.CompilerParams(vmem_limit_bytes=52 * 2**20),
        cost_estimate=pl.CostEstimate(
            flops=2 * 4 * shard * 3 * width * width,
            bytes_accessed=6 * width * width * 2,
            transcendentals=0,
        ),
        name="encode",
    )(
        place, up2, up1, down1, down2, code, near, tower_weight,
    )

    gathered = lax.all_to_all(parts, AXES, split_axis=0, concat_axis=0, tiled=True)
    return pair_call(
        place, gathered, dist_gain, bands, tile_rows, tile_cols
    )


def solution(mesh):
    placed = (P(AXES, None), P(), P(), P(), P(), P(), P(), P(), P())
    return jax.shard_map(
        on_device, mesh=mesh, in_specs=placed, out_specs=P(None, "rows", "cols"), check_vma=False
    )
```

```python
import functools
import math

import jax
import jax.numpy as jnp
from jax import lax
from jax.experimental import pallas as pl
from jax.experimental.pallas import tpu as pltpu
from jax.sharding import PartitionSpec as P

DMAX1 = 16
DMAX2 = 16
GROUP = 3
TAIL = 32
WIDE = 2
UNROLL = 4
LANES = 256
PITCH = 40
OUTSIDE = -1e30
AXES = ("rows", "cols")


def position_code(bin_index, start_pos, map_width):
    half_width = map_width // 2
    position = ((start_pos + bin_index) % 8192).astype(jnp.float32)
    rates = jnp.exp(-jnp.arange(half_width).astype(jnp.float32) * (math.log(1000.0) / half_width))
    phase_angle = position[:, None] * rates[None, :]
    return jnp.concatenate([jnp.cos(phase_angle), jnp.sin(phase_angle)], axis=1)


def encode_kernel(
    total, place, up2_far, up1_far, here_far, down1_far, down2_far, bias_far, proj_far, code_far,
    weight_far, out, window, bias, proj, code, weight, wide, mid, near_done, arrived,
):
    count = here_far.shape[0]
    pieces = [(far, window.at[k]) for k, far in enumerate((up2_far, up1_far, here_far, down1_far, down2_far))]
    pieces += [(bias_far, bias), (proj_far, proj), (code_far, code)]
    near = [
        pltpu.make_async_copy(far, here, near_done.at[k]) for k, (far, here) in enumerate(pieces)
    ]
    fetch = [
        [
            pltpu.make_async_copy(
                weight_far.at[which, tap], weight.at[which, tap], arrived.at[which, tap]
            )
            for tap in range(3)
        ]
        for which in range(2)
    ]
    for copy in near + fetch[0] + fetch[1]:
        copy.start()
    for copy in near:
        copy.wait()
    chunks = wide.shape[0]

    def keep(ref, first, value):
        for k in range(chunks):
            ref[k, first : first + value.shape[0], :] = value[:, k * 128 : (k + 1) * 128]

    def run(ref, first, span):
        return jnp.concatenate([ref[k, pl.ds(first, span), :] for k in range(chunks)], axis=1)

    def layer(which, ref, span):
        running = jnp.zeros((span, chunks * 128), jnp.float32)
        for tap in range(3):
            rows = run(ref, count + (tap - 1) * place[5 + which], span).astype(jnp.bfloat16)
            fetch[which][tap].wait()
            running += jnp.dot(rows, weight[which, tap], preferred_element_type=jnp.float32)
        return run(ref, count, span) + jnp.maximum(running + bias[which : which + 1, :], 0.0)

    for piece in range(5):
        keep(wide, piece * count, window[piece].astype(jnp.float32))
    value = layer(0, wide, 3 * count).astype(jnp.bfloat16).astype(jnp.float32)
    index = (place[0] - 1) * count + lax.broadcasted_iota(jnp.int32, value.shape, 0)
    keep(mid, 0, jnp.where((index >= 0) & (index < total), value, 0.0))
    value = layer(1, mid, count)
    parts = lax.dot_general(
        value.astype(jnp.bfloat16),
        proj[...],
        (((1,), (1,)), ((), ())),
        preferred_element_type=jnp.float32,
    )
    parts = (parts + code[...]).astype(jnp.bfloat16)
    parts = jnp.concatenate([parts[: count // 2], parts[count // 2 :]], axis=1)
    out[...] = jnp.broadcast_to(parts[None], out.shape)


def pair_kernel(
    total_shards, first_dil, place, parts, gain, weight, out,
    row_turned, distance, field_a, field_b, final, held,
):
    shard = 2 * parts.shape[1]
    chans = gain.shape[0]
    tile_rows = out.shape[1]
    margin = 3 * DMAX2
    reach = margin // shard
    row_place, col_place = place[1], place[2]
    last_row = place[3] - 1
    row_first = row_place * tile_rows
    col_first = col_place * 128
    dils = [place[first_dil + k] for k in range(3)]

    def pieces(first, count, wrap):
        taken = []
        for k in range(count):
            step = k - count if k >= wrap else k
            both = parts[jnp.clip(first + step, 0, total_shards - 1)]
            taken += [both[:, : 2 * chans], both[:, 2 * chans :]]
        return jnp.concatenate(taken, axis=0).astype(jnp.float32)

    lane = lax.broadcasted_iota(jnp.int32, (1, LANES), 1)
    col_local = jnp.where(lane < LANES - margin - 8, lane, lane - LANES)
    col_glob = col_first + col_local
    inside = (col_glob >= 0) & (col_glob < total_shards * shard)
    inside_high = jnp.where(inside[:, 128:], 1.0, 0.0)
    inside_high = jnp.broadcast_to(inside_high, (chans, 128)).astype(jnp.bfloat16)

    cols = pieces(col_first // shard, LANES // shard, LANES // shard - reach)
    col_turned = jnp.transpose(cols)[chans : 2 * chans, :]
    col_turned = jnp.where(inside, col_turned, OUTSIDE)
    span0 = tile_rows + 2 * margin
    blocks = -(-span0 // 128)
    rows = pieces(row_first // shard - reach, blocks * 128 // shard, blocks * 128)
    rows = jnp.transpose(rows)[:chans, :]
    row_glob = row_first - margin + lax.broadcasted_iota(jnp.int32, (1, blocks * 128), 1)
    rows = jnp.where((row_glob >= 0) & (row_glob < total_shards * shard), rows, OUTSIDE)
    for k in range(blocks):
        row_turned[k] = rows[:, k * 128 : (k + 1) * 128]

    row_local = lax.broadcasted_iota(jnp.int32, (span0, LANES), 0) - margin
    apart = jnp.abs(row_first + row_local - col_glob)
    distance[...] = jnp.log(1.0 + apart.astype(jnp.float32)) * 0.125
    gain_wide = jnp.broadcast_to(gain[...], (chans, LANES))
    lane16 = lax.broadcasted_iota(jnp.int16, (chans, 128), 1)

    def keep(field, d, masked):
        back = 128 - d
        at_left = lane16 < d.astype(jnp.int16)
        at_right = lane16 >= back.astype(jnp.int16)

        def store(i, low, high):
            low = low.astype(jnp.bfloat16)
            high = high.astype(jnp.bfloat16)
            if masked:
                high = high * inside_high
            field[i, chans : 2 * chans, :128] = low
            field[i, chans : 2 * chans, 128:] = high
            turned_low, turned_high = pltpu.roll(low, d, 1), pltpu.roll(high, d, 1)
            field[i, :chans, :128] = jnp.where(at_left, turned_high, turned_low)
            field[i, :chans, 128:] = jnp.where(at_left, turned_low, turned_high)
            turned_low, turned_high = pltpu.roll(low, back, 1), pltpu.roll(high, back, 1)
            field[i, 2 * chans :, :128] = jnp.where(at_right, turned_high, turned_low)
            field[i, 2 * chans :, 128:] = jnp.where(at_right, turned_low, turned_high)

        return store

    def clear(field, extra):
        @pl.when(row_place == 0)
        def _():
            @pl.loop(0, extra)
            def _(i):
                field[i] = jnp.zeros(field.shape[1:], field.dtype)

        @pl.when(row_place == last_row)
        def _():
            @pl.loop(0, extra)
            def _(i):
                field[extra + tile_rows + i] = jnp.zeros(field.shape[1:], field.dtype)

    need = dils[0] + dils[1] + dils[2]
    store_first = keep(field_a, dils[0], False)
    first_row, last_row_needed = margin - need, margin + tile_rows + need - 1

    def build(index, count):
        for k in range(count):
            i = jnp.minimum(first_row + index + k, last_row_needed)
            pick = jnp.full((chans, 128), i % 128, jnp.int32)
            row_term = jnp.take_along_axis(row_turned[i // 128], pick, axis=1)
            row_term = jnp.concatenate([row_term, row_term], axis=1)
            value = row_term + col_turned + gain_wide * distance[pl.ds(i, 1), :]
            value = jnp.maximum(value, 0.0)
            store_first(i, value[:, :128], value[:, 128:])

    @pl.loop(0, (last_row_needed - first_row + 8) // 8)
    def _(block):
        build(block * 8, 8)

    tail = jnp.ones((TAIL, WIDE * LANES), jnp.bfloat16)

    def tower(layer, source, extra, need, store):
        d = dils[layer]
        span = GROUP * d
        first = extra - need
        count = tile_rows + 2 * need
        final_layer = layer == 2
        width = 128 if final_layer else LANES
        each = WIDE * LANES // width

        def product(bases):
            taps = []
            for k in range(GROUP + 2):
                at = [base + DMAX2 + (k - 1) * d for base in bases]
                taps.append(jnp.concatenate([source[i, :, :width] for i in at], axis=1))
            stack = jnp.concatenate(taps + [tail], axis=0)
            return jnp.dot(weight[layer], stack, preferred_element_type=jnp.float32)

        def finish(bases, sums):
            for n, base in enumerate(bases):
                for k in range(GROUP):
                    at = slice(n * width, (n + 1) * width)
                    center = source[base + DMAX2 + k * d, chans : 2 * chans, :width]
                    value = sums[k * chans : (k + 1) * chans, at]
                    value = center.astype(jnp.float32) + jnp.maximum(value, 0.0)
                    if final_layer:
                        store(base + k * d, value)
                    else:
                        store(base + k * d, value[:, :128], value[:, 128:])

        def walk(start, phase):
            bases = []
            for _ in range(each):
                bases.append(first + jnp.minimum(start, count - span) + phase)
                wrap = phase + 1 >= d
                start = jnp.where(wrap, start + span, start)
                phase = jnp.where(wrap, 0, phase + 1)
            return bases, start, phase

        def step(_, carry):
            start, phase, bases = carry
            sums = held
            for k in range(UNROLL):
                next_bases, start, phase = walk(start, phase)
                next_sums = product(next_bases)
                finish(bases, sums)
                bases, sums = next_bases, next_sums
            held[...] = sums
            return start, phase, bases

        zero = jnp.int32(0)
        total = (count + span - 1) // span * d
        steps = (total + UNROLL * each - 1) // (UNROLL * each)
        carry = lax.fori_loop(0, steps, step, (zero, zero, walk(zero, zero)[0]))
        finish(carry[2], held)

    def keep_last(i, low):
        final[pl.ds(pl.multiple_of(i * PITCH, 8), chans), :] = low

    tower(0, field_a, 2 * DMAX2, dils[1] + dils[2], keep(field_b, dils[1], True))
    clear(field_b, 2 * DMAX2)
    tower(1, field_b, DMAX2, dils[2], keep(field_a, dils[2], True))
    clear(field_a, DMAX2)
    tower(2, field_a, 0, 0, keep_last)

    @pl.loop(0, tile_rows // 16)
    def _(block):
        first = pl.multiple_of(block * 16, 16)
        for c in range(chans):
            taken = final[pl.ds(first * PITCH + c, 16, stride=PITCH), :]
            out[c, pl.ds(first, 16), :] = taken.astype(jnp.bfloat16)


def banded(map_weight, map_bias):
    layers, _, _, outs, ins = map_weight.shape
    taps = jnp.transpose(map_weight, (0, 3, 1, 2, 4)).reshape(layers, outs, 9 * ins)
    left = map_bias
    split = []
    for _ in range(3):
        split.append(lax.reduce_precision(left, 8, 7))
        left = left - split[-1]
    split = jnp.stack(split, axis=2).astype(jnp.bfloat16)
    rows = []
    for k in range(GROUP):
        before, after = k * 3 * ins, (GROUP - 1 - k) * 3 * ins
        row = jnp.pad(taps, ((0, 0), (0, 0), (before, after)))
        rows.append(jnp.concatenate([row, jnp.pad(split, ((0, 0), (0, 0), (0, TAIL - 3)))], axis=2))
    return jnp.concatenate(rows, axis=1)


def pair_call(place, gathered, dist_gain, bands, tile_rows, tile_cols):
    chans = dist_gain.shape[0]
    smem = pl.BlockSpec(memory_space=pltpu.SMEM)
    vmem = pl.BlockSpec(memory_space=pltpu.VMEM)
    span = tile_rows + 6 * DMAX2
    return pl.pallas_call(
        functools.partial(pair_kernel, gathered.shape[0], place.shape[0] - 3),
        out_shape=jax.ShapeDtypeStruct((chans, tile_rows, tile_cols), jnp.bfloat16),
        in_specs=[smem] + [vmem] * 3,
        out_specs=vmem,
        scratch_shapes=[
            pltpu.VMEM((-(-span // 128), chans, 128), jnp.float32),
            pltpu.VMEM((span, LANES), jnp.float32),
            pltpu.VMEM((span, 3 * chans, LANES), jnp.bfloat16),
            pltpu.VMEM((span - 2 * DMAX2, 3 * chans, LANES), jnp.bfloat16),
            pltpu.VMEM((tile_rows * PITCH, 128), jnp.float32),
            pltpu.VMEM((GROUP * chans, WIDE * LANES), jnp.float32),
        ],
        compiler_params=pltpu.CompilerParams(vmem_limit_bytes=48 * 2**20),
        cost_estimate=pl.CostEstimate(
            flops=3 * 2 * tile_rows * 9 * chans * chans * LANES,
            bytes_accessed=tile_rows * tile_cols * chans * 2,
            transcendentals=0,
        ),
        name="pair_tower",
    )(
        place, gathered, dist_gain.reshape(chans, 1), bands,
    )


def on_device(
    features,
    tower_weight,
    tower_bias,
    pair_proj,
    dist_gain,
    map_weight,
    map_bias,
    dilations,
    start_bin,
):
    row_count = lax.axis_size("rows")
    col_count = lax.axis_size("cols")
    shards = row_count * col_count
    shard, width = features.shape
    total = shard * shards
    tile_rows = total // row_count
    tile_cols = total // col_count
    chans = map_weight.shape[-1]
    row_place = lax.axis_index("rows")
    col_place = lax.axis_index("cols")
    mine = row_place * col_count + col_place
    place = jnp.stack([mine, row_place, col_place, row_count, col_count]).astype(jnp.int32)
    place = jnp.concatenate([place, dilations])

    def moved(step):
        pairs = [(i, i + step) for i in range(shards) if 0 <= i + step < shards]
        return lax.ppermute(features, AXES, pairs)

    up2, up1, down1, down2 = moved(2), moved(1), moved(-1), moved(-2)
    code = position_code(mine * shard + jnp.arange(shard), start_bin[0], chans)
    code = jnp.pad(code, ((0, 0), (0, chans)))
    bands = banded(map_weight, map_bias)

    smem = pl.BlockSpec(memory_space=pltpu.SMEM)
    vmem = pl.BlockSpec(memory_space=pltpu.VMEM)
    parts = pl.pallas_call(
        functools.partial(encode_kernel, total),
        out_shape=jax.ShapeDtypeStruct((shards, shard // 2, 4 * chans), jnp.bfloat16),
        in_specs=[smem] + [pl.BlockSpec(memory_space=pltpu.HBM)] * 9,
        out_specs=vmem,
        scratch_shapes=[
            pltpu.VMEM((5, shard, width), features.dtype),
            pltpu.VMEM(tower_bias.shape, tower_bias.dtype),
            pltpu.VMEM(pair_proj.shape[::-1], pair_proj.dtype),
            pltpu.VMEM(code.shape, code.dtype),
            pltpu.VMEM(tower_weight.shape, tower_weight.dtype),
            pltpu.VMEM((width // 128, 5 * shard, 128), jnp.float32),
            pltpu.VMEM((width // 128, 3 * shard, 128), jnp.float32),
            pltpu.SemaphoreType.DMA((8,)),
            pltpu.SemaphoreType.DMA(tower_weight.shape[:2]),
        ],
        compiler_params=pltpu.CompilerParams(vmem_limit_bytes=56 * 2**20),
        cost_estimate=pl.CostEstimate(
            flops=2 * 4 * shard * 3 * width * width,
            bytes_accessed=6 * width * width * 2,
            transcendentals=0,
        ),
        name="encode",
    )(
        place, up2, up1, features, down1, down2, tower_bias, pair_proj.T, code, tower_weight,
    )

    gathered = lax.all_to_all(parts, AXES, split_axis=0, concat_axis=0, tiled=True)
    return pair_call(
        place, gathered, dist_gain, bands, tile_rows, tile_cols
    )


def solution(mesh):
    placed = (P(AXES, None), P(), P(), P(), P(), P(), P(), P(), P())
    return jax.shard_map(
        on_device, mesh=mesh, in_specs=placed, out_specs=P(None, "rows", "cols"), check_vma=False
    )
```

```python
import functools
import math

import jax
import jax.numpy as jnp
from jax import lax
from jax.experimental import pallas as pl
from jax.experimental.pallas import tpu as pltpu
from jax.sharding import PartitionSpec as P

DMAX1 = 16
DMAX2 = 16
GROUP = 4
TAIL = 32
WIDE = 2
UNROLL = 4
LANES = 256
PITCH = 40
OUTSIDE = -1e30
AXES = ("rows", "cols")


def position_code(bin_index, start_pos, map_width):
    half_width = map_width // 2
    position = ((start_pos + bin_index) % 8192).astype(jnp.float32)
    rates = jnp.exp(-jnp.arange(half_width).astype(jnp.float32) * (math.log(1000.0) / half_width))
    phase_angle = position[:, None] * rates[None, :]
    return jnp.concatenate([jnp.cos(phase_angle), jnp.sin(phase_angle)], axis=1)


def encode_kernel(
    total, place, up2, up1, down1, down2, near, extra, weight_far, out,
    weight, wide, mid, arrived,
):
    count = up1.shape[0]
    bias = extra[:2, :]
    proj = near[count:, :]
    fetch = [
        [
            pltpu.make_async_copy(
                weight_far.at[which, tap], weight.at[which, tap], arrived.at[which, tap]
            )
            for tap in range(3)
        ]
        for which in range(2)
    ]
    for copy in fetch[0] + fetch[1]:
        copy.start()
    chunks = wide.shape[0]

    def keep(ref, first, value):
        for k in range(chunks):
            ref[k, first : first + value.shape[0], :] = value[:, k * 128 : (k + 1) * 128]

    def run(ref, first, span):
        return jnp.concatenate([ref[k, pl.ds(first, span), :] for k in range(chunks)], axis=1)

    def layer(which, ref, span):
        running = jnp.zeros((span, chunks * 128), jnp.float32)
        for tap in range(3):
            rows = run(ref, count + (tap - 1) * place[5 + which], span).astype(jnp.bfloat16)
            fetch[which][tap].wait()
            running += jnp.dot(rows, weight[which, tap], preferred_element_type=jnp.float32)
        return run(ref, count, span) + jnp.maximum(running + bias[which : which + 1, :], 0.0)

    for piece, ref in enumerate((up2, up1, near, down1, down2)):
        keep(wide, piece * count, ref[:count, :].astype(jnp.float32))
    value = layer(0, wide, 3 * count).astype(jnp.bfloat16).astype(jnp.float32)
    index = (place[0] - 1) * count + lax.broadcasted_iota(jnp.int32, value.shape, 0)
    keep(mid, 0, jnp.where((index >= 0) & (index < total), value, 0.0))
    value = layer(1, mid, count)
    parts = lax.dot_general(
        value.astype(jnp.bfloat16),
        proj,
        (((1,), (1,)), ((), ())),
        preferred_element_type=jnp.float32,
    )
    parts = (parts + extra[2 : 2 + count, : proj.shape[0]]).astype(jnp.bfloat16)
    parts = jnp.concatenate([parts[: count // 2], parts[count // 2 :]], axis=1)
    out[...] = jnp.broadcast_to(parts[None], out.shape)


def pair_kernel(
    total_shards, first_dil, place, parts, gain, weight, out,
    row_turned, distance, field_a, field_b, final, held,
):
    shard = 2 * parts.shape[1]
    chans = gain.shape[0]
    tile_rows = out.shape[1]
    margin = 3 * DMAX2
    reach = margin // shard
    row_place, col_place = place[1], place[2]
    last_row = place[3] - 1
    row_first = row_place * tile_rows
    col_first = col_place * 128
    dils = [place[first_dil + k] for k in range(3)]

    def pieces(first, count, wrap):
        taken = []
        for k in range(count):
            step = k - count if k >= wrap else k
            both = parts[jnp.clip(first + step, 0, total_shards - 1)]
            taken += [both[:, : 2 * chans], both[:, 2 * chans :]]
        return jnp.concatenate(taken, axis=0).astype(jnp.float32)

    lane = lax.broadcasted_iota(jnp.int32, (1, LANES), 1)
    col_local = jnp.where(lane < LANES - margin - 8, lane, lane - LANES)
    col_glob = col_first + col_local
    inside = (col_glob >= 0) & (col_glob < total_shards * shard)
    inside_high = jnp.where(inside[:, 128:], 1.0, 0.0)
    inside_high = jnp.broadcast_to(inside_high, (chans, 128)).astype(jnp.bfloat16)

    cols = pieces(col_first // shard, LANES // shard, LANES // shard - reach)
    col_turned = jnp.transpose(cols)[chans : 2 * chans, :]
    col_turned = jnp.where(inside, col_turned, OUTSIDE)
    span0 = tile_rows + 2 * margin
    blocks = -(-span0 // 128)
    rows = pieces(row_first // shard - reach, blocks * 128 // shard, blocks * 128)
    rows = jnp.transpose(rows)[:chans, :]
    row_glob = row_first - margin + lax.broadcasted_iota(jnp.int32, (1, blocks * 128), 1)
    rows = jnp.where((row_glob >= 0) & (row_glob < total_shards * shard), rows, OUTSIDE)
    for k in range(blocks):
        row_turned[k] = rows[:, k * 128 : (k + 1) * 128]

    row_local = lax.broadcasted_iota(jnp.int32, (span0, LANES), 0) - margin
    apart = jnp.abs(row_first + row_local - col_glob)
    distance[...] = jnp.log(1.0 + apart.astype(jnp.float32)) * 0.125
    gain_wide = jnp.broadcast_to(gain[...], (chans, LANES))
    lane16 = lax.broadcasted_iota(jnp.int16, (chans, 128), 1)

    def keep(field, d, masked):
        back = 128 - d
        at_left = lane16 < d.astype(jnp.int16)
        at_right = lane16 >= back.astype(jnp.int16)

        def store(i, low, high):
            low = low.astype(jnp.bfloat16)
            high = high.astype(jnp.bfloat16)
            if masked:
                high = high * inside_high
            field[i, chans : 2 * chans, :128] = low
            field[i, chans : 2 * chans, 128:] = high
            turned_low, turned_high = pltpu.roll(low, d, 1), pltpu.roll(high, d, 1)
            field[i, :chans, :128] = jnp.where(at_left, turned_high, turned_low)
            field[i, :chans, 128:] = jnp.where(at_left, turned_low, turned_high)
            turned_low, turned_high = pltpu.roll(low, back, 1), pltpu.roll(high, back, 1)
            field[i, 2 * chans :, :128] = jnp.where(at_right, turned_high, turned_low)
            field[i, 2 * chans :, 128:] = jnp.where(at_right, turned_low, turned_high)

        return store

    def clear(field, extra):
        @pl.when(row_place == 0)
        def _():
            @pl.loop(0, extra)
            def _(i):
                field[i] = jnp.zeros(field.shape[1:], field.dtype)

        @pl.when(row_place == last_row)
        def _():
            @pl.loop(0, extra)
            def _(i):
                field[extra + tile_rows + i] = jnp.zeros(field.shape[1:], field.dtype)

    need = dils[0] + dils[1] + dils[2]
    store_first = keep(field_a, dils[0], False)
    first_row, last_row_needed = margin - need, margin + tile_rows + need - 1

    def build(index, count):
        for k in range(count):
            i = jnp.minimum(first_row + index + k, last_row_needed)
            pick = jnp.full((chans, 128), i % 128, jnp.int32)
            row_term = jnp.take_along_axis(row_turned[i // 128], pick, axis=1)
            row_term = jnp.concatenate([row_term, row_term], axis=1)
            value = row_term + col_turned + gain_wide * distance[pl.ds(i, 1), :]
            value = jnp.maximum(value, 0.0)
            store_first(i, value[:, :128], value[:, 128:])

    @pl.loop(0, (last_row_needed - first_row + 8) // 8)
    def _(block):
        build(block * 8, 8)

    tail = jnp.ones((TAIL, WIDE * LANES), jnp.bfloat16)

    def tower(layer, source, extra, need, store):
        d = dils[layer]
        span = GROUP * d
        first = extra - need
        count = tile_rows + 2 * need
        final_layer = layer == 2
        width = 128 if final_layer else LANES
        each = WIDE * LANES // width

        def product(bases):
            taps = []
            for k in range(GROUP + 2):
                at = [base + DMAX2 + (k - 1) * d for base in bases]
                taps.append(jnp.concatenate([source[i, :, :width] for i in at], axis=1))
            stack = jnp.concatenate(taps + [tail], axis=0)
            return jnp.dot(weight[layer], stack, preferred_element_type=jnp.float32)

        def finish(bases, sums):
            for n, base in enumerate(bases):
                for k in range(GROUP):
                    at = slice(n * width, (n + 1) * width)
                    center = source[base + DMAX2 + k * d, chans : 2 * chans, :width]
                    value = sums[k * chans : (k + 1) * chans, at]
                    value = center.astype(jnp.float32) + jnp.maximum(value, 0.0)
                    if final_layer:
                        store(base + k * d, value)
                    else:
                        store(base + k * d, value[:, :128], value[:, 128:])

        def walk(start, phase):
            bases = []
            for _ in range(each):
                bases.append(first + jnp.minimum(start, count - span) + phase)
                wrap = phase + 1 >= d
                start = jnp.where(wrap, start + span, start)
                phase = jnp.where(wrap, 0, phase + 1)
            return bases, start, phase

        def step(_, carry):
            start, phase, bases = carry
            sums = held
            for k in range(UNROLL):
                next_bases, start, phase = walk(start, phase)
                next_sums = product(next_bases)
                finish(bases, sums)
                bases, sums = next_bases, next_sums
            held[...] = sums
            return start, phase, bases

        zero = jnp.int32(0)
        total = (count + span - 1) // span * d
        steps = (total + UNROLL * each - 1) // (UNROLL * each)
        carry = lax.fori_loop(0, steps, step, (zero, zero, walk(zero, zero)[0]))
        finish(carry[2], held)

    def keep_last(i, low):
        final[pl.ds(pl.multiple_of(i * PITCH, 8), chans), :] = low

    tower(0, field_a, 2 * DMAX2, dils[1] + dils[2], keep(field_b, dils[1], True))
    clear(field_b, 2 * DMAX2)
    tower(1, field_b, DMAX2, dils[2], keep(field_a, dils[2], True))
    clear(field_a, DMAX2)
    tower(2, field_a, 0, 0, keep_last)

    @pl.loop(0, tile_rows // 16)
    def _(block):
        first = pl.multiple_of(block * 16, 16)
        for c in range(chans):
            taken = final[pl.ds(first * PITCH + c, 16, stride=PITCH), :]
            out[c, pl.ds(first, 16), :] = taken.astype(jnp.bfloat16)


def banded(map_weight, map_bias):
    layers, _, _, outs, ins = map_weight.shape
    taps = jnp.transpose(map_weight, (0, 3, 1, 2, 4)).reshape(layers, outs, 9 * ins)
    left = map_bias
    split = []
    for _ in range(3):
        split.append(lax.reduce_precision(left, 8, 7))
        left = left - split[-1]
    split = jnp.stack(split, axis=2).astype(jnp.bfloat16)
    rows = []
    for k in range(GROUP):
        before, after = k * 3 * ins, (GROUP - 1 - k) * 3 * ins
        row = jnp.pad(taps, ((0, 0), (0, 0), (before, after)))
        rows.append(jnp.concatenate([row, jnp.pad(split, ((0, 0), (0, 0), (0, TAIL - 3)))], axis=2))
    return jnp.concatenate(rows, axis=1)


def pair_call(place, gathered, dist_gain, bands, tile_rows, tile_cols):
    chans = dist_gain.shape[0]
    smem = pl.BlockSpec(memory_space=pltpu.SMEM)
    vmem = pl.BlockSpec(memory_space=pltpu.VMEM)
    span = tile_rows + 6 * DMAX2
    return pl.pallas_call(
        functools.partial(pair_kernel, gathered.shape[0], place.shape[0] - 3),
        out_shape=jax.ShapeDtypeStruct((chans, tile_rows, tile_cols), jnp.bfloat16),
        in_specs=[smem] + [vmem] * 3,
        out_specs=vmem,
        scratch_shapes=[
            pltpu.VMEM((-(-span // 128), chans, 128), jnp.float32),
            pltpu.VMEM((span, LANES), jnp.float32),
            pltpu.VMEM((span, 3 * chans, LANES), jnp.bfloat16),
            pltpu.VMEM((span - 2 * DMAX2, 3 * chans, LANES), jnp.bfloat16),
            pltpu.VMEM((tile_rows * PITCH, 128), jnp.float32),
            pltpu.VMEM((GROUP * chans, WIDE * LANES), jnp.float32),
        ],
        compiler_params=pltpu.CompilerParams(vmem_limit_bytes=48 * 2**20),
        cost_estimate=pl.CostEstimate(
            flops=3 * 2 * tile_rows * 9 * chans * chans * LANES,
            bytes_accessed=tile_rows * tile_cols * chans * 2,
            transcendentals=0,
        ),
        name="pair_tower",
    )(
        place, gathered, dist_gain.reshape(chans, 1), bands,
    )


def on_device(
    features,
    tower_weight,
    tower_bias,
    pair_proj,
    dist_gain,
    map_weight,
    map_bias,
    dilations,
    start_bin,
):
    row_count = lax.axis_size("rows")
    col_count = lax.axis_size("cols")
    shards = row_count * col_count
    shard, width = features.shape
    total = shard * shards
    tile_rows = total // row_count
    tile_cols = total // col_count
    chans = map_weight.shape[-1]
    row_place = lax.axis_index("rows")
    col_place = lax.axis_index("cols")
    mine = row_place * col_count + col_place
    place = jnp.stack([mine, row_place, col_place, row_count, col_count]).astype(jnp.int32)
    place = jnp.concatenate([place, dilations])

    def moved(step):
        pairs = [(i, i + step) for i in range(shards) if 0 <= i + step < shards]
        return lax.ppermute(features, AXES, pairs)

    up2, up1, down1, down2 = moved(2), moved(1), moved(-1), moved(-2)
    code = position_code(mine * shard + jnp.arange(shard), start_bin[0], chans)
    code = jnp.pad(code, ((0, 0), (0, width - chans)))
    extra = jnp.concatenate([tower_bias, code], axis=0)
    near = jnp.concatenate([features, pair_proj.T], axis=0)
    bands = banded(map_weight, map_bias)

    smem = pl.BlockSpec(memory_space=pltpu.SMEM)
    vmem = pl.BlockSpec(memory_space=pltpu.VMEM)
    parts = pl.pallas_call(
        functools.partial(encode_kernel, total),
        out_shape=jax.ShapeDtypeStruct((shards, shard // 2, 4 * chans), jnp.bfloat16),
        in_specs=[smem] + [vmem] * 6 + [pl.BlockSpec(memory_space=pltpu.HBM)],
        out_specs=vmem,
        scratch_shapes=[
            pltpu.VMEM(tower_weight.shape, tower_weight.dtype),
            pltpu.VMEM((width // 128, 5 * shard, 128), jnp.float32),
            pltpu.VMEM((width // 128, 3 * shard, 128), jnp.float32),
            pltpu.SemaphoreType.DMA(tower_weight.shape[:2]),
        ],
        compiler_params=pltpu.CompilerParams(vmem_limit_bytes=52 * 2**20),
        cost_estimate=pl.CostEstimate(
            flops=2 * 4 * shard * 3 * width * width,
            bytes_accessed=6 * width * width * 2,
            transcendentals=0,
        ),
        name="encode",
    )(
        place, up2, up1, down1, down2, near, extra, tower_weight,
    )

    gathered = lax.all_to_all(parts, AXES, split_axis=0, concat_axis=0, tiled=True)
    return pair_call(
        place, gathered, dist_gain, bands, tile_rows, tile_cols
    )


def solution(mesh):
    placed = (P(AXES, None), P(), P(), P(), P(), P(), P(), P(), P())
    return jax.shard_map(
        on_device, mesh=mesh, in_specs=placed, out_specs=P(None, "rows", "cols"), check_vma=False
    )
```

```python
import functools
import math

import jax
import jax.numpy as jnp
from jax import lax
from jax.experimental import pallas as pl
from jax.experimental.pallas import tpu as pltpu
from jax.sharding import PartitionSpec as P

DMAX1 = 16
DMAX2 = 16
GROUP = 4
TAIL = 32
WIDE = 2
UNROLL = 4
LANES = 256
PITCH = 40
OUTSIDE = -1e30
AXES = ("rows", "cols")


def position_code(bin_index, start_pos, map_width):
    half_width = map_width // 2
    position = ((start_pos + bin_index) % 8192).astype(jnp.float32)
    rates = jnp.exp(-jnp.arange(half_width).astype(jnp.float32) * (math.log(1000.0) / half_width))
    phase_angle = position[:, None] * rates[None, :]
    return jnp.concatenate([jnp.cos(phase_angle), jnp.sin(phase_angle)], axis=1)


def encode_kernel(
    total, place, inner1, outer1, inner2, outer2, near, extra, weight_far, out, none_16, none_32,
    weight, wide, mid, arrived,
):
    count = inner1.shape[0]
    bias = extra[:2, :]
    proj = near[count:, :]
    fetch = [
        [
            pltpu.make_async_copy(
                weight_far.at[which, tap], weight.at[which, tap], arrived.at[which, tap]
            )
            for tap in range(3)
        ]
        for which in range(2)
    ]
    for copy in fetch[0] + fetch[1]:
        copy.start()
    chunks = wide.shape[0]

    def keep(ref, first, value):
        for k in range(chunks):
            ref[k, pl.ds(first, value.shape[0]), :] = value[:, k * 128 : (k + 1) * 128]

    def run(ref, first, span):
        return jnp.concatenate([ref[k, pl.ds(first, span), :] for k in range(chunks)], axis=1)

    def layer(which, ref, span):
        running = jnp.zeros((span, chunks * 128), jnp.float32)
        for tap in range(3):
            rows = run(ref, count + (tap - 1) * place[5 + which], span).astype(jnp.bfloat16)
            fetch[which][tap].wait()
            running += jnp.dot(rows, weight[which, tap], preferred_element_type=jnp.float32)
        return run(ref, count, span) + jnp.maximum(running + bias[which : which + 1, :], 0.0)

    odd = place[0] % 2
    for side, ref in ((2, near), (3 - 2 * odd, inner1), (1 + 2 * odd, outer1),
                      (4 - 4 * odd, inner2), (4 * odd, outer2)):
        first = side * count
        if ref is not near:
            first = pl.multiple_of(first, count)
        keep(wide, first, ref[:count, :].astype(jnp.float32))
    value = layer(0, wide, 3 * count).astype(jnp.bfloat16).astype(jnp.float32)
    index = (place[0] - 1) * count + lax.broadcasted_iota(jnp.int32, value.shape, 0)
    keep(mid, 0, jnp.where((index >= 0) & (index < total), value, 0.0))
    value = layer(1, mid, count)
    parts = lax.dot_general(
        value.astype(jnp.bfloat16),
        proj,
        (((1,), (1,)), ((), ())),
        preferred_element_type=jnp.float32,
    )
    parts = (parts + extra[2 : 2 + count, : proj.shape[0]]).astype(jnp.bfloat16)
    parts = jnp.concatenate([parts[: count // 2], parts[count // 2 :]], axis=1)
    out[...] = jnp.broadcast_to(parts[None], out.shape)
    none_16[...] = jnp.zeros(none_16.shape, none_16.dtype)
    none_32[...] = jnp.zeros(none_32.shape, none_32.dtype)


def pair_kernel(
    total_shards, first_dil, place, parts, gain, weight, out,
    row_turned, distance, field_a, field_b, final, held,
):
    shard = 2 * parts.shape[1]
    chans = gain.shape[0]
    tile_rows = out.shape[1]
    margin = 3 * DMAX2
    reach = margin // shard
    row_place, col_place = place[1], place[2]
    last_row = place[3] - 1
    row_first = row_place * tile_rows
    col_first = col_place * 128
    dils = [place[first_dil + k] for k in range(3)]

    def pieces(first, count, wrap):
        taken = []
        for k in range(count):
            step = k - count if k >= wrap else k
            both = parts[jnp.clip(first + step, 0, total_shards - 1)]
            taken += [both[:, : 2 * chans], both[:, 2 * chans :]]
        return jnp.concatenate(taken, axis=0).astype(jnp.float32)

    lane = lax.broadcasted_iota(jnp.int32, (1, LANES), 1)
    col_local = jnp.where(lane < LANES - margin - 8, lane, lane - LANES)
    col_glob = col_first + col_local
    inside = (col_glob >= 0) & (col_glob < total_shards * shard)
    inside_high = jnp.where(inside[:, 128:], 1.0, 0.0)
    inside_high = jnp.broadcast_to(inside_high, (chans, 128)).astype(jnp.bfloat16)

    cols = pieces(col_first // shard, LANES // shard, LANES // shard - reach)
    col_turned = jnp.transpose(cols)[chans : 2 * chans, :]
    col_turned = jnp.where(inside, col_turned, OUTSIDE)
    span0 = tile_rows + 2 * margin
    blocks = -(-span0 // 128)
    rows = pieces(row_first // shard - reach, blocks * 128 // shard, blocks * 128)
    rows = jnp.transpose(rows)[:chans, :]
    row_glob = row_first - margin + lax.broadcasted_iota(jnp.int32, (1, blocks * 128), 1)
    rows = jnp.where((row_glob >= 0) & (row_glob < total_shards * shard), rows, OUTSIDE)
    for k in range(blocks):
        row_turned[k] = rows[:, k * 128 : (k + 1) * 128]

    row_local = lax.broadcasted_iota(jnp.int32, (span0, LANES), 0) - margin
    apart = jnp.abs(row_first + row_local - col_glob)
    distance[...] = jnp.log(1.0 + apart.astype(jnp.float32)) * 0.125
    gain_wide = jnp.broadcast_to(gain[...], (chans, LANES))
    lane16 = lax.broadcasted_iota(jnp.int16, (chans, 128), 1)

    def keep(field, d, masked):
        back = 128 - d
        at_left = lane16 < d.astype(jnp.int16)
        at_right = lane16 >= back.astype(jnp.int16)

        def store(i, low, high):
            low = low.astype(jnp.bfloat16)
            high = high.astype(jnp.bfloat16)
            if masked:
                high = high * inside_high
            field[i, chans : 2 * chans, :128] = low
            field[i, chans : 2 * chans, 128:] = high
            turned_low, turned_high = pltpu.roll(low, d, 1), pltpu.roll(high, d, 1)
            field[i, :chans, :128] = jnp.where(at_left, turned_high, turned_low)
            field[i, :chans, 128:] = jnp.where(at_left, turned_low, turned_high)
            turned_low, turned_high = pltpu.roll(low, back, 1), pltpu.roll(high, back, 1)
            field[i, 2 * chans :, :128] = jnp.where(at_right, turned_high, turned_low)
            field[i, 2 * chans :, 128:] = jnp.where(at_right, turned_low, turned_high)

        return store

    def clear(field, extra):
        @pl.when(row_place == 0)
        def _():
            @pl.loop(0, extra)
            def _(i):
                field[i] = jnp.zeros(field.shape[1:], field.dtype)

        @pl.when(row_place == last_row)
        def _():
            @pl.loop(0, extra)
            def _(i):
                field[extra + tile_rows + i] = jnp.zeros(field.shape[1:], field.dtype)

    need = dils[0] + dils[1] + dils[2]
    store_first = keep(field_a, dils[0], False)
    first_row, last_row_needed = margin - need, margin + tile_rows + need - 1

    def build(index, count):
        for k in range(count):
            i = jnp.minimum(first_row + index + k, last_row_needed)
            pick = jnp.full((chans, 128), i % 128, jnp.int32)
            row_term = jnp.take_along_axis(row_turned[i // 128], pick, axis=1)
            row_term = jnp.concatenate([row_term, row_term], axis=1)
            value = row_term + col_turned + gain_wide * distance[pl.ds(i, 1), :]
            value = jnp.maximum(value, 0.0)
            store_first(i, value[:, :128], value[:, 128:])

    @pl.loop(0, (last_row_needed - first_row + 8) // 8)
    def _(block):
        build(block * 8, 8)

    tail = jnp.ones((TAIL, WIDE * LANES), jnp.bfloat16)

    def tower(layer, source, extra, need, store):
        d = dils[layer]
        span = GROUP * d
        first = extra - need
        count = tile_rows + 2 * need
        final_layer = layer == 2
        width = 128 if final_layer else LANES
        each = WIDE * LANES // width

        def product(bases):
            taps = []
            for k in range(GROUP + 2):
                at = [base + DMAX2 + (k - 1) * d for base in bases]
                taps.append(jnp.concatenate([source[i, :, :width] for i in at], axis=1))
            stack = jnp.concatenate(taps + [tail], axis=0)
            return jnp.dot(weight[layer], stack, preferred_element_type=jnp.float32)

        def finish(bases, sums):
            for n, base in enumerate(bases):
                for k in range(GROUP):
                    at = slice(n * width, (n + 1) * width)
                    center = source[base + DMAX2 + k * d, chans : 2 * chans, :width]
                    value = sums[k * chans : (k + 1) * chans, at]
                    value = center.astype(jnp.float32) + jnp.maximum(value, 0.0)
                    if final_layer:
                        store(base + k * d, value)
                    else:
                        store(base + k * d, value[:, :128], value[:, 128:])

        def walk(start, phase):
            bases = []
            for _ in range(each):
                bases.append(first + jnp.minimum(start, count - span) + phase)
                wrap = phase + 1 >= d
                start = jnp.where(wrap, start + span, start)
                phase = jnp.where(wrap, 0, phase + 1)
            return bases, start, phase

        def step(_, carry):
            start, phase, bases = carry
            sums = held
            for k in range(UNROLL):
                next_bases, start, phase = walk(start, phase)
                next_sums = product(next_bases)
                finish(bases, sums)
                bases, sums = next_bases, next_sums
            held[...] = sums
            return start, phase, bases

        zero = jnp.int32(0)
        total = (count + span - 1) // span * d
        steps = (total + UNROLL * each - 1) // (UNROLL * each)
        carry = lax.fori_loop(0, steps, step, (zero, zero, walk(zero, zero)[0]))
        finish(carry[2], held)

    def keep_last(i, low):
        final[pl.ds(pl.multiple_of(i * PITCH, 8), chans), :] = low

    tower(0, field_a, 2 * DMAX2, dils[1] + dils[2], keep(field_b, dils[1], True))
    clear(field_b, 2 * DMAX2)
    tower(1, field_b, DMAX2, dils[2], keep(field_a, dils[2], True))
    clear(field_a, DMAX2)
    tower(2, field_a, 0, 0, keep_last)

    @pl.loop(0, tile_rows // 16)
    def _(block):
        first = pl.multiple_of(block * 16, 16)
        for c in range(chans):
            taken = final[pl.ds(first * PITCH + c, 16, stride=PITCH), :]
            out[c, pl.ds(first, 16), :] = taken.astype(jnp.bfloat16)


def banded(map_weight, map_bias):
    layers, _, _, outs, ins = map_weight.shape
    taps = jnp.transpose(map_weight, (0, 3, 1, 2, 4)).reshape(layers, outs, 9 * ins)
    left = map_bias
    split = []
    for _ in range(3):
        split.append(lax.reduce_precision(left, 8, 7))
        left = left - split[-1]
    split = jnp.stack(split, axis=2).astype(jnp.bfloat16)
    rows = []
    for k in range(GROUP):
        before, after = k * 3 * ins, (GROUP - 1 - k) * 3 * ins
        row = jnp.pad(taps, ((0, 0), (0, 0), (before, after)))
        rows.append(jnp.concatenate([row, jnp.pad(split, ((0, 0), (0, 0), (0, TAIL - 3)))], axis=2))
    return jnp.concatenate(rows, axis=1)


def pair_call(place, gathered, dist_gain, bands, tile_rows, tile_cols):
    chans = dist_gain.shape[0]
    smem = pl.BlockSpec(memory_space=pltpu.SMEM)
    vmem = pl.BlockSpec(memory_space=pltpu.VMEM)
    span = tile_rows + 6 * DMAX2
    return pl.pallas_call(
        functools.partial(pair_kernel, gathered.shape[0], place.shape[0] - 3),
        out_shape=jax.ShapeDtypeStruct((chans, tile_rows, tile_cols), jnp.bfloat16),
        in_specs=[smem] + [vmem] * 3,
        out_specs=vmem,
        scratch_shapes=[
            pltpu.VMEM((-(-span // 128), chans, 128), jnp.float32),
            pltpu.VMEM((span, LANES), jnp.float32),
            pltpu.VMEM((span, 3 * chans, LANES), jnp.bfloat16),
            pltpu.VMEM((span - 2 * DMAX2, 3 * chans, LANES), jnp.bfloat16),
            pltpu.VMEM((tile_rows * PITCH, 128), jnp.float32),
            pltpu.VMEM((GROUP * chans, WIDE * LANES), jnp.float32),
        ],
        compiler_params=pltpu.CompilerParams(vmem_limit_bytes=48 * 2**20),
        cost_estimate=pl.CostEstimate(
            flops=3 * 2 * tile_rows * 9 * chans * chans * LANES,
            bytes_accessed=tile_rows * tile_cols * chans * 2,
            transcendentals=0,
        ),
        name="pair_tower",
    )(
        place, gathered, dist_gain.reshape(chans, 1), bands,
    )


def on_device(
    features,
    tower_weight,
    tower_bias,
    pair_proj,
    dist_gain,
    map_weight,
    map_bias,
    dilations,
    start_bin,
):
    row_count = lax.axis_size("rows")
    col_count = lax.axis_size("cols")
    shards = row_count * col_count
    shard, width = features.shape
    total = shard * shards
    tile_rows = total // row_count
    tile_cols = total // col_count
    chans = map_weight.shape[-1]
    row_place = lax.axis_index("rows")
    col_place = lax.axis_index("cols")
    mine = row_place * col_count + col_place
    place = jnp.stack([mine, row_place, col_place, row_count, col_count]).astype(jnp.int32)
    place = jnp.concatenate([place, dilations])

    inner = [(i, i ^ 1) for i in range(shards)]
    outer = [(i, i + 1 if i % 2 else i - 1) for i in range(1, shards - 1)]
    inner1 = lax.ppermute(features, AXES, inner)
    outer1 = lax.ppermute(features, AXES, outer)
    outer2 = lax.ppermute(inner1, AXES, outer)
    inner2 = lax.ppermute(outer1, AXES, inner)
    code = position_code(mine * shard + jnp.arange(shard), start_bin[0], chans)
    code = jnp.pad(code, ((0, 0), (0, width - chans)))
    extra = jnp.concatenate([tower_bias, code], axis=0)
    near = jnp.concatenate([features, pair_proj.T], axis=0)

    smem = pl.BlockSpec(memory_space=pltpu.SMEM)
    vmem = pl.BlockSpec(memory_space=pltpu.VMEM)
    parts, none_16, none_32 = pl.pallas_call(
        functools.partial(encode_kernel, total),
        out_shape=[
            jax.ShapeDtypeStruct((shards, shard // 2, 4 * chans), jnp.bfloat16),
            jax.ShapeDtypeStruct(map_weight.shape, map_weight.dtype),
            jax.ShapeDtypeStruct((map_bias.shape[0] + 1, chans), jnp.float32),
        ],
        in_specs=[smem] + [vmem] * 6 + [pl.BlockSpec(memory_space=pltpu.HBM)],
        out_specs=[vmem] * 3,
        scratch_shapes=[
            pltpu.VMEM(tower_weight.shape, tower_weight.dtype),
            pltpu.VMEM((width // 128, 5 * shard, 128), jnp.float32),
            pltpu.VMEM((width // 128, 3 * shard, 128), jnp.float32),
            pltpu.SemaphoreType.DMA(tower_weight.shape[:2]),
        ],
        compiler_params=pltpu.CompilerParams(vmem_limit_bytes=52 * 2**20),
        cost_estimate=pl.CostEstimate(
            flops=2 * 4 * shard * 3 * width * width,
            bytes_accessed=6 * width * width * 2,
            transcendentals=0,
        ),
        name="encode",
    )(
        place, inner1, outer1, inner2, outer2, near, extra, tower_weight,
    )

    gathered = lax.all_to_all(parts, AXES, split_axis=0, concat_axis=0, tiled=True)

    bands = banded(map_weight + none_16, map_bias + none_32[:-1])
    dist_gain = dist_gain + none_32[-1]

    return pair_call(
        place, gathered, dist_gain, bands, tile_rows, tile_cols
    )


def solution(mesh):
    placed = (P(AXES, None), P(), P(), P(), P(), P(), P(), P(), P())
    return jax.shard_map(
        on_device, mesh=mesh, in_specs=placed, out_specs=P(None, "rows", "cols"), check_vma=False
    )
```

```python
import functools
import math

import jax
import jax.numpy as jnp
from jax import lax
from jax.experimental import pallas as pl
from jax.experimental.pallas import tpu as pltpu
from jax.sharding import PartitionSpec as P

DMAX1 = 16
DMAX2 = 16
GROUP = 4
TAIL = 32
WIDE = 2
UNROLL = 4
LANES = 256
PITCH = 40
CHUNK = 64
OUTSIDE = -1e30
AXES = ("rows", "cols")


def position_code(bin_index, start_pos, map_width):
    half_width = map_width // 2
    position = ((start_pos + bin_index) % 8192).astype(jnp.float32)
    rates = jnp.exp(-jnp.arange(half_width).astype(jnp.float32) * (math.log(1000.0) / half_width))
    phase_angle = position[:, None] * rates[None, :]
    return jnp.concatenate([jnp.cos(phase_angle), jnp.sin(phase_angle)], axis=1)


def encode_kernel(
    total, place, both, outer, inner, proj, extra, weight_far, out, none_16, none_32,
    weight, wide, mid, arrived,
):
    count = both.shape[0] // 2
    bias = extra[:2, :]
    fetch = [
        [
            pltpu.make_async_copy(
                weight_far.at[which, tap], weight.at[which, tap], arrived.at[which, tap]
            )
            for tap in range(3)
        ]
        for which in range(2)
    ]
    for copy in fetch[0] + fetch[1]:
        copy.start()
    chunks = wide.shape[0]

    def keep(ref, first, value):
        for k in range(chunks):
            ref[k, pl.ds(first, value.shape[0]), :] = value[:, k * 128 : (k + 1) * 128]

    def run(ref, first, span):
        return jnp.concatenate([ref[k, pl.ds(first, span), :] for k in range(chunks)], axis=1)

    def layer(which, ref, span):
        running = jnp.zeros((span, chunks * 128), jnp.float32)
        for tap in range(3):
            rows = run(ref, count + (tap - 1) * place[5 + which], span).astype(jnp.bfloat16)
            fetch[which][tap].wait()
            running += jnp.dot(rows, weight[which, tap], preferred_element_type=jnp.float32)
        return run(ref, count, span) + jnp.maximum(running + bias[which : which + 1, :], 0.0)

    odd = place[0] % 2
    for side, ref, half in ((2, both, 0), (3 - 2 * odd, both, 1), (1 + 2 * odd, outer, 0),
                            (4 * odd, outer, 1), (4 - 4 * odd, inner, 0)):
        first = side * count
        if ref is not both or half:
            first = pl.multiple_of(first, count)
        keep(wide, first, ref[half * count : (half + 1) * count, :].astype(jnp.float32))
    value = layer(0, wide, 3 * count).astype(jnp.bfloat16).astype(jnp.float32)
    index = (place[0] - 1) * count + lax.broadcasted_iota(jnp.int32, value.shape, 0)
    keep(mid, 0, jnp.where((index >= 0) & (index < total), value, 0.0))
    value = layer(1, mid, count)
    parts = lax.dot_general(
        value.astype(jnp.bfloat16),
        proj[...],
        (((1,), (1,)), ((), ())),
        preferred_element_type=jnp.float32,
    )
    parts = (parts + extra[2 : 2 + count, : proj.shape[0]]).astype(jnp.bfloat16)
    parts = parts[:, : proj.shape[0] // 2]
    parts = jnp.concatenate([parts[: count // 2], parts[count // 2 :]], axis=1)
    out[...] = jnp.broadcast_to(parts[None], out.shape)
    none_16[...] = jnp.zeros(none_16.shape, none_16.dtype)
    none_32[...] = jnp.zeros(none_32.shape, none_32.dtype)


def local_columns(rows):
    lane = lax.broadcasted_iota(jnp.int32, (rows, LANES), 1)
    return jnp.where(lane < LANES - 3 * DMAX2 - 8, lane, lane - LANES)


def distance_kernel(tile_rows, place, none, out):
    row_first = place[1] * tile_rows - 3 * DMAX2
    row = row_first + lax.broadcasted_iota(jnp.int32, out.shape, 0)
    apart = jnp.abs(row - (place[2] * 128 + local_columns(out.shape[0])))
    out[...] = jnp.log(1.0 + apart.astype(jnp.float32)) * 0.125 + none[0, 0]


def pair_kernel(
    total_shards, first_dil, place, parts, distance, gain, weight, out_far,
    row_turned, field_a, field_b, final, held, out, sent,
):
    shard = 2 * parts.shape[1]
    chans = gain.shape[0]
    tile_rows = out.shape[1]
    margin = 3 * DMAX2
    reach = margin // shard
    row_place, col_place = place[1], place[2]
    last_row = place[3] - 1
    row_first = row_place * tile_rows
    col_first = col_place * 128
    dils = [place[first_dil + k] for k in range(3)]

    def pieces(first, count, wrap):
        taken = []
        for k in range(count):
            step = k - count if k >= wrap else k
            both = parts[jnp.clip(first + step, 0, total_shards - 1)]
            taken += [both[:, : 2 * chans], both[:, 2 * chans :]]
        return jnp.concatenate(taken, axis=0).astype(jnp.float32)

    col_glob = col_first + local_columns(1)
    inside = (col_glob >= 0) & (col_glob < total_shards * shard)
    inside_high = jnp.where(inside[:, 128:], 1.0, 0.0)
    inside_high = jnp.broadcast_to(inside_high, (chans, 128)).astype(jnp.bfloat16)

    cols = pieces(col_first // shard, LANES // shard, LANES // shard - reach)
    col_turned = jnp.transpose(cols)[chans : 2 * chans, :]
    col_turned = jnp.where(inside, col_turned, OUTSIDE)
    span0 = tile_rows + 2 * margin
    blocks = -(-span0 // 128)
    rows = pieces(row_first // shard - reach, blocks * 128 // shard, blocks * 128)
    rows = jnp.transpose(rows)[:chans, :]
    row_glob = row_first - margin + lax.broadcasted_iota(jnp.int32, (1, blocks * 128), 1)
    rows = jnp.where((row_glob >= 0) & (row_glob < total_shards * shard), rows, OUTSIDE)
    for k in range(blocks):
        row_turned[k] = rows[:, k * 128 : (k + 1) * 128]

    gain_wide = jnp.broadcast_to(gain[...], (chans, LANES))
    lane16 = lax.broadcasted_iota(jnp.int16, (chans, 128), 1)

    def keep(field, d, masked):
        back = 128 - d
        at_left = lane16 < d.astype(jnp.int16)
        at_right = lane16 >= back.astype(jnp.int16)

        def store(i, low, high):
            low = low.astype(jnp.bfloat16)
            high = high.astype(jnp.bfloat16)
            if masked:
                high = high * inside_high
            field[i, chans : 2 * chans, :128] = low
            field[i, chans : 2 * chans, 128:] = high
            turned_low, turned_high = pltpu.roll(low, d, 1), pltpu.roll(high, d, 1)
            field[i, :chans, :128] = jnp.where(at_left, turned_high, turned_low)
            field[i, :chans, 128:] = jnp.where(at_left, turned_low, turned_high)
            turned_low, turned_high = pltpu.roll(low, back, 1), pltpu.roll(high, back, 1)
            field[i, 2 * chans :, :128] = jnp.where(at_right, turned_high, turned_low)
            field[i, 2 * chans :, 128:] = jnp.where(at_right, turned_low, turned_high)

        return store

    def clear(field, extra):
        @pl.when(row_place == 0)
        def _():
            @pl.loop(0, extra)
            def _(i):
                field[i] = jnp.zeros(field.shape[1:], field.dtype)

        @pl.when(row_place == last_row)
        def _():
            @pl.loop(0, extra)
            def _(i):
                field[extra + tile_rows + i] = jnp.zeros(field.shape[1:], field.dtype)

    need = dils[0] + dils[1] + dils[2]
    store_first = keep(field_a, dils[0], False)
    first_row, last_row_needed = margin - need, margin + tile_rows + need - 1

    def build(index, count):
        for k in range(count):
            i = jnp.minimum(first_row + index + k, last_row_needed)
            pick = jnp.full((chans, 128), i % 128, jnp.int32)
            row_term = jnp.take_along_axis(row_turned[i // 128], pick, axis=1)
            row_term = jnp.concatenate([row_term, row_term], axis=1)
            value = row_term + col_turned + gain_wide * distance[pl.ds(i, 1), :]
            value = jnp.maximum(value, 0.0)
            store_first(i, value[:, :128], value[:, 128:])

    @pl.loop(0, (last_row_needed - first_row + 8) // 8)
    def _(block):
        build(block * 8, 8)

    tail = jnp.ones((TAIL, WIDE * LANES), jnp.bfloat16)

    def tower(layer, source, extra, need, store, first_in_step=None):
        d = dils[layer]
        span = GROUP * d
        first = extra - need
        count = tile_rows + 2 * need
        final_layer = layer == 2
        width = 128 if final_layer else LANES
        each = WIDE * LANES // width

        def product(bases):
            taps = []
            for k in range(GROUP + 2):
                at = [base + DMAX2 + (k - 1) * d for base in bases]
                taps.append(jnp.concatenate([source[i, :, :width] for i in at], axis=1))
            stack = jnp.concatenate(taps + [tail], axis=0)
            return jnp.dot(weight[layer], stack, preferred_element_type=jnp.float32)

        def finish(bases, sums):
            for n, base in enumerate(bases):
                for k in range(GROUP):
                    at = slice(n * width, (n + 1) * width)
                    center = source[base + DMAX2 + k * d, chans : 2 * chans, :width]
                    value = sums[k * chans : (k + 1) * chans, at]
                    value = center.astype(jnp.float32) + jnp.maximum(value, 0.0)
                    if final_layer:
                        store(base + k * d, value)
                    else:
                        store(base + k * d, value[:, :128], value[:, 128:])

        def walk(start, phase):
            bases = []
            for _ in range(each):
                bases.append(first + jnp.minimum(start, count - span) + phase)
                wrap = phase + 1 >= d
                start = jnp.where(wrap, start + span, start)
                phase = jnp.where(wrap, 0, phase + 1)
            return bases, start, phase

        def step(index, carry):
            start, phase, bases = carry
            if first_in_step is not None:
                first_in_step(index)
            sums = held
            for k in range(UNROLL):
                next_bases, start, phase = walk(start, phase)
                next_sums = product(next_bases)
                finish(bases, sums)
                bases, sums = next_bases, next_sums
            held[...] = sums
            return start, phase, bases

        zero = jnp.int32(0)
        total = (count + span - 1) // span * d
        steps = (total + UNROLL * each - 1) // (UNROLL * each)
        carry = lax.fori_loop(0, steps, step, (zero, zero, walk(zero, zero)[0]))
        finish(carry[2], held)

    def keep_last(i, low):
        final[pl.ds(pl.multiple_of(i * PITCH, 8), chans), :] = low

    def turn(chunk):
        @functools.partial(lax.fori_loop, 0, CHUNK // 16, init_val=0, unroll=True)
        def _(block, carry):
            first = pl.multiple_of(chunk * CHUNK + block * 16, 16)
            for c in range(chans):
                taken = final[pl.ds(first * PITCH + c, 16, stride=PITCH), :]
                out[c, pl.ds(first, 16), :] = taken.astype(jnp.bfloat16)
            return carry

    def send(chunk):
        rows = pl.ds(chunk * CHUNK, CHUNK)
        return pltpu.make_async_copy(out.at[:, rows, :], out_far.at[:, rows, :], sent.at[chunk])

    early = 2

    def turn_early(step):
        turn(jnp.clip(step - 2, 0, early - 1))

    tower(0, field_a, 2 * DMAX2, dils[1] + dils[2], keep(field_b, dils[1], True))
    clear(field_b, 2 * DMAX2)
    tower(1, field_b, DMAX2, dils[2], keep(field_a, dils[2], True))
    clear(field_a, DMAX2)
    tower(2, field_a, 0, 0, keep_last, turn_early)

    for k in range(tile_rows // CHUNK):
        if k >= early:
            turn(k)
        send(k).start()
    for k in range(tile_rows // CHUNK):
        send(k).wait()


def banded(map_weight, map_bias):
    layers, _, _, outs, ins = map_weight.shape
    taps = jnp.transpose(map_weight, (0, 3, 1, 2, 4)).reshape(layers, outs, 9 * ins)
    left = map_bias
    split = []
    for _ in range(3):
        split.append(lax.reduce_precision(left, 8, 7))
        left = left - split[-1]
    split = jnp.stack(split, axis=2).astype(jnp.bfloat16)
    rows = []
    for k in range(GROUP):
        before, after = k * 3 * ins, (GROUP - 1 - k) * 3 * ins
        row = jnp.pad(taps, ((0, 0), (0, 0), (before, after)))
        rows.append(jnp.concatenate([row, jnp.pad(split, ((0, 0), (0, 0), (0, TAIL - 3)))], axis=2))
    return jnp.concatenate(rows, axis=1)


def distance_call(place, none, tile_rows):
    return pl.pallas_call(
        functools.partial(distance_kernel, tile_rows),
        out_shape=jax.ShapeDtypeStruct((tile_rows + 6 * DMAX2, LANES), jnp.float32),
        in_specs=[
            pl.BlockSpec(memory_space=pltpu.SMEM),
            pl.BlockSpec(memory_space=pltpu.VMEM),
        ],
        out_specs=pl.BlockSpec(memory_space=pltpu.VMEM),
        name="distances",
    )(place, none)


def pair_call(place, gathered, distance, dist_gain, bands, tile_rows, tile_cols):
    chans = dist_gain.shape[0]
    smem = pl.BlockSpec(memory_space=pltpu.SMEM)
    vmem = pl.BlockSpec(memory_space=pltpu.VMEM)
    span = tile_rows + 6 * DMAX2
    return pl.pallas_call(
        functools.partial(pair_kernel, gathered.shape[0], place.shape[0] - 3),
        out_shape=jax.ShapeDtypeStruct((chans, tile_rows, tile_cols), jnp.bfloat16),
        in_specs=[smem] + [vmem] * 4,
        out_specs=pl.BlockSpec(memory_space=pltpu.HBM),
        scratch_shapes=[
            pltpu.VMEM((-(-span // 128), chans, 128), jnp.float32),
            pltpu.VMEM((span, 3 * chans, LANES), jnp.bfloat16),
            pltpu.VMEM((span - 2 * DMAX2, 3 * chans, LANES), jnp.bfloat16),
            pltpu.VMEM((tile_rows * PITCH, 128), jnp.float32),
            pltpu.VMEM((GROUP * chans, WIDE * LANES), jnp.float32),
            pltpu.VMEM((chans, tile_rows, tile_cols), jnp.bfloat16),
            pltpu.SemaphoreType.DMA((tile_rows // CHUNK,)),
        ],
        compiler_params=pltpu.CompilerParams(vmem_limit_bytes=48 * 2**20),
        cost_estimate=pl.CostEstimate(
            flops=3 * 2 * tile_rows * 9 * chans * chans * LANES,
            bytes_accessed=tile_rows * tile_cols * chans * 2,
            transcendentals=0,
        ),
        name="pair_tower",
    )(
        place, gathered, distance, dist_gain.reshape(chans, 1), bands,
    )


def on_device(
    features,
    tower_weight,
    tower_bias,
    pair_proj,
    dist_gain,
    map_weight,
    map_bias,
    dilations,
    start_bin,
):
    row_count = lax.axis_size("rows")
    col_count = lax.axis_size("cols")
    shards = row_count * col_count
    shard, width = features.shape
    total = shard * shards
    tile_rows = total // row_count
    tile_cols = total // col_count
    chans = map_weight.shape[-1]
    row_place = lax.axis_index("rows")
    col_place = lax.axis_index("cols")
    mine = row_place * col_count + col_place
    place = jnp.stack([mine, row_place, col_place, row_count, col_count]).astype(jnp.int32)
    place = jnp.concatenate([place, dilations])

    inner = [(i, i ^ 1) for i in range(shards)]
    outer = [(i, i + 1 if i % 2 else i - 1) for i in range(1, shards - 1)]
    both = jnp.concatenate([features, lax.ppermute(features, AXES, inner)], axis=0)
    from_outer = lax.ppermute(both, AXES, outer)
    from_inner = lax.ppermute(from_outer, AXES, inner)
    code = position_code(mine * shard + jnp.arange(shard), start_bin[0], chans)
    code = jnp.pad(code, ((0, 0), (0, width - chans)))
    extra = jnp.concatenate([tower_bias, code], axis=0)
    proj = jnp.pad(pair_proj.T, ((0, 2 * chans), (0, 0)))

    smem = pl.BlockSpec(memory_space=pltpu.SMEM)
    vmem = pl.BlockSpec(memory_space=pltpu.VMEM)
    parts, none_16, none_32 = pl.pallas_call(
        functools.partial(encode_kernel, total),
        out_shape=[
            jax.ShapeDtypeStruct((shards, shard // 2, 4 * chans), jnp.bfloat16),
            jax.ShapeDtypeStruct(map_weight.shape, map_weight.dtype),
            jax.ShapeDtypeStruct((map_bias.shape[0] + 1, chans), jnp.float32),
        ],
        in_specs=[smem] + [vmem] * 5 + [pl.BlockSpec(memory_space=pltpu.HBM)],
        out_specs=[vmem] * 3,
        scratch_shapes=[
            pltpu.VMEM(tower_weight.shape, tower_weight.dtype),
            pltpu.VMEM((width // 128, 5 * shard, 128), jnp.float32),
            pltpu.VMEM((width // 128, 3 * shard, 128), jnp.float32),
            pltpu.SemaphoreType.DMA(tower_weight.shape[:2]),
        ],
        compiler_params=pltpu.CompilerParams(vmem_limit_bytes=52 * 2**20),
        cost_estimate=pl.CostEstimate(
            flops=2 * 4 * shard * 3 * width * width,
            bytes_accessed=6 * width * width * 2,
            transcendentals=0,
        ),
        name="encode",
    )(
        place, both, from_outer, from_inner, proj, extra, tower_weight,
    )

    gathered = lax.all_to_all(parts, AXES, split_axis=0, concat_axis=0, tiled=True)

    bands = banded(map_weight + none_16, map_bias + none_32[:-1])
    dist_gain = dist_gain + none_32[-1]

    distance = distance_call(place, none_32, tile_rows)
    return pair_call(
        place, gathered, distance, dist_gain, bands, tile_rows, tile_cols
    )


def solution(mesh):
    placed = (P(AXES, None), P(), P(), P(), P(), P(), P(), P(), P())
    return jax.shard_map(
        on_device, mesh=mesh, in_specs=placed, out_specs=P(None, "rows", "cols"), check_vma=False
    )
```

```python
import functools
import math

import jax
import jax.numpy as jnp
from jax import lax
from jax.experimental import pallas as pl
from jax.experimental.pallas import tpu as pltpu
from jax.sharding import PartitionSpec as P

DMAX1 = 16
DMAX2 = 16
GROUP = 4
TAIL = 32
WIDE = 2
UNROLL = 4
LANES = 256
PITCH = 40
CHUNK = 64
OUTSIDE = -1e30
AXES = ("rows", "cols")


def position_code(bin_index, start_pos, map_width):
    half_width = map_width // 2
    position = ((start_pos + bin_index) % 8192).astype(jnp.float32)
    rates = jnp.exp(-jnp.arange(half_width).astype(jnp.float32) * (math.log(1000.0) / half_width))
    phase_angle = position[:, None] * rates[None, :]
    return jnp.concatenate([jnp.cos(phase_angle), jnp.sin(phase_angle)], axis=1)


def encode_kernel(
    total, place, both, outer, inner, proj, extra, weight_far, out, none_16, none_32,
    weight, wide, mid, arrived,
):
    count = both.shape[0] // 2
    bias = extra[:2, :]
    fetch = [
        [
            pltpu.make_async_copy(
                weight_far.at[which, tap], weight.at[which, tap], arrived.at[which, tap]
            )
            for tap in range(3)
        ]
        for which in range(2)
    ]
    for copy in fetch[0] + fetch[1]:
        copy.start()
    chunks = wide.shape[0]

    def keep(ref, first, value):
        for k in range(chunks):
            ref[k, pl.ds(first, value.shape[0]), :] = value[:, k * 128 : (k + 1) * 128]

    def run(ref, first, span):
        return jnp.concatenate([ref[k, pl.ds(first, span), :] for k in range(chunks)], axis=1)

    def layer(which, ref, span):
        running = jnp.zeros((span, chunks * 128), jnp.float32)
        for tap in range(3):
            rows = run(ref, count + (tap - 1) * place[5 + which], span).astype(jnp.bfloat16)
            fetch[which][tap].wait()
            running += jnp.dot(rows, weight[which, tap], preferred_element_type=jnp.float32)
        return run(ref, count, span) + jnp.maximum(running + bias[which : which + 1, :], 0.0)

    odd = place[0] % 2
    for side, ref, half in ((2, both, 0), (3 - 2 * odd, both, 1), (1 + 2 * odd, outer, 0),
                            (4 * odd, outer, 1), (4 - 4 * odd, inner, 0)):
        first = side * count
        if ref is not both or half:
            first = pl.multiple_of(first, count)
        keep(wide, first, ref[half * count : (half + 1) * count, :].astype(jnp.float32))
    value = layer(0, wide, 3 * count).astype(jnp.bfloat16).astype(jnp.float32)
    index = (place[0] - 1) * count + lax.broadcasted_iota(jnp.int32, value.shape, 0)
    keep(mid, 0, jnp.where((index >= 0) & (index < total), value, 0.0))
    value = layer(1, mid, count)
    parts = lax.dot_general(
        value.astype(jnp.bfloat16),
        proj[...],
        (((1,), (1,)), ((), ())),
        preferred_element_type=jnp.float32,
    )
    parts = (parts + extra[2 : 2 + count, : proj.shape[0]]).astype(jnp.bfloat16)
    parts = parts[:, : proj.shape[0] // 2]
    parts = jnp.concatenate([parts[: count // 2], parts[count // 2 :]], axis=1)
    out[...] = jnp.broadcast_to(parts[None], out.shape)
    none_16[...] = jnp.zeros(none_16.shape, none_16.dtype)
    none_32[...] = jnp.zeros(none_32.shape, none_32.dtype)


def local_columns(rows):
    lane = lax.broadcasted_iota(jnp.int32, (rows, LANES), 1)
    return jnp.where(lane < LANES - 3 * DMAX2 - 8, lane, lane - LANES)


def pair_kernel(
    total_shards, first_dil, place, parts, gain, weight, out_far,
    row_turned, distance, field_a, field_b, final, held, out, sent,
):
    shard = 2 * parts.shape[1]
    chans = gain.shape[0]
    tile_rows = out.shape[1]
    margin = 3 * DMAX2
    reach = margin // shard
    row_place, col_place = place[1], place[2]
    last_row = place[3] - 1
    row_first = row_place * tile_rows
    col_first = col_place * 128
    dils = [place[first_dil + k] for k in range(3)]

    def pieces(first, count, wrap):
        taken = []
        for k in range(count):
            step = k - count if k >= wrap else k
            both = parts[jnp.clip(first + step, 0, total_shards - 1)]
            taken += [both[:, : 2 * chans], both[:, 2 * chans :]]
        return jnp.concatenate(taken, axis=0).astype(jnp.float32)

    col_glob = col_first + local_columns(1)
    inside = (col_glob >= 0) & (col_glob < total_shards * shard)
    inside_high = jnp.where(inside[:, 128:], 1.0, 0.0)
    inside_high = jnp.broadcast_to(inside_high, (chans, 128)).astype(jnp.bfloat16)

    cols = pieces(col_first // shard, LANES // shard, LANES // shard - reach)
    col_turned = jnp.transpose(cols)[chans : 2 * chans, :]
    col_turned = jnp.where(inside, col_turned, OUTSIDE)
    span0 = tile_rows + 2 * margin
    blocks = -(-span0 // 128)
    rows = pieces(row_first // shard - reach, blocks * 128 // shard, blocks * 128)
    rows = jnp.transpose(rows)[:chans, :]
    row_glob = row_first - margin + lax.broadcasted_iota(jnp.int32, (1, blocks * 128), 1)
    rows = jnp.where((row_glob >= 0) & (row_glob < total_shards * shard), rows, OUTSIDE)
    for k in range(blocks):
        row_turned[k] = rows[:, k * 128 : (k + 1) * 128]

    row_local = lax.broadcasted_iota(jnp.int32, (span0, LANES), 0) - margin
    apart = jnp.abs(row_first + row_local - col_glob)
    distance[...] = jnp.log(1.0 + apart.astype(jnp.float32)) * 0.125
    gain_wide = jnp.broadcast_to(gain[...], (chans, LANES))
    lane16 = lax.broadcasted_iota(jnp.int16, (chans, 128), 1)

    def keep(field, d, masked):
        back = 128 - d
        at_left = lane16 < d.astype(jnp.int16)
        at_right = lane16 >= back.astype(jnp.int16)

        def store(i, low, high):
            low = low.astype(jnp.bfloat16)
            high = high.astype(jnp.bfloat16)
            if masked:
                high = high * inside_high
            field[i, chans : 2 * chans, :128] = low
            field[i, chans : 2 * chans, 128:] = high
            turned_low, turned_high = pltpu.roll(low, d, 1), pltpu.roll(high, d, 1)
            field[i, :chans, :128] = jnp.where(at_left, turned_high, turned_low)
            field[i, :chans, 128:] = jnp.where(at_left, turned_low, turned_high)
            turned_low, turned_high = pltpu.roll(low, back, 1), pltpu.roll(high, back, 1)
            field[i, 2 * chans :, :128] = jnp.where(at_right, turned_high, turned_low)
            field[i, 2 * chans :, 128:] = jnp.where(at_right, turned_low, turned_high)

        return store

    def clear(field, extra):
        @pl.when(row_place == 0)
        def _():
            @pl.loop(0, extra)
            def _(i):
                field[i] = jnp.zeros(field.shape[1:], field.dtype)

        @pl.when(row_place == last_row)
        def _():
            @pl.loop(0, extra)
            def _(i):
                field[extra + tile_rows + i] = jnp.zeros(field.shape[1:], field.dtype)

    need = dils[0] + dils[1] + dils[2]
    store_first = keep(field_a, dils[0], False)
    first_row, last_row_needed = margin - need, margin + tile_rows + need - 1

    def build(index, count):
        for k in range(count):
            i = jnp.minimum(first_row + index + k, last_row_needed)
            pick = jnp.full((chans, 128), i % 128, jnp.int32)
            row_term = jnp.take_along_axis(row_turned[i // 128], pick, axis=1)
            row_term = jnp.concatenate([row_term, row_term], axis=1)
            value = row_term + col_turned + gain_wide * distance[pl.ds(i, 1), :]
            value = jnp.maximum(value, 0.0)
            store_first(i, value[:, :128], value[:, 128:])

    @pl.loop(0, (last_row_needed - first_row + 8) // 8)
    def _(block):
        build(block * 8, 8)

    tail = jnp.ones((TAIL, WIDE * LANES), jnp.bfloat16)

    def tower(layer, source, extra, need, store, first_in_step=None):
        d = dils[layer]
        span = GROUP * d
        first = extra - need
        count = tile_rows + 2 * need
        final_layer = layer == 2
        width = 128 if final_layer else LANES
        each = WIDE * LANES // width

        def product(bases):
            taps = []
            for k in range(GROUP + 2):
                at = [base + DMAX2 + (k - 1) * d for base in bases]
                taps.append(jnp.concatenate([source[i, :, :width] for i in at], axis=1))
            stack = jnp.concatenate(taps + [tail], axis=0)
            return jnp.dot(weight[layer], stack, preferred_element_type=jnp.float32)

        def finish(bases, sums):
            for n, base in enumerate(bases):
                for k in range(GROUP):
                    at = slice(n * width, (n + 1) * width)
                    center = source[base + DMAX2 + k * d, chans : 2 * chans, :width]
                    value = sums[k * chans : (k + 1) * chans, at]
                    value = center.astype(jnp.float32) + jnp.maximum(value, 0.0)
                    if final_layer:
                        store(base + k * d, value)
                    else:
                        store(base + k * d, value[:, :128], value[:, 128:])

        def walk(start, phase):
            bases = []
            for _ in range(each):
                bases.append(first + jnp.minimum(start, count - span) + phase)
                wrap = phase + 1 >= d
                start = jnp.where(wrap, start + span, start)
                phase = jnp.where(wrap, 0, phase + 1)
            return bases, start, phase

        def step(index, carry):
            start, phase, bases = carry
            if first_in_step is not None:
                first_in_step(index)
            sums = held
            for k in range(UNROLL):
                next_bases, start, phase = walk(start, phase)
                next_sums = product(next_bases)
                finish(bases, sums)
                bases, sums = next_bases, next_sums
            held[...] = sums
            return start, phase, bases

        zero = jnp.int32(0)
        total = (count + span - 1) // span * d
        steps = (total + UNROLL * each - 1) // (UNROLL * each)
        carry = lax.fori_loop(0, steps, step, (zero, zero, walk(zero, zero)[0]))
        finish(carry[2], held)

    def keep_last(i, low):
        final[pl.ds(pl.multiple_of(i * PITCH, 8), chans), :] = low

    def turn(chunk):
        @functools.partial(lax.fori_loop, 0, CHUNK // 16, init_val=0, unroll=True)
        def _(block, carry):
            first = pl.multiple_of(chunk * CHUNK + block * 16, 16)
            for c in range(chans):
                taken = final[pl.ds(first * PITCH + c, 16, stride=PITCH), :]
                out[c, pl.ds(first, 16), :] = taken.astype(jnp.bfloat16)
            return carry

    def send(chunk):
        rows = pl.ds(chunk * CHUNK, CHUNK)
        return pltpu.make_async_copy(out.at[:, rows, :], out_far.at[:, rows, :], sent.at[chunk])

    early = 2

    def turn_early(step):
        turn(jnp.clip(step - 2, 0, early - 1))

    tower(0, field_a, 2 * DMAX2, dils[1] + dils[2], keep(field_b, dils[1], True))
    clear(field_b, 2 * DMAX2)
    tower(1, field_b, DMAX2, dils[2], keep(field_a, dils[2], True))
    clear(field_a, DMAX2)
    tower(2, field_a, 0, 0, keep_last, turn_early)

    for k in range(tile_rows // CHUNK):
        if k >= early:
            turn(k)
        send(k).start()
    for k in range(tile_rows // CHUNK):
        send(k).wait()


def banded(map_weight, map_bias):
    layers, _, _, outs, ins = map_weight.shape
    taps = jnp.transpose(map_weight, (0, 3, 1, 2, 4)).reshape(layers, outs, 9 * ins)
    left = map_bias
    split = []
    for _ in range(3):
        split.append(lax.reduce_precision(left, 8, 7))
        left = left - split[-1]
    split = jnp.stack(split, axis=2).astype(jnp.bfloat16)
    rows = []
    for k in range(GROUP):
        before, after = k * 3 * ins, (GROUP - 1 - k) * 3 * ins
        row = jnp.pad(taps, ((0, 0), (0, 0), (before, after)))
        rows.append(jnp.concatenate([row, jnp.pad(split, ((0, 0), (0, 0), (0, TAIL - 3)))], axis=2))
    return jnp.concatenate(rows, axis=1)


def pair_call(place, gathered, dist_gain, bands, tile_rows, tile_cols):
    chans = dist_gain.shape[0]
    smem = pl.BlockSpec(memory_space=pltpu.SMEM)
    vmem = pl.BlockSpec(memory_space=pltpu.VMEM)
    span = tile_rows + 6 * DMAX2
    return pl.pallas_call(
        functools.partial(pair_kernel, gathered.shape[0], place.shape[0] - 3),
        out_shape=jax.ShapeDtypeStruct((chans, tile_rows, tile_cols), jnp.bfloat16),
        in_specs=[smem] + [vmem] * 3,
        out_specs=pl.BlockSpec(memory_space=pltpu.HBM),
        scratch_shapes=[
            pltpu.VMEM((-(-span // 128), chans, 128), jnp.float32),
            pltpu.VMEM((span, LANES), jnp.float32),
            pltpu.VMEM((span, 3 * chans, LANES), jnp.bfloat16),
            pltpu.VMEM((span - 2 * DMAX2, 3 * chans, LANES), jnp.bfloat16),
            pltpu.VMEM((tile_rows * PITCH, 128), jnp.float32),
            pltpu.VMEM((GROUP * chans, WIDE * LANES), jnp.float32),
            pltpu.VMEM((chans, tile_rows, tile_cols), jnp.bfloat16),
            pltpu.SemaphoreType.DMA((tile_rows // CHUNK,)),
        ],
        compiler_params=pltpu.CompilerParams(vmem_limit_bytes=48 * 2**20),
        cost_estimate=pl.CostEstimate(
            flops=3 * 2 * tile_rows * 9 * chans * chans * LANES,
            bytes_accessed=tile_rows * tile_cols * chans * 2,
            transcendentals=0,
        ),
        name="pair_tower",
    )(
        place, gathered, dist_gain.reshape(chans, 1), bands,
    )


def on_device(
    features,
    tower_weight,
    tower_bias,
    pair_proj,
    dist_gain,
    map_weight,
    map_bias,
    dilations,
    start_bin,
):
    row_count = lax.axis_size("rows")
    col_count = lax.axis_size("cols")
    shards = row_count * col_count
    shard, width = features.shape
    total = shard * shards
    tile_rows = total // row_count
    tile_cols = total // col_count
    chans = map_weight.shape[-1]
    row_place = lax.axis_index("rows")
    col_place = lax.axis_index("cols")
    mine = row_place * col_count + col_place
    place = jnp.stack([mine, row_place, col_place, row_count, col_count]).astype(jnp.int32)
    place = jnp.concatenate([place, dilations])

    inner = [(i, i ^ 1) for i in range(shards)]
    outer = [(i, i + 1 if i % 2 else i - 1) for i in range(1, shards - 1)]
    brought = lax.ppermute(features, AXES, inner)
    brought, start_bin = lax.optimization_barrier((brought, start_bin))
    both = jnp.concatenate([features, brought], axis=0)
    from_outer = lax.ppermute(both, AXES, outer)
    code = position_code(mine * shard + jnp.arange(shard), start_bin[0], chans)
    code = jnp.pad(code, ((0, 0), (0, width - chans)))
    extra = jnp.concatenate([tower_bias, code], axis=0)
    proj = jnp.pad(pair_proj.T, ((0, 2 * chans), (0, 0)))
    from_outer, extra, proj, place = lax.optimization_barrier((from_outer, extra, proj, place))
    from_inner = lax.ppermute(from_outer, AXES, inner)

    smem = pl.BlockSpec(memory_space=pltpu.SMEM)
    vmem = pl.BlockSpec(memory_space=pltpu.VMEM)
    parts, none_16, none_32 = pl.pallas_call(
        functools.partial(encode_kernel, total),
        out_shape=[
            jax.ShapeDtypeStruct((shards, shard // 2, 4 * chans), jnp.bfloat16),
            jax.ShapeDtypeStruct(map_weight.shape, map_weight.dtype),
            jax.ShapeDtypeStruct((map_bias.shape[0] + 1, chans), jnp.float32),
        ],
        in_specs=[smem] + [vmem] * 5 + [pl.BlockSpec(memory_space=pltpu.HBM)],
        out_specs=[vmem] * 3,
        scratch_shapes=[
            pltpu.VMEM(tower_weight.shape, tower_weight.dtype),
            pltpu.VMEM((width // 128, 5 * shard, 128), jnp.float32),
            pltpu.VMEM((width // 128, 3 * shard, 128), jnp.float32),
            pltpu.SemaphoreType.DMA(tower_weight.shape[:2]),
        ],
        compiler_params=pltpu.CompilerParams(vmem_limit_bytes=52 * 2**20),
        cost_estimate=pl.CostEstimate(
            flops=2 * 4 * shard * 3 * width * width,
            bytes_accessed=6 * width * width * 2,
            transcendentals=0,
        ),
        name="encode",
    )(
        place, both, from_outer, from_inner, proj, extra, tower_weight,
    )

    gathered = lax.all_to_all(parts, AXES, split_axis=0, concat_axis=0, tiled=True)

    bands = banded(map_weight + none_16, map_bias + none_32[:-1])
    dist_gain = dist_gain + none_32[-1]

    return pair_call(
        place, gathered, dist_gain, bands, tile_rows, tile_cols
    )


def solution(mesh):
    placed = (P(AXES, None), P(), P(), P(), P(), P(), P(), P(), P())
    return jax.shard_map(
        on_device, mesh=mesh, in_specs=placed, out_specs=P(None, "rows", "cols"), check_vma=False
    )
```

```python
import functools
import math

import jax
import jax.numpy as jnp
from jax import lax
from jax.experimental import pallas as pl
from jax.experimental.pallas import tpu as pltpu
from jax.sharding import PartitionSpec as P

DMAX1 = 16
DMAX2 = 16
GROUP = 4
TAIL = 32
WIDE = 2
UNROLL = 4
LANES = 256
PITCH = 40
FETCH_LIMIT = 50
CHUNK = 64
OUTSIDE = -1e30
AXES = ("rows", "cols")


def position_code(bin_index, start_pos, map_width):
    half_width = map_width // 2
    position = ((start_pos + bin_index) % 8192).astype(jnp.float32)
    rates = jnp.exp(-jnp.arange(half_width).astype(jnp.float32) * (math.log(1000.0) / half_width))
    phase_angle = position[:, None] * rates[None, :]
    return jnp.concatenate([jnp.cos(phase_angle), jnp.sin(phase_angle)], axis=1)


def fetch_kernel(far, near, arrived):
    copies = [
        pltpu.make_async_copy(far.at[which, tap], near.at[which, tap], arrived.at[which, tap])
        for which in range(far.shape[0])
        for tap in range(far.shape[1])
    ]
    for copy in copies:
        copy.start()
    for copy in copies:
        copy.wait()


def fetch_call(far):
    return pl.pallas_call(
        fetch_kernel,
        out_shape=jax.ShapeDtypeStruct(far.shape, far.dtype),
        in_specs=[pl.BlockSpec(memory_space=pltpu.HBM)],
        out_specs=pl.BlockSpec(memory_space=pltpu.VMEM),
        scratch_shapes=[pltpu.SemaphoreType.DMA(far.shape[:2])],
        compiler_params=pltpu.CompilerParams(vmem_limit_bytes=FETCH_LIMIT * 2**20),
        name="fetch",
    )(far)


def encode_kernel(
    total, place, both, outer, inner, proj, extra, weight, out, none_16, none_32, wide, mid,
):
    count = both.shape[0] // 2
    bias = extra[:2, :]
    chunks = wide.shape[0]

    def keep(ref, first, value):
        for k in range(chunks):
            ref[k, pl.ds(first, value.shape[0]), :] = value[:, k * 128 : (k + 1) * 128]

    def run(ref, first, span):
        return jnp.concatenate([ref[k, pl.ds(first, span), :] for k in range(chunks)], axis=1)

    def layer(which, ref, span):
        running = jnp.zeros((span, chunks * 128), jnp.float32)
        for tap in range(3):
            rows = run(ref, count + (tap - 1) * place[5 + which], span).astype(jnp.bfloat16)
            running += jnp.dot(rows, weight[which, tap], preferred_element_type=jnp.float32)
        return run(ref, count, span) + jnp.maximum(running + bias[which : which + 1, :], 0.0)

    odd = place[0] % 2
    for side, ref, half in ((2, both, 0), (3 - 2 * odd, both, 1), (1 + 2 * odd, outer, 0),
                            (4 * odd, outer, 1), (4 - 4 * odd, inner, 0)):
        first = side * count
        if ref is not both or half:
            first = pl.multiple_of(first, count)
        keep(wide, first, ref[half * count : (half + 1) * count, :].astype(jnp.float32))
    value = layer(0, wide, 3 * count).astype(jnp.bfloat16).astype(jnp.float32)
    index = (place[0] - 1) * count + lax.broadcasted_iota(jnp.int32, value.shape, 0)
    keep(mid, 0, jnp.where((index >= 0) & (index < total), value, 0.0))
    value = layer(1, mid, count)
    parts = lax.dot_general(
        value.astype(jnp.bfloat16),
        proj[...],
        (((1,), (1,)), ((), ())),
        preferred_element_type=jnp.float32,
    )
    parts = (parts + extra[2 : 2 + count, : proj.shape[0]]).astype(jnp.bfloat16)
    parts = parts[:, : proj.shape[0] // 2]
    parts = jnp.concatenate([parts[: count // 2], parts[count // 2 :]], axis=1)
    out[...] = jnp.broadcast_to(parts[None], out.shape)
    none_16[...] = jnp.zeros(none_16.shape, none_16.dtype)
    none_32[...] = jnp.zeros(none_32.shape, none_32.dtype)


def local_columns(rows):
    lane = lax.broadcasted_iota(jnp.int32, (rows, LANES), 1)
    return jnp.where(lane < LANES - 3 * DMAX2 - 8, lane, lane - LANES)


def pair_kernel(
    total_shards, first_dil, place, parts, gain, weight, out_far,
    row_turned, distance, field_a, field_b, final, held, out, sent,
):
    shard = 2 * parts.shape[1]
    chans = gain.shape[0]
    tile_rows = out.shape[1]
    margin = 3 * DMAX2
    reach = margin // shard
    row_place, col_place = place[1], place[2]
    last_row = place[3] - 1
    row_first = row_place * tile_rows
    col_first = col_place * 128
    dils = [place[first_dil + k] for k in range(3)]

    def pieces(first, count, wrap):
        taken = []
        for k in range(count):
            step = k - count if k >= wrap else k
            both = parts[jnp.clip(first + step, 0, total_shards - 1)]
            taken += [both[:, : 2 * chans], both[:, 2 * chans :]]
        return jnp.concatenate(taken, axis=0).astype(jnp.float32)

    col_glob = col_first + local_columns(1)
    inside = (col_glob >= 0) & (col_glob < total_shards * shard)
    inside_high = jnp.where(inside[:, 128:], 1.0, 0.0)
    inside_high = jnp.broadcast_to(inside_high, (chans, 128)).astype(jnp.bfloat16)

    cols = pieces(col_first // shard, LANES // shard, LANES // shard - reach)
    col_turned = jnp.transpose(cols)[chans : 2 * chans, :]
    col_turned = jnp.where(inside, col_turned, OUTSIDE)
    span0 = tile_rows + 2 * margin
    blocks = -(-span0 // 128)
    rows = pieces(row_first // shard - reach, blocks * 128 // shard, blocks * 128)
    rows = jnp.transpose(rows)[:chans, :]
    row_glob = row_first - margin + lax.broadcasted_iota(jnp.int32, (1, blocks * 128), 1)
    rows = jnp.where((row_glob >= 0) & (row_glob < total_shards * shard), rows, OUTSIDE)
    for k in range(blocks):
        row_turned[k] = rows[:, k * 128 : (k + 1) * 128]

    row_local = lax.broadcasted_iota(jnp.int32, (span0, LANES), 0) - margin
    apart = jnp.abs(row_first + row_local - col_glob)
    distance[...] = jnp.log(1.0 + apart.astype(jnp.float32)) * 0.125
    gain_wide = jnp.broadcast_to(gain[...], (chans, LANES))
    lane16 = lax.broadcasted_iota(jnp.int16, (chans, 128), 1)

    def keep(field, d, masked):
        back = 128 - d
        at_left = lane16 < d.astype(jnp.int16)
        at_right = lane16 >= back.astype(jnp.int16)

        def store(i, low, high):
            low = low.astype(jnp.bfloat16)
            high = high.astype(jnp.bfloat16)
            if masked:
                high = high * inside_high
            field[i, chans : 2 * chans, :128] = low
            field[i, chans : 2 * chans, 128:] = high
            turned_low, turned_high = pltpu.roll(low, d, 1), pltpu.roll(high, d, 1)
            field[i, :chans, :128] = jnp.where(at_left, turned_high, turned_low)
            field[i, :chans, 128:] = jnp.where(at_left, turned_low, turned_high)
            turned_low, turned_high = pltpu.roll(low, back, 1), pltpu.roll(high, back, 1)
            field[i, 2 * chans :, :128] = jnp.where(at_right, turned_high, turned_low)
            field[i, 2 * chans :, 128:] = jnp.where(at_right, turned_low, turned_high)

        return store

    def clear(field, extra):
        @pl.when(row_place == 0)
        def _():
            @pl.loop(0, extra)
            def _(i):
                field[i] = jnp.zeros(field.shape[1:], field.dtype)

        @pl.when(row_place == last_row)
        def _():
            @pl.loop(0, extra)
            def _(i):
                field[extra + tile_rows + i] = jnp.zeros(field.shape[1:], field.dtype)

    need = dils[0] + dils[1] + dils[2]
    store_first = keep(field_a, dils[0], False)
    first_row, last_row_needed = margin - need, margin + tile_rows + need - 1

    def build(index, count):
        for k in range(count):
            i = jnp.minimum(first_row + index + k, last_row_needed)
            pick = jnp.full((chans, 128), i % 128, jnp.int32)
            row_term = jnp.take_along_axis(row_turned[i // 128], pick, axis=1)
            row_term = jnp.concatenate([row_term, row_term], axis=1)
            value = row_term + col_turned + gain_wide * distance[pl.ds(i, 1), :]
            value = jnp.maximum(value, 0.0)
            store_first(i, value[:, :128], value[:, 128:])

    @pl.loop(0, (last_row_needed - first_row + 8) // 8)
    def _(block):
        build(block * 8, 8)

    tail = jnp.ones((TAIL, WIDE * LANES), jnp.bfloat16)

    def tower(layer, source, extra, need, store, first_in_step=None):
        d = dils[layer]
        span = GROUP * d
        first = extra - need
        count = tile_rows + 2 * need
        final_layer = layer == 2
        width = 128 if final_layer else LANES
        each = WIDE * LANES // width

        def product(bases):
            taps = []
            for k in range(GROUP + 2):
                at = [base + DMAX2 + (k - 1) * d for base in bases]
                taps.append(jnp.concatenate([source[i, :, :width] for i in at], axis=1))
            stack = jnp.concatenate(taps + [tail], axis=0)
            return jnp.dot(weight[layer], stack, preferred_element_type=jnp.float32)

        def finish(bases, sums):
            for n, base in enumerate(bases):
                for k in range(GROUP):
                    at = slice(n * width, (n + 1) * width)
                    center = source[base + DMAX2 + k * d, chans : 2 * chans, :width]
                    value = sums[k * chans : (k + 1) * chans, at]
                    if final_layer:
                        value = center.astype(jnp.float32) + jnp.maximum(value, 0.0)
                        store(base + k * d, value)
                    else:
                        value = center + jnp.maximum(value.astype(jnp.bfloat16), 0)
                        store(base + k * d, value[:, :128], value[:, 128:])

        def walk(start, phase):
            bases = []
            for _ in range(each):
                bases.append(first + jnp.minimum(start, count - span) + phase)
                wrap = phase + 1 >= d
                start = jnp.where(wrap, start + span, start)
                phase = jnp.where(wrap, 0, phase + 1)
            return bases, start, phase

        def step(index, carry):
            start, phase, bases = carry
            if first_in_step is not None:
                first_in_step(index)
            sums = held
            for k in range(UNROLL):
                next_bases, start, phase = walk(start, phase)
                next_sums = product(next_bases)
                finish(bases, sums)
                bases, sums = next_bases, next_sums
            held[...] = sums
            return start, phase, bases

        zero = jnp.int32(0)
        total = (count + span - 1) // span * d
        steps = (total + UNROLL * each - 1) // (UNROLL * each)
        carry = lax.fori_loop(0, steps, step, (zero, zero, walk(zero, zero)[0]))
        finish(carry[2], held)

    def keep_last(i, low):
        final[pl.ds(pl.multiple_of(i * PITCH, 8), chans), :] = low

    def turn(chunk):
        @functools.partial(lax.fori_loop, 0, CHUNK // 16, init_val=0, unroll=True)
        def _(block, carry):
            first = pl.multiple_of(chunk * CHUNK + block * 16, 16)
            for c in range(chans):
                taken = final[pl.ds(first * PITCH + c, 16, stride=PITCH), :]
                out[c, pl.ds(first, 16), :] = taken.astype(jnp.bfloat16)
            return carry

    def send(chunk):
        rows = pl.ds(chunk * CHUNK, CHUNK)
        return pltpu.make_async_copy(out.at[:, rows, :], out_far.at[:, rows, :], sent.at[chunk])

    early = 2

    def turn_early(step):
        turn(jnp.clip(step - 2, 0, early - 1))

    tower(0, field_a, 2 * DMAX2, dils[1] + dils[2], keep(field_b, dils[1], True))
    clear(field_b, 2 * DMAX2)
    tower(1, field_b, DMAX2, dils[2], keep(field_a, dils[2], True))
    clear(field_a, DMAX2)
    tower(2, field_a, 0, 0, keep_last, turn_early)

    for k in range(tile_rows // CHUNK):
        if k >= early:
            turn(k)
        send(k).start()
    for k in range(tile_rows // CHUNK):
        send(k).wait()


def banded(map_weight, map_bias):
    layers, _, _, outs, ins = map_weight.shape
    taps = jnp.transpose(map_weight, (0, 3, 1, 2, 4)).reshape(layers, outs, 9 * ins)
    left = map_bias
    split = []
    for _ in range(3):
        split.append(lax.reduce_precision(left, 8, 7))
        left = left - split[-1]
    split = jnp.stack(split, axis=2).astype(jnp.bfloat16)
    rows = []
    for k in range(GROUP):
        before, after = k * 3 * ins, (GROUP - 1 - k) * 3 * ins
        row = jnp.pad(taps, ((0, 0), (0, 0), (before, after)))
        rows.append(jnp.concatenate([row, jnp.pad(split, ((0, 0), (0, 0), (0, TAIL - 3)))], axis=2))
    return jnp.concatenate(rows, axis=1)


def pair_call(place, gathered, dist_gain, bands, tile_rows, tile_cols):
    chans = dist_gain.shape[0]
    smem = pl.BlockSpec(memory_space=pltpu.SMEM)
    vmem = pl.BlockSpec(memory_space=pltpu.VMEM)
    span = tile_rows + 6 * DMAX2
    return pl.pallas_call(
        functools.partial(pair_kernel, gathered.shape[0], place.shape[0] - 3),
        out_shape=jax.ShapeDtypeStruct((chans, tile_rows, tile_cols), jnp.bfloat16),
        in_specs=[smem] + [vmem] * 3,
        out_specs=pl.BlockSpec(memory_space=pltpu.HBM),
        scratch_shapes=[
            pltpu.VMEM((-(-span // 128), chans, 128), jnp.float32),
            pltpu.VMEM((span, LANES), jnp.float32),
            pltpu.VMEM((span, 3 * chans, LANES), jnp.bfloat16),
            pltpu.VMEM((span - 2 * DMAX2, 3 * chans, LANES), jnp.bfloat16),
            pltpu.VMEM((tile_rows * PITCH, 128), jnp.float32),
            pltpu.VMEM((GROUP * chans, WIDE * LANES), jnp.float32),
            pltpu.VMEM((chans, tile_rows, tile_cols), jnp.bfloat16),
            pltpu.SemaphoreType.DMA((tile_rows // CHUNK,)),
        ],
        compiler_params=pltpu.CompilerParams(vmem_limit_bytes=48 * 2**20),
        cost_estimate=pl.CostEstimate(
            flops=3 * 2 * tile_rows * 9 * chans * chans * LANES,
            bytes_accessed=tile_rows * tile_cols * chans * 2,
            transcendentals=0,
        ),
        name="pair_tower",
    )(
        place, gathered, dist_gain.reshape(chans, 1), bands,
    )


def on_device(
    features,
    tower_weight,
    tower_bias,
    pair_proj,
    dist_gain,
    map_weight,
    map_bias,
    dilations,
    start_bin,
):
    row_count = lax.axis_size("rows")
    col_count = lax.axis_size("cols")
    shards = row_count * col_count
    shard, width = features.shape
    total = shard * shards
    tile_rows = total // row_count
    tile_cols = total // col_count
    chans = map_weight.shape[-1]
    row_place = lax.axis_index("rows")
    col_place = lax.axis_index("cols")
    mine = row_place * col_count + col_place
    place = jnp.stack([mine, row_place, col_place, row_count, col_count]).astype(jnp.int32)
    place = jnp.concatenate([place, dilations])

    inner = [(i, i ^ 1) for i in range(shards)]
    outer = [(i, i + 1 if i % 2 else i - 1) for i in range(1, shards - 1)]
    brought = lax.ppermute(features, AXES, inner)
    brought, start_bin = lax.optimization_barrier((brought, start_bin))
    both = jnp.concatenate([features, brought], axis=0)
    from_outer = lax.ppermute(both, AXES, outer)
    code = position_code(mine * shard + jnp.arange(shard), start_bin[0], chans)
    code = jnp.pad(code, ((0, 0), (0, width - chans)))
    extra = jnp.concatenate([tower_bias, code], axis=0)
    proj = jnp.pad(pair_proj.T, ((0, 2 * chans), (0, 0)))
    weight = fetch_call(lax.optimization_barrier((tower_weight, both))[0])
    from_outer, extra, proj, place, weight = lax.optimization_barrier(
        (from_outer, extra, proj, place, weight)
    )
    from_inner = lax.ppermute(from_outer, AXES, inner)

    smem = pl.BlockSpec(memory_space=pltpu.SMEM)
    vmem = pl.BlockSpec(memory_space=pltpu.VMEM)
    parts, none_16, none_32 = pl.pallas_call(
        functools.partial(encode_kernel, total),
        out_shape=[
            jax.ShapeDtypeStruct((shards, shard // 2, 4 * chans), jnp.bfloat16),
            jax.ShapeDtypeStruct(map_weight.shape, map_weight.dtype),
            jax.ShapeDtypeStruct((map_bias.shape[0] + 1, chans), jnp.float32),
        ],
        in_specs=[smem] + [vmem] * 6,
        out_specs=[vmem] * 3,
        scratch_shapes=[
            pltpu.VMEM((width // 128, 5 * shard, 128), jnp.float32),
            pltpu.VMEM((width // 128, 3 * shard, 128), jnp.float32),
        ],
        compiler_params=pltpu.CompilerParams(vmem_limit_bytes=16 * 2**20),
        cost_estimate=pl.CostEstimate(
            flops=2 * 4 * shard * 3 * width * width,
            bytes_accessed=6 * width * width * 2,
            transcendentals=0,
        ),
        name="encode",
    )(
        place, both, from_outer, from_inner, proj, extra, weight,
    )

    gathered = lax.all_to_all(parts, AXES, split_axis=0, concat_axis=0, tiled=True)

    bands = banded(map_weight + none_16, map_bias + none_32[:-1])
    dist_gain = dist_gain + none_32[-1]

    return pair_call(
        place, gathered, dist_gain, bands, tile_rows, tile_cols
    )


def solution(mesh):
    placed = (P(AXES, None), P(), P(), P(), P(), P(), P(), P(), P())
    return jax.shard_map(
        on_device, mesh=mesh, in_specs=placed, out_specs=P(None, "rows", "cols"), check_vma=False
    )
```

```python
import functools
import math

import jax
import jax.numpy as jnp
from jax import lax
from jax.experimental import pallas as pl
from jax.experimental.pallas import tpu as pltpu
from jax.sharding import PartitionSpec as P

DMAX1 = 16
DMAX2 = 16
GROUP = 4
WIDE = 2
UNROLL = 4
LANES = 256
PITCH = 40
FETCH_LIMIT = 50
CHUNK = 64
OUTSIDE = -1e30
AXES = ("rows", "cols")


def position_code(bin_index, start_pos, map_width):
    half_width = map_width // 2
    position = ((start_pos + bin_index) % 8192).astype(jnp.float32)
    rates = jnp.exp(-jnp.arange(half_width).astype(jnp.float32) * (math.log(1000.0) / half_width))
    phase_angle = position[:, None] * rates[None, :]
    return jnp.concatenate([jnp.cos(phase_angle), jnp.sin(phase_angle)], axis=1)


def fetch_kernel(far, near, arrived):
    copies = [
        pltpu.make_async_copy(far.at[which, tap], near.at[which, tap], arrived.at[which, tap])
        for which in range(far.shape[0])
        for tap in range(far.shape[1])
    ]
    for copy in copies:
        copy.start()
    for copy in copies:
        copy.wait()


def fetch_call(far):
    return pl.pallas_call(
        fetch_kernel,
        out_shape=jax.ShapeDtypeStruct(far.shape, far.dtype),
        in_specs=[pl.BlockSpec(memory_space=pltpu.HBM)],
        out_specs=pl.BlockSpec(memory_space=pltpu.VMEM),
        scratch_shapes=[pltpu.SemaphoreType.DMA(far.shape[:2])],
        compiler_params=pltpu.CompilerParams(vmem_limit_bytes=FETCH_LIMIT * 2**20),
        name="fetch",
    )(far)


def encode_kernel(
    total, place, both, outer, inner, proj, extra, weight, out, none_16, none_32, wide, mid,
):
    count = both.shape[0] // 2
    bias = extra[:2, :]
    chunks = wide.shape[0]

    def keep(ref, first, value):
        for k in range(chunks):
            ref[k, pl.ds(first, value.shape[0]), :] = value[:, k * 128 : (k + 1) * 128]

    def run(ref, first, span):
        return jnp.concatenate([ref[k, pl.ds(first, span), :] for k in range(chunks)], axis=1)

    def layer(which, ref, span):
        running = jnp.zeros((span, chunks * 128), jnp.float32)
        for tap in range(3):
            rows = run(ref, count + (tap - 1) * place[5 + which], span).astype(jnp.bfloat16)
            running += jnp.dot(rows, weight[which, tap], preferred_element_type=jnp.float32)
        return run(ref, count, span) + jnp.maximum(running + bias[which : which + 1, :], 0.0)

    odd = place[0] % 2
    for side, ref, half in ((2, both, 0), (3 - 2 * odd, both, 1), (1 + 2 * odd, outer, 0),
                            (4 * odd, outer, 1), (4 - 4 * odd, inner, 0)):
        first = side * count
        if ref is not both or half:
            first = pl.multiple_of(first, count)
        keep(wide, first, ref[half * count : (half + 1) * count, :].astype(jnp.float32))
    value = layer(0, wide, 3 * count).astype(jnp.bfloat16).astype(jnp.float32)
    index = (place[0] - 1) * count + lax.broadcasted_iota(jnp.int32, value.shape, 0)
    keep(mid, 0, jnp.where((index >= 0) & (index < total), value, 0.0))
    value = layer(1, mid, count)
    parts = lax.dot_general(
        value.astype(jnp.bfloat16),
        proj[...],
        (((1,), (1,)), ((), ())),
        preferred_element_type=jnp.float32,
    )
    parts = (parts + extra[2 : 2 + count, : proj.shape[0]]).astype(jnp.bfloat16)
    parts = parts[:, : proj.shape[0] // 2]
    parts = jnp.concatenate([parts[: count // 2], parts[count // 2 :]], axis=1)
    out[...] = jnp.broadcast_to(parts[None], out.shape)
    none_16[...] = jnp.zeros(none_16.shape, none_16.dtype)
    none_32[...] = jnp.zeros(none_32.shape, none_32.dtype)


def local_columns(rows):
    lane = lax.broadcasted_iota(jnp.int32, (rows, LANES), 1)
    return jnp.where(lane < LANES - 3 * DMAX2 - 8, lane, lane - LANES)


def pair_kernel(
    total_shards, first_dil, place, parts, gain, weight, bias, out_far,
    row_turned, distance, field_a, field_b, final, held, out, sent,
):
    shard = 2 * parts.shape[1]
    chans = gain.shape[0]
    tile_rows = out.shape[1]
    margin = 3 * DMAX2
    reach = margin // shard
    row_place, col_place = place[1], place[2]
    last_row = place[3] - 1
    row_first = row_place * tile_rows
    col_first = col_place * 128
    dils = [place[first_dil + k] for k in range(3)]

    def pieces(first, count, wrap):
        taken = []
        for k in range(count):
            step = k - count if k >= wrap else k
            both = parts[jnp.clip(first + step, 0, total_shards - 1)]
            taken += [both[:, : 2 * chans], both[:, 2 * chans :]]
        return jnp.concatenate(taken, axis=0).astype(jnp.float32)

    col_glob = col_first + local_columns(1)
    inside = (col_glob >= 0) & (col_glob < total_shards * shard)
    inside_high = jnp.where(inside[:, 128:], 1.0, 0.0)
    inside_high = jnp.broadcast_to(inside_high, (chans, 128)).astype(jnp.bfloat16)

    cols = pieces(col_first // shard, LANES // shard, LANES // shard - reach)
    col_turned = jnp.transpose(cols)[chans : 2 * chans, :]
    col_turned = jnp.where(inside, col_turned, OUTSIDE)
    span0 = tile_rows + 2 * margin
    count = -(-span0 // shard)
    half = shard // 2
    rows = [
        parts[jnp.clip(row_first // shard - reach + k, 0, total_shards - 1)] for k in range(count)
    ]
    rows = jnp.transpose(jnp.concatenate(rows, axis=0).astype(jnp.float32))
    spot = lax.broadcasted_iota(jnp.int32, (1, count * half), 1)
    for side in range(2):
        row_glob = row_first - margin + spot // half * shard + side * half + spot % half
        valid = (row_glob >= 0) & (row_glob < total_shards * shard)
        turned = rows[side * 2 * chans : (side * 2 + 1) * chans, :]
        turned = jnp.where(valid, turned, OUTSIDE)
        row_turned[2 * side] = turned[:, :128]
        row_turned[2 * side + 1, :, : count * half - 128] = turned[:, 128:]

    row_local = lax.broadcasted_iota(jnp.int32, (span0, LANES), 0) - margin
    apart = jnp.abs(row_first + row_local - col_glob)
    distance[...] = jnp.log(1.0 + apart.astype(jnp.float32)) * 0.125
    gain_wide = jnp.broadcast_to(gain[...], (chans, LANES))
    lane16 = lax.broadcasted_iota(jnp.int16, (chans, 128), 1)

    def keep(field, d, masked):
        back = 128 - d
        at_left = lane16 < d.astype(jnp.int16)
        at_right = lane16 >= back.astype(jnp.int16)

        def store(i, low, high):
            low = low.astype(jnp.bfloat16)
            high = high.astype(jnp.bfloat16)
            if masked:
                high = high * inside_high
            field[i, chans : 2 * chans, :128] = low
            field[i, chans : 2 * chans, 128:] = high
            turned_low, turned_high = pltpu.roll(low, d, 1), pltpu.roll(high, d, 1)
            field[i, :chans, :128] = jnp.where(at_left, turned_high, turned_low)
            field[i, :chans, 128:] = jnp.where(at_left, turned_low, turned_high)
            turned_low, turned_high = pltpu.roll(low, back, 1), pltpu.roll(high, back, 1)
            field[i, 2 * chans :, :128] = jnp.where(at_right, turned_high, turned_low)
            field[i, 2 * chans :, 128:] = jnp.where(at_right, turned_low, turned_high)

        return store

    def clear(field, extra):
        @pl.when(row_place == 0)
        def _():
            @pl.loop(0, extra)
            def _(i):
                field[i] = jnp.zeros(field.shape[1:], field.dtype)

        @pl.when(row_place == last_row)
        def _():
            @pl.loop(0, extra)
            def _(i):
                field[extra + tile_rows + i] = jnp.zeros(field.shape[1:], field.dtype)

    need = dils[0] + dils[1] + dils[2]
    store_first = keep(field_a, dils[0], False)
    first_row, last_row_needed = margin - need, margin + tile_rows + need - 1

    def build(index, count):
        for k in range(count):
            i = jnp.minimum(first_row + index + k, last_row_needed)
            spot = i // shard * half + i % half
            pick = jnp.full((chans, 128), spot % 128, jnp.int32)
            turned = row_turned[i // half % 2 * 2 + spot // 128]
            row_term = jnp.take_along_axis(turned, pick, axis=1)
            row_term = jnp.concatenate([row_term, row_term], axis=1)
            value = row_term + col_turned + gain_wide * distance[pl.ds(i, 1), :]
            value = jnp.maximum(value, 0.0)
            store_first(i, value[:, :128], value[:, 128:])

    @pl.loop(0, (last_row_needed - first_row + 8) // 8)
    def _(block):
        build(block * 8, 8)

    def tower(layer, source, extra, need, store, first_in_step=None):
        d = dils[layer]
        span = GROUP * d
        first = extra - need
        count = tile_rows + 2 * need
        final_layer = layer == 2
        width = 128 if final_layer else LANES
        each = WIDE * LANES // width

        bias_wide = jnp.broadcast_to(bias[layer], (chans, width))

        def product(bases):
            taps = []
            for k in range(GROUP + 2):
                at = [base + DMAX2 + (k - 1) * d for base in bases]
                taps.append(jnp.concatenate([source[i, :, :width] for i in at], axis=1))
            stack = jnp.concatenate(taps, axis=0)
            return jnp.dot(weight[layer], stack, preferred_element_type=jnp.float32)

        def finish(bases, sums):
            for n, base in enumerate(bases):
                for k in range(GROUP):
                    at = slice(n * width, (n + 1) * width)
                    center = source[base + DMAX2 + k * d, chans : 2 * chans, :width]
                    value = sums[k * chans : (k + 1) * chans, at] + bias_wide
                    if final_layer:
                        value = center.astype(jnp.float32) + jnp.maximum(value, 0.0)
                        store(base + k * d, value)
                    else:
                        value = center + jnp.maximum(value.astype(jnp.bfloat16), 0)
                        store(base + k * d, value[:, :128], value[:, 128:])

        def walk(start, phase):
            bases = []
            for _ in range(each):
                bases.append(first + jnp.minimum(start, count - span) + phase)
                wrap = phase + 1 >= d
                start = jnp.where(wrap, start + span, start)
                phase = jnp.where(wrap, 0, phase + 1)
            return bases, start, phase

        def step(index, carry):
            start, phase, bases = carry
            if first_in_step is not None:
                first_in_step(index)
            sums = held
            for k in range(UNROLL):
                next_bases, start, phase = walk(start, phase)
                next_sums = product(next_bases)
                finish(bases, sums)
                bases, sums = next_bases, next_sums
            held[...] = sums
            return start, phase, bases

        zero = jnp.int32(0)
        total = (count + span - 1) // span * d
        steps = (total + UNROLL * each - 1) // (UNROLL * each)
        carry = lax.fori_loop(0, steps, step, (zero, zero, walk(zero, zero)[0]))
        finish(carry[2], held)

    def keep_last(i, low):
        final[pl.ds(pl.multiple_of(i * PITCH, 8), chans), :] = low

    def turn(chunk):
        @functools.partial(lax.fori_loop, 0, CHUNK // 16, init_val=0, unroll=True)
        def _(block, carry):
            first = pl.multiple_of(chunk * CHUNK + block * 16, 16)
            for c in range(chans):
                taken = final[pl.ds(first * PITCH + c, 16, stride=PITCH), :]
                out[c, pl.ds(first, 16), :] = taken.astype(jnp.bfloat16)
            return carry

    def send(chunk):
        rows = pl.ds(chunk * CHUNK, CHUNK)
        return pltpu.make_async_copy(out.at[:, rows, :], out_far.at[:, rows, :], sent.at[chunk])

    early = 2

    def turn_early(step):
        turn(jnp.clip(step - 2, 0, early - 1))

    tower(0, field_a, 2 * DMAX2, dils[1] + dils[2], keep(field_b, dils[1], True))
    clear(field_b, 2 * DMAX2)
    tower(1, field_b, DMAX2, dils[2], keep(field_a, dils[2], True))
    clear(field_a, DMAX2)
    tower(2, field_a, 0, 0, keep_last, turn_early)

    for k in range(tile_rows // CHUNK):
        if k >= early:
            turn(k)
        send(k).start()
    for k in range(tile_rows // CHUNK):
        send(k).wait()


def banded(map_weight):
    layers, _, _, outs, ins = map_weight.shape
    taps = jnp.transpose(map_weight, (0, 3, 1, 2, 4)).reshape(layers, outs, 9 * ins)
    rows = [
        jnp.pad(taps, ((0, 0), (0, 0), (k * 3 * ins, (GROUP - 1 - k) * 3 * ins)))
        for k in range(GROUP)
    ]
    return jnp.concatenate(rows, axis=1)


def pair_call(place, gathered, dist_gain, bands, map_bias, tile_rows, tile_cols):
    chans = dist_gain.shape[0]
    smem = pl.BlockSpec(memory_space=pltpu.SMEM)
    vmem = pl.BlockSpec(memory_space=pltpu.VMEM)
    span = tile_rows + 6 * DMAX2
    return pl.pallas_call(
        functools.partial(pair_kernel, gathered.shape[0], place.shape[0] - 3),
        out_shape=jax.ShapeDtypeStruct((chans, tile_rows, tile_cols), jnp.bfloat16),
        in_specs=[smem] + [vmem] * 4,
        out_specs=pl.BlockSpec(memory_space=pltpu.HBM),
        scratch_shapes=[
            pltpu.VMEM((4, chans, 128), jnp.float32),
            pltpu.VMEM((span, LANES), jnp.float32),
            pltpu.VMEM((span, 3 * chans, LANES), jnp.bfloat16),
            pltpu.VMEM((span - 2 * DMAX2, 3 * chans, LANES), jnp.bfloat16),
            pltpu.VMEM((tile_rows * PITCH, 128), jnp.float32),
            pltpu.VMEM((GROUP * chans, WIDE * LANES), jnp.float32),
            pltpu.VMEM((chans, tile_rows, tile_cols), jnp.bfloat16),
            pltpu.SemaphoreType.DMA((tile_rows // CHUNK,)),
        ],
        compiler_params=pltpu.CompilerParams(vmem_limit_bytes=48 * 2**20),
        cost_estimate=pl.CostEstimate(
            flops=3 * 2 * tile_rows * 9 * chans * chans * LANES,
            bytes_accessed=tile_rows * tile_cols * chans * 2,
            transcendentals=0,
        ),
        name="pair_tower",
    )(
        place, gathered, dist_gain.reshape(chans, 1), bands, map_bias.reshape(-1, chans, 1),
    )


def on_device(
    features,
    tower_weight,
    tower_bias,
    pair_proj,
    dist_gain,
    map_weight,
    map_bias,
    dilations,
    start_bin,
):
    row_count = lax.axis_size("rows")
    col_count = lax.axis_size("cols")
    shards = row_count * col_count
    shard, width = features.shape
    total = shard * shards
    tile_rows = total // row_count
    tile_cols = total // col_count
    chans = map_weight.shape[-1]
    row_place = lax.axis_index("rows")
    col_place = lax.axis_index("cols")
    mine = row_place * col_count + col_place
    place = jnp.stack([mine, row_place, col_place, row_count, col_count]).astype(jnp.int32)
    place = jnp.concatenate([place, dilations])

    inner = [(i, i ^ 1) for i in range(shards)]
    outer = [(i, i + 1 if i % 2 else i - 1) for i in range(1, shards - 1)]
    brought = lax.ppermute(features, AXES, inner)
    brought, start_bin = lax.optimization_barrier((brought, start_bin))
    both = jnp.concatenate([features, brought], axis=0)
    from_outer = lax.ppermute(both, AXES, outer)
    code = position_code(mine * shard + jnp.arange(shard), start_bin[0], chans)
    code = jnp.pad(code, ((0, 0), (0, width - chans)))
    extra = jnp.concatenate([tower_bias, code], axis=0)
    proj = jnp.pad(pair_proj.T, ((0, 2 * chans), (0, 0)))
    weight = fetch_call(lax.optimization_barrier((tower_weight, both))[0])
    from_outer, extra, proj, place, weight = lax.optimization_barrier(
        (from_outer, extra, proj, place, weight)
    )
    from_inner = lax.ppermute(from_outer, AXES, inner)

    smem = pl.BlockSpec(memory_space=pltpu.SMEM)
    vmem = pl.BlockSpec(memory_space=pltpu.VMEM)
    parts, none_16, none_32 = pl.pallas_call(
        functools.partial(encode_kernel, total),
        out_shape=[
            jax.ShapeDtypeStruct((shards, shard // 2, 4 * chans), jnp.bfloat16),
            jax.ShapeDtypeStruct(map_weight.shape, map_weight.dtype),
            jax.ShapeDtypeStruct((map_bias.shape[0] + 1, chans), jnp.float32),
        ],
        in_specs=[smem] + [vmem] * 6,
        out_specs=[vmem] * 3,
        scratch_shapes=[
            pltpu.VMEM((width // 128, 5 * shard, 128), jnp.float32),
            pltpu.VMEM((width // 128, 3 * shard, 128), jnp.float32),
        ],
        compiler_params=pltpu.CompilerParams(vmem_limit_bytes=16 * 2**20),
        cost_estimate=pl.CostEstimate(
            flops=2 * 4 * shard * 3 * width * width,
            bytes_accessed=6 * width * width * 2,
            transcendentals=0,
        ),
        name="encode",
    )(
        place, both, from_outer, from_inner, proj, extra, weight,
    )

    gathered = lax.all_to_all(parts, AXES, split_axis=0, concat_axis=0, tiled=True)

    bands = banded(map_weight + none_16)
    map_bias = map_bias + none_32[:-1]
    dist_gain = dist_gain + none_32[-1]

    return pair_call(
        place, gathered, dist_gain, bands, map_bias, tile_rows, tile_cols
    )


def solution(mesh):
    placed = (P(AXES, None), P(), P(), P(), P(), P(), P(), P(), P())
    return jax.shard_map(
        on_device, mesh=mesh, in_specs=placed, out_specs=P(None, "rows", "cols"), check_vma=False
    )
```

```python
import functools
import math

import jax
import jax.numpy as jnp
from jax import lax
from jax.experimental import pallas as pl
from jax.experimental.pallas import tpu as pltpu
from jax.sharding import PartitionSpec as P

DMAX1 = 16
DMAX2 = 16
GROUP = 4
TAIL = 32
WIDE = 2
UNROLL = 4
LANES = 256
PITCH = 40
FETCH_LIMIT = 50
CHUNK = 64
OUTSIDE = -1e30
AXES = ("rows", "cols")


def position_code(bin_index, start_pos, map_width):
    half_width = map_width // 2
    position = ((start_pos + bin_index) % 8192).astype(jnp.float32)
    rates = jnp.exp(-jnp.arange(half_width).astype(jnp.float32) * (math.log(1000.0) / half_width))
    phase_angle = position[:, None] * rates[None, :]
    return jnp.concatenate([jnp.cos(phase_angle), jnp.sin(phase_angle)], axis=1)


def fetch_kernel(far, near, arrived):
    copies = [
        pltpu.make_async_copy(far.at[which, tap], near.at[which, tap], arrived.at[which, tap])
        for which in range(far.shape[0])
        for tap in range(far.shape[1])
    ]
    for copy in copies:
        copy.start()
    for copy in copies:
        copy.wait()


def fetch_call(far):
    return pl.pallas_call(
        fetch_kernel,
        out_shape=jax.ShapeDtypeStruct(far.shape, far.dtype),
        in_specs=[pl.BlockSpec(memory_space=pltpu.HBM)],
        out_specs=pl.BlockSpec(memory_space=pltpu.VMEM),
        scratch_shapes=[pltpu.SemaphoreType.DMA(far.shape[:2])],
        compiler_params=pltpu.CompilerParams(vmem_limit_bytes=FETCH_LIMIT * 2**20),
        name="fetch",
    )(far)


def encode_kernel(
    total, place, both, outer, inner, proj, extra, weight, out, none_16, none_32, wide, mid,
):
    count = both.shape[0] // 2
    bias = extra[:2, :]
    chunks = wide.shape[0]

    def keep(ref, first, value):
        for k in range(chunks):
            ref[k, pl.ds(first, value.shape[0]), :] = value[:, k * 128 : (k + 1) * 128]

    def run(ref, first, span):
        return jnp.concatenate([ref[k, pl.ds(first, span), :] for k in range(chunks)], axis=1)

    def layer(which, ref, span):
        running = jnp.zeros((span, chunks * 128), jnp.float32)
        for tap in range(3):
            rows = run(ref, count + (tap - 1) * place[5 + which], span).astype(jnp.bfloat16)
            running += jnp.dot(rows, weight[which, tap], preferred_element_type=jnp.float32)
        return run(ref, count, span) + jnp.maximum(running + bias[which : which + 1, :], 0.0)

    odd = place[0] % 2
    for side, ref, half in ((2, both, 0), (3 - 2 * odd, both, 1), (1 + 2 * odd, outer, 0),
                            (4 * odd, outer, 1), (4 - 4 * odd, inner, 0)):
        first = side * count
        if ref is not both or half:
            first = pl.multiple_of(first, count)
        keep(wide, first, ref[half * count : (half + 1) * count, :].astype(jnp.float32))
    value = layer(0, wide, 3 * count).astype(jnp.bfloat16).astype(jnp.float32)
    index = (place[0] - 1) * count + lax.broadcasted_iota(jnp.int32, value.shape, 0)
    keep(mid, 0, jnp.where((index >= 0) & (index < total), value, 0.0))
    value = layer(1, mid, count)
    parts = lax.dot_general(
        value.astype(jnp.bfloat16),
        proj[...],
        (((1,), (1,)), ((), ())),
        preferred_element_type=jnp.float32,
    )
    parts = (parts + extra[2 : 2 + count, : proj.shape[0]]).astype(jnp.bfloat16)
    parts = parts[:, : proj.shape[0] // 2]
    parts = jnp.concatenate([parts[: count // 2], parts[count // 2 :]], axis=1)
    out[...] = jnp.broadcast_to(parts[None], out.shape)
    none_16[...] = jnp.zeros(none_16.shape, none_16.dtype)
    none_32[...] = jnp.zeros(none_32.shape, none_32.dtype)


def local_columns(rows):
    lane = lax.broadcasted_iota(jnp.int32, (rows, LANES), 1)
    return jnp.where(lane < LANES - 3 * DMAX2 - 8, lane, lane - LANES)


def pair_kernel(
    total_shards, first_dil, place, parts, gain, weight, out_far,
    row_turned, distance, field_a, field_b, final, held, out, sent,
):
    shard = 2 * parts.shape[1]
    chans = gain.shape[0]
    tile_rows = out.shape[1]
    margin = 3 * DMAX2
    reach = margin // shard
    row_place, col_place = place[1], place[2]
    last_row = place[3] - 1
    row_first = row_place * tile_rows
    col_first = col_place * 128
    dils = [place[first_dil + k] for k in range(3)]

    def pieces(first, count, wrap):
        taken = []
        for k in range(count):
            step = k - count if k >= wrap else k
            both = parts[jnp.clip(first + step, 0, total_shards - 1)]
            taken += [both[:, : 2 * chans], both[:, 2 * chans :]]
        return jnp.concatenate(taken, axis=0).astype(jnp.float32)

    col_glob = col_first + local_columns(1)
    inside = (col_glob >= 0) & (col_glob < total_shards * shard)
    inside_high = jnp.where(inside[:, 128:], 1.0, 0.0)
    inside_high = jnp.broadcast_to(inside_high, (chans, 128)).astype(jnp.bfloat16)

    cols = pieces(col_first // shard, LANES // shard, LANES // shard - reach)
    col_turned = jnp.transpose(cols)[chans : 2 * chans, :]
    col_turned = jnp.where(inside, col_turned, OUTSIDE)
    span0 = tile_rows + 2 * margin
    blocks = -(-span0 // 128)
    rows = pieces(row_first // shard - reach, blocks * 128 // shard, blocks * 128)
    rows = jnp.transpose(rows)[:chans, :]
    row_glob = row_first - margin + lax.broadcasted_iota(jnp.int32, (1, blocks * 128), 1)
    rows = jnp.where((row_glob >= 0) & (row_glob < total_shards * shard), rows, OUTSIDE)
    for k in range(blocks):
        row_turned[k] = rows[:, k * 128 : (k + 1) * 128]

    row_local = lax.broadcasted_iota(jnp.int32, (span0, LANES), 0) - margin
    apart = jnp.abs(row_first + row_local - col_glob)
    distance[...] = jnp.log(1.0 + apart.astype(jnp.float32)) * 0.125
    gain_wide = jnp.broadcast_to(gain[...], (chans, LANES))
    lane16 = lax.broadcasted_iota(jnp.int16, (chans, 128), 1)

    def keep(field, d, masked):
        back = 128 - d
        at_left = lane16 < d.astype(jnp.int16)
        at_right = lane16 >= back.astype(jnp.int16)

        def store(i, low, high):
            low = low.astype(jnp.bfloat16)
            high = high.astype(jnp.bfloat16)
            if masked:
                high = high * inside_high
            field[i, chans : 2 * chans, :128] = low
            field[i, chans : 2 * chans, 128:] = high
            turned_low, turned_high = pltpu.roll(low, d, 1), pltpu.roll(high, d, 1)
            field[i, :chans, :128] = jnp.where(at_left, turned_high, turned_low)
            field[i, :chans, 128:] = jnp.where(at_left, turned_low, turned_high)
            turned_low, turned_high = pltpu.roll(low, back, 1), pltpu.roll(high, back, 1)
            field[i, 2 * chans :, :128] = jnp.where(at_right, turned_high, turned_low)
            field[i, 2 * chans :, 128:] = jnp.where(at_right, turned_low, turned_high)

        return store

    def clear(field, extra):
        @pl.when(row_place == 0)
        def _():
            @pl.loop(0, extra)
            def _(i):
                field[i] = jnp.zeros(field.shape[1:], field.dtype)

        @pl.when(row_place == last_row)
        def _():
            @pl.loop(0, extra)
            def _(i):
                field[extra + tile_rows + i] = jnp.zeros(field.shape[1:], field.dtype)

    need = dils[0] + dils[1] + dils[2]
    store_first = keep(field_a, dils[0], False)
    first_row, last_row_needed = margin - need, margin + tile_rows + need - 1

    def build(index, count):
        for k in range(count):
            i = jnp.minimum(first_row + index + k, last_row_needed)
            pick = jnp.full((chans, 128), i % 128, jnp.int32)
            row_term = jnp.take_along_axis(row_turned[i // 128], pick, axis=1)
            row_term = jnp.concatenate([row_term, row_term], axis=1)
            value = row_term + col_turned + gain_wide * distance[pl.ds(i, 1), :]
            value = jnp.maximum(value, 0.0)
            store_first(i, value[:, :128], value[:, 128:])

    @pl.loop(0, (last_row_needed - first_row + 8) // 8)
    def _(block):
        build(block * 8, 8)

    tail = jnp.ones((TAIL, WIDE * LANES), jnp.bfloat16)

    def tower(layer, source, extra, need, store, first_in_step=None):
        d = dils[layer]
        span = GROUP * d
        first = extra - need
        count = tile_rows + 2 * need
        final_layer = layer == 2
        width = 128 if final_layer else LANES
        each = WIDE * LANES // width

        def product(bases):
            taps = []
            for k in range(GROUP + 2):
                at = [base + DMAX2 + (k - 1) * d for base in bases]
                taps.append(jnp.concatenate([source[i, :, :width] for i in at], axis=1))
            stack = jnp.concatenate(taps + [tail], axis=0)
            sums = jnp.dot(weight[layer], stack, preferred_element_type=jnp.float32)
            return sums.astype(jnp.bfloat16)

        def finish(bases, sums):
            for n, base in enumerate(bases):
                for k in range(GROUP):
                    at = slice(n * width, (n + 1) * width)
                    center = source[base + DMAX2 + k * d, chans : 2 * chans, :width]
                    value = sums[k * chans : (k + 1) * chans, at]
                    value = center + jnp.maximum(value, 0)
                    if final_layer:
                        store(base + k * d, value.astype(jnp.float32))
                    else:
                        store(base + k * d, value[:, :128], value[:, 128:])

        def walk(start, phase):
            bases = []
            for _ in range(each):
                bases.append(first + jnp.minimum(start, count - span) + phase)
                wrap = phase + 1 >= d
                start = jnp.where(wrap, start + span, start)
                phase = jnp.where(wrap, 0, phase + 1)
            return bases, start, phase

        def step(index, carry):
            start, phase, bases = carry
            if first_in_step is not None:
                first_in_step(index)
            sums = held
            for k in range(UNROLL):
                next_bases, start, phase = walk(start, phase)
                next_sums = product(next_bases)
                finish(bases, sums)
                bases, sums = next_bases, next_sums
            held[...] = sums
            return start, phase, bases

        zero = jnp.int32(0)
        total = (count + span - 1) // span * d
        steps = (total + UNROLL * each - 1) // (UNROLL * each)
        carry = lax.fori_loop(0, steps, step, (zero, zero, walk(zero, zero)[0]))
        finish(carry[2], held)

    def keep_last(i, low):
        final[pl.ds(pl.multiple_of(i * PITCH, 8), chans), :] = low

    def turn(chunk):
        @functools.partial(lax.fori_loop, 0, CHUNK // 16, init_val=0, unroll=True)
        def _(block, carry):
            first = pl.multiple_of(chunk * CHUNK + block * 16, 16)
            for c in range(chans):
                taken = final[pl.ds(first * PITCH + c, 16, stride=PITCH), :]
                out[c, pl.ds(first, 16), :] = taken.astype(jnp.bfloat16)
            return carry

    def send(chunk):
        rows = pl.ds(chunk * CHUNK, CHUNK)
        return pltpu.make_async_copy(out.at[:, rows, :], out_far.at[:, rows, :], sent.at[chunk])

    early = 2

    def turn_early(step):
        turn(jnp.clip(step - 2, 0, early - 1))

    tower(0, field_a, 2 * DMAX2, dils[1] + dils[2], keep(field_b, dils[1], True))
    clear(field_b, 2 * DMAX2)
    tower(1, field_b, DMAX2, dils[2], keep(field_a, dils[2], True))
    clear(field_a, DMAX2)
    tower(2, field_a, 0, 0, keep_last, turn_early)

    for k in range(tile_rows // CHUNK):
        if k >= early:
            turn(k)
        send(k).start()
    for k in range(tile_rows // CHUNK):
        send(k).wait()


def banded(map_weight, map_bias):
    layers, _, _, outs, ins = map_weight.shape
    taps = jnp.transpose(map_weight, (0, 3, 1, 2, 4)).reshape(layers, outs, 9 * ins)
    left = map_bias
    split = []
    for _ in range(3):
        split.append(lax.reduce_precision(left, 8, 7))
        left = left - split[-1]
    split = jnp.stack(split, axis=2).astype(jnp.bfloat16)
    rows = []
    for k in range(GROUP):
        before, after = k * 3 * ins, (GROUP - 1 - k) * 3 * ins
        row = jnp.pad(taps, ((0, 0), (0, 0), (before, after)))
        rows.append(jnp.concatenate([row, jnp.pad(split, ((0, 0), (0, 0), (0, TAIL - 3)))], axis=2))
    return jnp.concatenate(rows, axis=1)


def pair_call(place, gathered, dist_gain, bands, tile_rows, tile_cols):
    chans = dist_gain.shape[0]
    smem = pl.BlockSpec(memory_space=pltpu.SMEM)
    vmem = pl.BlockSpec(memory_space=pltpu.VMEM)
    span = tile_rows + 6 * DMAX2
    return pl.pallas_call(
        functools.partial(pair_kernel, gathered.shape[0], place.shape[0] - 3),
        out_shape=jax.ShapeDtypeStruct((chans, tile_rows, tile_cols), jnp.bfloat16),
        in_specs=[smem] + [vmem] * 3,
        out_specs=pl.BlockSpec(memory_space=pltpu.HBM),
        scratch_shapes=[
            pltpu.VMEM((-(-span // 128), chans, 128), jnp.float32),
            pltpu.VMEM((span, LANES), jnp.float32),
            pltpu.VMEM((span, 3 * chans, LANES), jnp.bfloat16),
            pltpu.VMEM((span - 2 * DMAX2, 3 * chans, LANES), jnp.bfloat16),
            pltpu.VMEM((tile_rows * PITCH, 128), jnp.float32),
            pltpu.VMEM((GROUP * chans, WIDE * LANES), jnp.bfloat16),
            pltpu.VMEM((chans, tile_rows, tile_cols), jnp.bfloat16),
            pltpu.SemaphoreType.DMA((tile_rows // CHUNK,)),
        ],
        compiler_params=pltpu.CompilerParams(vmem_limit_bytes=48 * 2**20),
        cost_estimate=pl.CostEstimate(
            flops=3 * 2 * tile_rows * 9 * chans * chans * LANES,
            bytes_accessed=tile_rows * tile_cols * chans * 2,
            transcendentals=0,
        ),
        name="pair_tower",
    )(
        place, gathered, dist_gain.reshape(chans, 1), bands,
    )


def on_device(
    features,
    tower_weight,
    tower_bias,
    pair_proj,
    dist_gain,
    map_weight,
    map_bias,
    dilations,
    start_bin,
):
    row_count = lax.axis_size("rows")
    col_count = lax.axis_size("cols")
    shards = row_count * col_count
    shard, width = features.shape
    total = shard * shards
    tile_rows = total // row_count
    tile_cols = total // col_count
    chans = map_weight.shape[-1]
    row_place = lax.axis_index("rows")
    col_place = lax.axis_index("cols")
    mine = row_place * col_count + col_place
    place = jnp.stack([mine, row_place, col_place, row_count, col_count]).astype(jnp.int32)
    place = jnp.concatenate([place, dilations])

    inner = [(i, i ^ 1) for i in range(shards)]
    outer = [(i, i + 1 if i % 2 else i - 1) for i in range(1, shards - 1)]
    brought = lax.ppermute(features, AXES, inner)
    brought, start_bin = lax.optimization_barrier((brought, start_bin))
    both = jnp.concatenate([features, brought], axis=0)
    from_outer = lax.ppermute(both, AXES, outer)
    code = position_code(mine * shard + jnp.arange(shard), start_bin[0], chans)
    code = jnp.pad(code, ((0, 0), (0, width - chans)))
    extra = jnp.concatenate([tower_bias, code], axis=0)
    proj = jnp.pad(pair_proj.T, ((0, 2 * chans), (0, 0)))
    weight = fetch_call(lax.optimization_barrier((tower_weight, both))[0])
    from_outer, extra, proj, place, weight = lax.optimization_barrier(
        (from_outer, extra, proj, place, weight)
    )
    from_inner = lax.ppermute(from_outer, AXES, inner)

    smem = pl.BlockSpec(memory_space=pltpu.SMEM)
    vmem = pl.BlockSpec(memory_space=pltpu.VMEM)
    parts, none_16, none_32 = pl.pallas_call(
        functools.partial(encode_kernel, total),
        out_shape=[
            jax.ShapeDtypeStruct((shards, shard // 2, 4 * chans), jnp.bfloat16),
            jax.ShapeDtypeStruct(map_weight.shape, map_weight.dtype),
            jax.ShapeDtypeStruct((map_bias.shape[0] + 1, chans), jnp.float32),
        ],
        in_specs=[smem] + [vmem] * 6,
        out_specs=[vmem] * 3,
        scratch_shapes=[
            pltpu.VMEM((width // 128, 5 * shard, 128), jnp.float32),
            pltpu.VMEM((width // 128, 3 * shard, 128), jnp.float32),
        ],
        compiler_params=pltpu.CompilerParams(vmem_limit_bytes=16 * 2**20),
        cost_estimate=pl.CostEstimate(
            flops=2 * 4 * shard * 3 * width * width,
            bytes_accessed=6 * width * width * 2,
            transcendentals=0,
        ),
        name="encode",
    )(
        place, both, from_outer, from_inner, proj, extra, weight,
    )

    gathered = lax.all_to_all(parts, AXES, split_axis=0, concat_axis=0, tiled=True)

    bands = banded(map_weight + none_16, map_bias + none_32[:-1])
    dist_gain = dist_gain + none_32[-1]

    return pair_call(
        place, gathered, dist_gain, bands, tile_rows, tile_cols
    )


def solution(mesh):
    placed = (P(AXES, None), P(), P(), P(), P(), P(), P(), P(), P())
    return jax.shard_map(
        on_device, mesh=mesh, in_specs=placed, out_specs=P(None, "rows", "cols"), check_vma=False
    )
```

```python
import functools
import math

import jax
import jax.numpy as jnp
from jax import lax
from jax.experimental import pallas as pl
from jax.experimental.pallas import tpu as pltpu
from jax.sharding import PartitionSpec as P

DMAX1 = 16
DMAX2 = 16
GROUP = 4
TAIL = 32
WIDE = 2
UNROLL = 4
LANES = 256
PITCH = 40
FETCH_LIMIT = 50
CHUNK = 64
OUTSIDE = -1e30
AXES = ("rows", "cols")


def position_code(bin_index, start_pos, map_width):
    half_width = map_width // 2
    position = ((start_pos + bin_index) % 8192).astype(jnp.float32)
    rates = jnp.exp(-jnp.arange(half_width).astype(jnp.float32) * (math.log(1000.0) / half_width))
    phase_angle = position[:, None] * rates[None, :]
    return jnp.concatenate([jnp.cos(phase_angle), jnp.sin(phase_angle)], axis=1)


def fetch_kernel(far, near, arrived):
    copies = [
        pltpu.make_async_copy(far.at[which, tap], near.at[which, tap], arrived.at[which, tap])
        for which in range(far.shape[0])
        for tap in range(far.shape[1])
    ]
    for copy in copies:
        copy.start()
    for copy in copies:
        copy.wait()


def fetch_call(far):
    return pl.pallas_call(
        fetch_kernel,
        out_shape=jax.ShapeDtypeStruct(far.shape, far.dtype),
        in_specs=[pl.BlockSpec(memory_space=pltpu.HBM)],
        out_specs=pl.BlockSpec(memory_space=pltpu.VMEM),
        scratch_shapes=[pltpu.SemaphoreType.DMA(far.shape[:2])],
        compiler_params=pltpu.CompilerParams(vmem_limit_bytes=FETCH_LIMIT * 2**20),
        name="fetch",
    )(far)


def encode_kernel(
    total, place, both, outer, inner, proj, extra, weight, out, none_16, none_32, wide, mid,
):
    count = both.shape[0] // 2
    bias = extra[:2, :]
    chunks = wide.shape[0]

    def keep(ref, first, value):
        for k in range(chunks):
            ref[k, pl.ds(first, value.shape[0]), :] = value[:, k * 128 : (k + 1) * 128]

    def run(ref, first, span):
        return jnp.concatenate([ref[k, pl.ds(first, span), :] for k in range(chunks)], axis=1)

    def layer(which, ref, span):
        running = jnp.zeros((span, chunks * 128), jnp.float32)
        for tap in range(3):
            rows = run(ref, count + (tap - 1) * place[5 + which], span).astype(jnp.bfloat16)
            running += jnp.dot(rows, weight[which, tap], preferred_element_type=jnp.float32)
        return run(ref, count, span) + jnp.maximum(running + bias[which : which + 1, :], 0.0)

    odd = place[0] % 2
    for side, ref, half in ((2, both, 0), (3 - 2 * odd, both, 1), (1 + 2 * odd, outer, 0),
                            (4 * odd, outer, 1), (4 - 4 * odd, inner, 0)):
        first = side * count
        if ref is not both or half:
            first = pl.multiple_of(first, count)
        keep(wide, first, ref[half * count : (half + 1) * count, :].astype(jnp.float32))
    value = layer(0, wide, 3 * count).astype(jnp.bfloat16).astype(jnp.float32)
    index = (place[0] - 1) * count + lax.broadcasted_iota(jnp.int32, value.shape, 0)
    keep(mid, 0, jnp.where((index >= 0) & (index < total), value, 0.0))
    value = layer(1, mid, count)
    parts = lax.dot_general(
        value.astype(jnp.bfloat16),
        proj[...],
        (((1,), (1,)), ((), ())),
        preferred_element_type=jnp.float32,
    )
    parts = (parts + extra[2 : 2 + count, : proj.shape[0]]).astype(jnp.bfloat16)
    parts = parts[:, : proj.shape[0] // 2]
    parts = jnp.concatenate([parts[: count // 2], parts[count // 2 :]], axis=1)
    out[...] = jnp.broadcast_to(parts[None], out.shape)
    none_16[...] = jnp.zeros(none_16.shape, none_16.dtype)
    none_32[...] = jnp.zeros(none_32.shape, none_32.dtype)


def local_columns(rows):
    lane = lax.broadcasted_iota(jnp.int32, (rows, LANES), 1)
    return jnp.where(lane < LANES - 3 * DMAX2 - 8, lane, lane - LANES)


def pair_kernel(
    total_shards, first_dil, place, parts, gain, weight, out_far,
    row_turned, distance, field_a, field_b, final, held, out, sent,
):
    shard = 2 * parts.shape[1]
    chans = gain.shape[0]
    tile_rows = out.shape[1]
    margin = 3 * DMAX2
    reach = margin // shard
    row_place, col_place = place[1], place[2]
    last_row = place[3] - 1
    row_first = row_place * tile_rows
    col_first = col_place * 128
    dils = [place[first_dil + k] for k in range(3)]

    def pieces(first, count, wrap):
        taken = []
        for k in range(count):
            step = k - count if k >= wrap else k
            both = parts[jnp.clip(first + step, 0, total_shards - 1)]
            taken += [both[:, : 2 * chans], both[:, 2 * chans :]]
        return jnp.concatenate(taken, axis=0).astype(jnp.float32)

    col_glob = col_first + local_columns(1)
    inside = (col_glob >= 0) & (col_glob < total_shards * shard)
    inside_high = jnp.where(inside[:, 128:], 1.0, 0.0)
    inside_high = jnp.broadcast_to(inside_high, (chans, 128)).astype(jnp.bfloat16)

    cols = pieces(col_first // shard, LANES // shard, LANES // shard - reach)
    col_turned = jnp.transpose(cols)[chans : 2 * chans, :]
    col_turned = jnp.where(inside, col_turned, OUTSIDE)
    span0 = tile_rows + 2 * margin
    count = -(-span0 // shard)
    half = shard // 2
    rows = [
        parts[jnp.clip(row_first // shard - reach + k, 0, total_shards - 1)] for k in range(count)
    ]
    rows = jnp.transpose(jnp.concatenate(rows, axis=0).astype(jnp.float32))
    spot = lax.broadcasted_iota(jnp.int32, (1, count * half), 1)
    for side in range(2):
        row_glob = row_first - margin + spot // half * shard + side * half + spot % half
        valid = (row_glob >= 0) & (row_glob < total_shards * shard)
        turned = rows[side * 2 * chans : (side * 2 + 1) * chans, :]
        turned = jnp.where(valid, turned, OUTSIDE)
        row_turned[2 * side] = turned[:, :128]
        row_turned[2 * side + 1, :, : count * half - 128] = turned[:, 128:]

    row_local = lax.broadcasted_iota(jnp.int32, (span0, LANES), 0) - margin
    apart = jnp.abs(row_first + row_local - col_glob)
    distance[...] = jnp.log(1.0 + apart.astype(jnp.float32)) * 0.125
    gain_wide = jnp.broadcast_to(gain[...], (chans, LANES))
    lane16 = lax.broadcasted_iota(jnp.int16, (chans, 128), 1)

    def keep(field, d, masked):
        back = 128 - d
        at_left = lane16 < d.astype(jnp.int16)
        at_right = lane16 >= back.astype(jnp.int16)

        def store(i, low, high):
            low = low.astype(jnp.bfloat16)
            high = high.astype(jnp.bfloat16)
            if masked:
                high = high * inside_high
            field[i, chans : 2 * chans, :128] = low
            field[i, chans : 2 * chans, 128:] = high
            turned_low, turned_high = pltpu.roll(low, d, 1), pltpu.roll(high, d, 1)
            field[i, :chans, :128] = jnp.where(at_left, turned_high, turned_low)
            field[i, :chans, 128:] = jnp.where(at_left, turned_low, turned_high)
            turned_low, turned_high = pltpu.roll(low, back, 1), pltpu.roll(high, back, 1)
            field[i, 2 * chans :, :128] = jnp.where(at_right, turned_high, turned_low)
            field[i, 2 * chans :, 128:] = jnp.where(at_right, turned_low, turned_high)

        return store

    def clear(field, extra):
        @pl.when(row_place == 0)
        def _():
            @pl.loop(0, extra)
            def _(i):
                field[i] = jnp.zeros(field.shape[1:], field.dtype)

        @pl.when(row_place == last_row)
        def _():
            @pl.loop(0, extra)
            def _(i):
                field[extra + tile_rows + i] = jnp.zeros(field.shape[1:], field.dtype)

    need = dils[0] + dils[1] + dils[2]
    store_first = keep(field_a, dils[0], False)
    first_row, last_row_needed = margin - need, margin + tile_rows + need - 1

    @pl.loop(first_row // half, last_row_needed // half + 1)
    def _(block):
        first = pl.multiple_of(block * half, half)
        spot = block // 2 * half
        turned = row_turned[block % 2 * 2 + spot // 128]
        apart = distance[pl.ds(first, half), :]
        for k in range(half):
            pick = jnp.full((chans, 128), spot % 128 + k, jnp.int32)
            row_term = jnp.take_along_axis(turned, pick, axis=1)
            row_term = jnp.concatenate([row_term, row_term], axis=1)
            value = row_term + col_turned + gain_wide * apart[k : k + 1, :]
            value = jnp.maximum(value, 0.0)
            store_first(first + k, value[:, :128], value[:, 128:])

    tail = jnp.ones((TAIL, WIDE * LANES), jnp.bfloat16)

    def tower(layer, source, extra, need, store, first_in_step=None):
        d = dils[layer]
        span = GROUP * d
        first = extra - need
        count = tile_rows + 2 * need
        final_layer = layer == 2
        width = 128 if final_layer else LANES
        each = WIDE * LANES // width

        def product(bases):
            taps = []
            for k in range(GROUP + 2):
                at = [base + DMAX2 + (k - 1) * d for base in bases]
                taps.append(jnp.concatenate([source[i, :, :width] for i in at], axis=1))
            stack = jnp.concatenate(taps + [tail], axis=0)
            return jnp.dot(weight[layer], stack, preferred_element_type=jnp.float32)

        def finish(bases, sums):
            for n, base in enumerate(bases):
                for k in range(GROUP):
                    at = slice(n * width, (n + 1) * width)
                    center = source[base + DMAX2 + k * d, chans : 2 * chans, :width]
                    value = sums[k * chans : (k + 1) * chans, at]
                    if final_layer:
                        value = center.astype(jnp.float32) + jnp.maximum(value, 0.0)
                        store(base + k * d, value)
                    else:
                        value = center + jnp.maximum(value.astype(jnp.bfloat16), 0)
                        store(base + k * d, value[:, :128], value[:, 128:])

        def walk(start, phase):
            bases = []
            for _ in range(each):
                bases.append(first + jnp.minimum(start, count - span) + phase)
                wrap = phase + 1 >= d
                start = jnp.where(wrap, start + span, start)
                phase = jnp.where(wrap, 0, phase + 1)
            return bases, start, phase

        def step(index, carry):
            start, phase, bases = carry
            if first_in_step is not None:
                first_in_step(index)
            sums = held
            for k in range(UNROLL):
                next_bases, start, phase = walk(start, phase)
                next_sums = product(next_bases)
                finish(bases, sums)
                bases, sums = next_bases, next_sums
            held[...] = sums
            return start, phase, bases

        zero = jnp.int32(0)
        total = (count + span - 1) // span * d
        steps = (total + UNROLL * each - 1) // (UNROLL * each)
        carry = lax.fori_loop(0, steps, step, (zero, zero, walk(zero, zero)[0]))
        finish(carry[2], held)

    def keep_last(i, low):
        final[pl.ds(pl.multiple_of(i * PITCH, 8), chans), :] = low

    def turn(chunk):
        @functools.partial(lax.fori_loop, 0, CHUNK // 16, init_val=0, unroll=True)
        def _(block, carry):
            first = pl.multiple_of(chunk * CHUNK + block * 16, 16)
            for c in range(chans):
                taken = final[pl.ds(first * PITCH + c, 16, stride=PITCH), :]
                out[c, pl.ds(first, 16), :] = taken.astype(jnp.bfloat16)
            return carry

    def send(chunk):
        rows = pl.ds(chunk * CHUNK, CHUNK)
        return pltpu.make_async_copy(out.at[:, rows, :], out_far.at[:, rows, :], sent.at[chunk])

    early = 2

    def turn_early(step):
        turn(jnp.clip(step - 2, 0, early - 1))

    tower(0, field_a, 2 * DMAX2, dils[1] + dils[2], keep(field_b, dils[1], True))
    clear(field_b, 2 * DMAX2)
    tower(1, field_b, DMAX2, dils[2], keep(field_a, dils[2], True))
    clear(field_a, DMAX2)
    tower(2, field_a, 0, 0, keep_last, turn_early)

    for k in range(tile_rows // CHUNK):
        if k >= early:
            turn(k)
        send(k).start()
    for k in range(tile_rows // CHUNK):
        send(k).wait()


def banded(map_weight, map_bias):
    layers, _, _, outs, ins = map_weight.shape
    taps = jnp.transpose(map_weight, (0, 3, 1, 2, 4)).reshape(layers, outs, 9 * ins)
    left = map_bias
    split = []
    for _ in range(3):
        split.append(lax.reduce_precision(left, 8, 7))
        left = left - split[-1]
    split = jnp.stack(split, axis=2).astype(jnp.bfloat16)
    rows = []
    for k in range(GROUP):
        before, after = k * 3 * ins, (GROUP - 1 - k) * 3 * ins
        row = jnp.pad(taps, ((0, 0), (0, 0), (before, after)))
        rows.append(jnp.concatenate([row, jnp.pad(split, ((0, 0), (0, 0), (0, TAIL - 3)))], axis=2))
    return jnp.concatenate(rows, axis=1)


def pair_call(place, gathered, dist_gain, bands, tile_rows, tile_cols):
    chans = dist_gain.shape[0]
    smem = pl.BlockSpec(memory_space=pltpu.SMEM)
    vmem = pl.BlockSpec(memory_space=pltpu.VMEM)
    span = tile_rows + 6 * DMAX2
    return pl.pallas_call(
        functools.partial(pair_kernel, gathered.shape[0], place.shape[0] - 3),
        out_shape=jax.ShapeDtypeStruct((chans, tile_rows, tile_cols), jnp.bfloat16),
        in_specs=[smem] + [vmem] * 3,
        out_specs=pl.BlockSpec(memory_space=pltpu.HBM),
        scratch_shapes=[
            pltpu.VMEM((4, chans, 128), jnp.float32),
            pltpu.VMEM((span, LANES), jnp.float32),
            pltpu.VMEM((span, 3 * chans, LANES), jnp.bfloat16),
            pltpu.VMEM((span - 2 * DMAX2, 3 * chans, LANES), jnp.bfloat16),
            pltpu.VMEM((tile_rows * PITCH, 128), jnp.float32),
            pltpu.VMEM((GROUP * chans, WIDE * LANES), jnp.float32),
            pltpu.VMEM((chans, tile_rows, tile_cols), jnp.bfloat16),
            pltpu.SemaphoreType.DMA((tile_rows // CHUNK,)),
        ],
        compiler_params=pltpu.CompilerParams(vmem_limit_bytes=48 * 2**20),
        cost_estimate=pl.CostEstimate(
            flops=3 * 2 * tile_rows * 9 * chans * chans * LANES,
            bytes_accessed=tile_rows * tile_cols * chans * 2,
            transcendentals=0,
        ),
        name="pair_tower",
    )(
        place, gathered, dist_gain.reshape(chans, 1), bands,
    )


def on_device(
    features,
    tower_weight,
    tower_bias,
    pair_proj,
    dist_gain,
    map_weight,
    map_bias,
    dilations,
    start_bin,
):
    row_count = lax.axis_size("rows")
    col_count = lax.axis_size("cols")
    shards = row_count * col_count
    shard, width = features.shape
    total = shard * shards
    tile_rows = total // row_count
    tile_cols = total // col_count
    chans = map_weight.shape[-1]
    row_place = lax.axis_index("rows")
    col_place = lax.axis_index("cols")
    mine = row_place * col_count + col_place
    place = jnp.stack([mine, row_place, col_place, row_count, col_count]).astype(jnp.int32)
    place = jnp.concatenate([place, dilations])

    inner = [(i, i ^ 1) for i in range(shards)]
    outer = [(i, i + 1 if i % 2 else i - 1) for i in range(1, shards - 1)]
    brought = lax.ppermute(features, AXES, inner)
    brought, start_bin = lax.optimization_barrier((brought, start_bin))
    both = jnp.concatenate([features, brought], axis=0)
    from_outer = lax.ppermute(both, AXES, outer)
    code = position_code(mine * shard + jnp.arange(shard), start_bin[0], chans)
    code = jnp.pad(code, ((0, 0), (0, width - chans)))
    extra = jnp.concatenate([tower_bias, code], axis=0)
    proj = jnp.pad(pair_proj.T, ((0, 2 * chans), (0, 0)))
    weight = fetch_call(lax.optimization_barrier((tower_weight, both))[0])
    from_outer, extra, proj, place, weight = lax.optimization_barrier(
        (from_outer, extra, proj, place, weight)
    )
    from_inner = lax.ppermute(from_outer, AXES, inner)

    smem = pl.BlockSpec(memory_space=pltpu.SMEM)
    vmem = pl.BlockSpec(memory_space=pltpu.VMEM)
    parts, none_16, none_32 = pl.pallas_call(
        functools.partial(encode_kernel, total),
        out_shape=[
            jax.ShapeDtypeStruct((shards, shard // 2, 4 * chans), jnp.bfloat16),
            jax.ShapeDtypeStruct(map_weight.shape, map_weight.dtype),
            jax.ShapeDtypeStruct((map_bias.shape[0] + 1, chans), jnp.float32),
        ],
        in_specs=[smem] + [vmem] * 6,
        out_specs=[vmem] * 3,
        scratch_shapes=[
            pltpu.VMEM((width // 128, 5 * shard, 128), jnp.float32),
            pltpu.VMEM((width // 128, 3 * shard, 128), jnp.float32),
        ],
        compiler_params=pltpu.CompilerParams(vmem_limit_bytes=16 * 2**20),
        cost_estimate=pl.CostEstimate(
            flops=2 * 4 * shard * 3 * width * width,
            bytes_accessed=6 * width * width * 2,
            transcendentals=0,
        ),
        name="encode",
    )(
        place, both, from_outer, from_inner, proj, extra, weight,
    )

    gathered = lax.all_to_all(parts, AXES, split_axis=0, concat_axis=0, tiled=True)

    bands = banded(map_weight + none_16, map_bias + none_32[:-1])
    dist_gain = dist_gain + none_32[-1]

    return pair_call(
        place, gathered, dist_gain, bands, tile_rows, tile_cols
    )


def solution(mesh):
    placed = (P(AXES, None), P(), P(), P(), P(), P(), P(), P(), P())
    return jax.shard_map(
        on_device, mesh=mesh, in_specs=placed, out_specs=P(None, "rows", "cols"), check_vma=False
    )
```

```python
import functools
import math

import jax
import jax.numpy as jnp
from jax import lax
from jax.experimental import pallas as pl
from jax.experimental.pallas import tpu as pltpu
from jax.sharding import PartitionSpec as P

DMAX1 = 16
DMAX2 = 16
GROUP = 4
TAIL = 32
WIDE = 2
UNROLL = 4
LANES = 256
PITCH = 40
FETCH_LIMIT = 50
CHUNK = 64
OUTSIDE = -1e30
AXES = ("rows", "cols")


def position_code(bin_index, start_pos, map_width):
    half_width = map_width // 2
    position = ((start_pos + bin_index) % 8192).astype(jnp.float32)
    rates = jnp.exp(-jnp.arange(half_width).astype(jnp.float32) * (math.log(1000.0) / half_width))
    phase_angle = position[:, None] * rates[None, :]
    return jnp.concatenate([jnp.cos(phase_angle), jnp.sin(phase_angle)], axis=1)


def fetch_kernel(far, near, arrived):
    copies = [
        pltpu.make_async_copy(far.at[which, tap], near.at[which, tap], arrived.at[which, tap])
        for which in range(far.shape[0])
        for tap in range(far.shape[1])
    ]
    for copy in copies:
        copy.start()
    for copy in copies:
        copy.wait()


def fetch_call(far):
    return pl.pallas_call(
        fetch_kernel,
        out_shape=jax.ShapeDtypeStruct(far.shape, far.dtype),
        in_specs=[pl.BlockSpec(memory_space=pltpu.HBM)],
        out_specs=pl.BlockSpec(memory_space=pltpu.VMEM),
        scratch_shapes=[pltpu.SemaphoreType.DMA(far.shape[:2])],
        compiler_params=pltpu.CompilerParams(vmem_limit_bytes=FETCH_LIMIT * 2**20),
        name="fetch",
    )(far)


def encode_kernel(
    total, place, both, outer, inner, proj, extra, weight, out, none_16, none_32, wide, mid,
):
    count = both.shape[0] // 2
    bias = extra[:2, :]
    chunks = wide.shape[0]

    def keep(ref, first, value):
        for k in range(chunks):
            ref[k, pl.ds(first, value.shape[0]), :] = value[:, k * 128 : (k + 1) * 128]

    def run(ref, first, span):
        return jnp.concatenate([ref[k, pl.ds(first, span), :] for k in range(chunks)], axis=1)

    def layer(which, ref, span):
        running = jnp.zeros((span, chunks * 128), jnp.float32)
        for tap in range(3):
            rows = run(ref, count + (tap - 1) * place[5 + which], span).astype(jnp.bfloat16)
            running += jnp.dot(rows, weight[which, tap], preferred_element_type=jnp.float32)
        return run(ref, count, span) + jnp.maximum(running + bias[which : which + 1, :], 0.0)

    odd = place[0] % 2
    for side, ref, half in ((2, both, 0), (3 - 2 * odd, both, 1), (1 + 2 * odd, outer, 0),
                            (4 * odd, outer, 1), (4 - 4 * odd, inner, 0)):
        first = side * count
        if ref is not both or half:
            first = pl.multiple_of(first, count)
        keep(wide, first, ref[half * count : (half + 1) * count, :].astype(jnp.float32))
    value = layer(0, wide, 3 * count).astype(jnp.bfloat16).astype(jnp.float32)
    index = (place[0] - 1) * count + lax.broadcasted_iota(jnp.int32, value.shape, 0)
    keep(mid, 0, jnp.where((index >= 0) & (index < total), value, 0.0))
    value = layer(1, mid, count)
    parts = lax.dot_general(
        value.astype(jnp.bfloat16),
        proj[...],
        (((1,), (1,)), ((), ())),
        preferred_element_type=jnp.float32,
    )
    parts = (parts + extra[2 : 2 + count, : proj.shape[0]]).astype(jnp.bfloat16)
    parts = parts[:, : proj.shape[0] // 2]
    parts = jnp.concatenate([parts[: count // 2], parts[count // 2 :]], axis=1)
    out[...] = jnp.broadcast_to(parts[None], out.shape)
    none_16[...] = jnp.zeros(none_16.shape, none_16.dtype)
    none_32[...] = jnp.zeros(none_32.shape, none_32.dtype)


def local_columns(rows):
    lane = lax.broadcasted_iota(jnp.int32, (rows, LANES), 1)
    return jnp.where(lane < LANES - 3 * DMAX2 - 8, lane, lane - LANES)


def pair_kernel(
    total_shards, first_dil, place, parts, gain, weight, out_far,
    row_turned, distance, field_a, field_b, final, held, out, sent,
):
    shard = 2 * parts.shape[1]
    chans = gain.shape[0]
    tile_rows = out.shape[1]
    margin = 3 * DMAX2
    reach = margin // shard
    row_place, col_place = place[1], place[2]
    last_row = place[3] - 1
    row_first = row_place * tile_rows
    col_first = col_place * 128
    dils = [place[first_dil + k] for k in range(3)]

    def pieces(first, count, wrap):
        taken = []
        for k in range(count):
            step = k - count if k >= wrap else k
            both = parts[jnp.clip(first + step, 0, total_shards - 1)]
            taken += [both[:, : 2 * chans], both[:, 2 * chans :]]
        return jnp.concatenate(taken, axis=0).astype(jnp.float32)

    col_glob = col_first + local_columns(1)
    inside = (col_glob >= 0) & (col_glob < total_shards * shard)
    inside_high = jnp.where(inside[:, 128:], 1.0, 0.0)
    inside_high = jnp.broadcast_to(inside_high, (chans, 128)).astype(jnp.bfloat16)

    cols = pieces(col_first // shard, LANES // shard, LANES // shard - reach)
    col_turned = jnp.transpose(cols)[chans : 2 * chans, :]
    col_turned = jnp.where(inside, col_turned, OUTSIDE)
    span0 = tile_rows + 2 * margin
    count = -(-span0 // shard)
    half = shard // 2
    rows = [
        parts[jnp.clip(row_first // shard - reach + k, 0, total_shards - 1)] for k in range(count)
    ]
    rows = jnp.transpose(jnp.concatenate(rows, axis=0).astype(jnp.float32))
    spot = lax.broadcasted_iota(jnp.int32, (1, count * half), 1)
    for side in range(2):
        row_glob = row_first - margin + spot // half * shard + side * half + spot % half
        valid = (row_glob >= 0) & (row_glob < total_shards * shard)
        turned = rows[side * 2 * chans : (side * 2 + 1) * chans, :]
        turned = jnp.where(valid, turned, OUTSIDE)
        row_turned[2 * side] = turned[:, :128]
        row_turned[2 * side + 1, :, : count * half - 128] = turned[:, 128:]

    row_local = lax.broadcasted_iota(jnp.int32, (span0, LANES), 0) - margin
    apart = jnp.abs(row_first + row_local - col_glob)
    distance[...] = jnp.log(1.0 + apart.astype(jnp.float32)) * 0.125
    gain_wide = jnp.broadcast_to(gain[...], (chans, LANES))
    lane16 = lax.broadcasted_iota(jnp.int16, (chans, 128), 1)

    def keep(field, d, masked, narrow=False):
        back = 128 - d
        at_left = lane16 < d.astype(jnp.int16)
        at_right = lane16 >= back.astype(jnp.int16)

        def store(i, low, high):
            low = low.astype(jnp.bfloat16)
            high = high.astype(jnp.bfloat16)
            if masked:
                high = high * inside_high
            field[i, chans : 2 * chans, :128] = low
            turned_low, turned_high = pltpu.roll(low, d, 1), pltpu.roll(high, d, 1)
            field[i, :chans, :128] = jnp.where(at_left, turned_high, turned_low)
            if not narrow:
                field[i, chans : 2 * chans, 128:] = high
                field[i, :chans, 128:] = jnp.where(at_left, turned_low, turned_high)
            turned_low, turned_high = pltpu.roll(low, back, 1), pltpu.roll(high, back, 1)
            field[i, 2 * chans :, :128] = jnp.where(at_right, turned_high, turned_low)
            if not narrow:
                field[i, 2 * chans :, 128:] = jnp.where(at_right, turned_low, turned_high)

        return store

    def clear(field, extra):
        @pl.when(row_place == 0)
        def _():
            @pl.loop(0, extra)
            def _(i):
                field[i] = jnp.zeros(field.shape[1:], field.dtype)

        @pl.when(row_place == last_row)
        def _():
            @pl.loop(0, extra)
            def _(i):
                field[extra + tile_rows + i] = jnp.zeros(field.shape[1:], field.dtype)

    need = dils[0] + dils[1] + dils[2]
    store_first = keep(field_a, dils[0], False)
    first_row, last_row_needed = margin - need, margin + tile_rows + need - 1

    @pl.loop(first_row // half, last_row_needed // half + 1)
    def _(block):
        first = pl.multiple_of(block * half, half)
        spot = block // 2 * half
        turned = row_turned[block % 2 * 2 + spot // 128]
        apart = distance[pl.ds(first, half), :]
        for k in range(half):
            pick = jnp.full((chans, 128), spot % 128 + k, jnp.int32)
            row_term = jnp.take_along_axis(turned, pick, axis=1)
            row_term = jnp.concatenate([row_term, row_term], axis=1)
            value = row_term + col_turned + gain_wide * apart[k : k + 1, :]
            value = jnp.maximum(value, 0.0)
            store_first(first + k, value[:, :128], value[:, 128:])

    tail = jnp.ones((TAIL, WIDE * LANES), jnp.bfloat16)

    def tower(layer, source, extra, need, store, first_in_step=None):
        d = dils[layer]
        span = GROUP * d
        first = extra - need
        count = tile_rows + 2 * need
        final_layer = layer == 2
        width = 128 if final_layer else LANES
        each = WIDE * LANES // width

        def product(bases):
            taps = []
            for k in range(GROUP + 2):
                at = [base + DMAX2 + (k - 1) * d for base in bases]
                taps.append(jnp.concatenate([source[i, :, :width] for i in at], axis=1))
            stack = jnp.concatenate(taps + [tail], axis=0)
            return jnp.dot(weight[layer], stack, preferred_element_type=jnp.float32)

        def finish(bases, sums):
            for n, base in enumerate(bases):
                for k in range(GROUP):
                    at = slice(n * width, (n + 1) * width)
                    center = source[base + DMAX2 + k * d, chans : 2 * chans, :width]
                    value = sums[k * chans : (k + 1) * chans, at]
                    if final_layer:
                        value = center.astype(jnp.float32) + jnp.maximum(value, 0.0)
                        store(base + k * d, value)
                    else:
                        value = center + jnp.maximum(value.astype(jnp.bfloat16), 0)
                        store(base + k * d, value[:, :128], value[:, 128:])

        def walk(start, phase):
            bases = []
            for _ in range(each):
                bases.append(first + jnp.minimum(start, count - span) + phase)
                wrap = phase + 1 >= d
                start = jnp.where(wrap, start + span, start)
                phase = jnp.where(wrap, 0, phase + 1)
            return bases, start, phase

        def step(index, carry):
            start, phase, bases = carry
            if first_in_step is not None:
                first_in_step(index)
            sums = held
            for k in range(UNROLL):
                next_bases, start, phase = walk(start, phase)
                next_sums = product(next_bases)
                finish(bases, sums)
                bases, sums = next_bases, next_sums
            held[...] = sums
            return start, phase, bases

        zero = jnp.int32(0)
        total = (count + span - 1) // span * d
        steps = (total + UNROLL * each - 1) // (UNROLL * each)
        carry = lax.fori_loop(0, steps, step, (zero, zero, walk(zero, zero)[0]))
        finish(carry[2], held)

    def keep_last(i, low):
        final[pl.ds(pl.multiple_of(i * PITCH, 8), chans), :] = low

    def turn(chunk):
        @functools.partial(lax.fori_loop, 0, CHUNK // 16, init_val=0, unroll=True)
        def _(block, carry):
            first = pl.multiple_of(chunk * CHUNK + block * 16, 16)
            for c in range(chans):
                taken = final[pl.ds(first * PITCH + c, 16, stride=PITCH), :]
                out[c, pl.ds(first, 16), :] = taken.astype(jnp.bfloat16)
            return carry

    def send(chunk):
        rows = pl.ds(chunk * CHUNK, CHUNK)
        return pltpu.make_async_copy(out.at[:, rows, :], out_far.at[:, rows, :], sent.at[chunk])

    early = 2

    def turn_early(step):
        turn(jnp.clip(step - 2, 0, early - 1))

    tower(0, field_a, 2 * DMAX2, dils[1] + dils[2], keep(field_b, dils[1], True))
    clear(field_b, 2 * DMAX2)
    tower(1, field_b, DMAX2, dils[2], keep(field_a, dils[2], True, True))
    clear(field_a, DMAX2)
    tower(2, field_a, 0, 0, keep_last, turn_early)

    for k in range(tile_rows // CHUNK):
        if k >= early:
            turn(k)
        send(k).start()
    for k in range(tile_rows // CHUNK):
        send(k).wait()


def banded(map_weight, map_bias):
    layers, _, _, outs, ins = map_weight.shape
    taps = jnp.transpose(map_weight, (0, 3, 1, 2, 4)).reshape(layers, outs, 9 * ins)
    left = map_bias
    split = []
    for _ in range(3):
        split.append(lax.reduce_precision(left, 8, 7))
        left = left - split[-1]
    split = jnp.stack(split, axis=2).astype(jnp.bfloat16)
    rows = []
    for k in range(GROUP):
        before, after = k * 3 * ins, (GROUP - 1 - k) * 3 * ins
        row = jnp.pad(taps, ((0, 0), (0, 0), (before, after)))
        rows.append(jnp.concatenate([row, jnp.pad(split, ((0, 0), (0, 0), (0, TAIL - 3)))], axis=2))
    return jnp.concatenate(rows, axis=1)


def pair_call(place, gathered, dist_gain, bands, tile_rows, tile_cols):
    chans = dist_gain.shape[0]
    smem = pl.BlockSpec(memory_space=pltpu.SMEM)
    vmem = pl.BlockSpec(memory_space=pltpu.VMEM)
    span = tile_rows + 6 * DMAX2
    return pl.pallas_call(
        functools.partial(pair_kernel, gathered.shape[0], place.shape[0] - 3),
        out_shape=jax.ShapeDtypeStruct((chans, tile_rows, tile_cols), jnp.bfloat16),
        in_specs=[smem] + [vmem] * 3,
        out_specs=pl.BlockSpec(memory_space=pltpu.HBM),
        scratch_shapes=[
            pltpu.VMEM((4, chans, 128), jnp.float32),
            pltpu.VMEM((span, LANES), jnp.float32),
            pltpu.VMEM((span, 3 * chans, LANES), jnp.bfloat16),
            pltpu.VMEM((span - 2 * DMAX2, 3 * chans, LANES), jnp.bfloat16),
            pltpu.VMEM((tile_rows * PITCH, 128), jnp.float32),
            pltpu.VMEM((GROUP * chans, WIDE * LANES), jnp.float32),
            pltpu.VMEM((chans, tile_rows, tile_cols), jnp.bfloat16),
            pltpu.SemaphoreType.DMA((tile_rows // CHUNK,)),
        ],
        compiler_params=pltpu.CompilerParams(vmem_limit_bytes=48 * 2**20),
        cost_estimate=pl.CostEstimate(
            flops=3 * 2 * tile_rows * 9 * chans * chans * LANES,
            bytes_accessed=tile_rows * tile_cols * chans * 2,
            transcendentals=0,
        ),
        name="pair_tower",
    )(
        place, gathered, dist_gain.reshape(chans, 1), bands,
    )


def on_device(
    features,
    tower_weight,
    tower_bias,
    pair_proj,
    dist_gain,
    map_weight,
    map_bias,
    dilations,
    start_bin,
):
    row_count = lax.axis_size("rows")
    col_count = lax.axis_size("cols")
    shards = row_count * col_count
    shard, width = features.shape
    total = shard * shards
    tile_rows = total // row_count
    tile_cols = total // col_count
    chans = map_weight.shape[-1]
    row_place = lax.axis_index("rows")
    col_place = lax.axis_index("cols")
    mine = row_place * col_count + col_place
    place = jnp.stack([mine, row_place, col_place, row_count, col_count]).astype(jnp.int32)
    place = jnp.concatenate([place, dilations])

    inner = [(i, i ^ 1) for i in range(shards)]
    outer = [(i, i + 1 if i % 2 else i - 1) for i in range(1, shards - 1)]
    brought = lax.ppermute(features, AXES, inner)
    brought, start_bin = lax.optimization_barrier((brought, start_bin))
    both = jnp.concatenate([features, brought], axis=0)
    from_outer = lax.ppermute(both, AXES, outer)
    code = position_code(mine * shard + jnp.arange(shard), start_bin[0], chans)
    code = jnp.pad(code, ((0, 0), (0, width - chans)))
    extra = jnp.concatenate([tower_bias, code], axis=0)
    proj = jnp.pad(pair_proj.T, ((0, 2 * chans), (0, 0)))
    weight = fetch_call(lax.optimization_barrier((tower_weight, both))[0])
    from_outer, extra, proj, place, weight = lax.optimization_barrier(
        (from_outer, extra, proj, place, weight)
    )
    from_inner = lax.ppermute(from_outer, AXES, inner)

    smem = pl.BlockSpec(memory_space=pltpu.SMEM)
    vmem = pl.BlockSpec(memory_space=pltpu.VMEM)
    parts, none_16, none_32 = pl.pallas_call(
        functools.partial(encode_kernel, total),
        out_shape=[
            jax.ShapeDtypeStruct((shards, shard // 2, 4 * chans), jnp.bfloat16),
            jax.ShapeDtypeStruct(map_weight.shape, map_weight.dtype),
            jax.ShapeDtypeStruct((map_bias.shape[0] + 1, chans), jnp.float32),
        ],
        in_specs=[smem] + [vmem] * 6,
        out_specs=[vmem] * 3,
        scratch_shapes=[
            pltpu.VMEM((width // 128, 5 * shard, 128), jnp.float32),
            pltpu.VMEM((width // 128, 3 * shard, 128), jnp.float32),
        ],
        compiler_params=pltpu.CompilerParams(vmem_limit_bytes=16 * 2**20),
        cost_estimate=pl.CostEstimate(
            flops=2 * 4 * shard * 3 * width * width,
            bytes_accessed=6 * width * width * 2,
            transcendentals=0,
        ),
        name="encode",
    )(
        place, both, from_outer, from_inner, proj, extra, weight,
    )

    gathered = lax.all_to_all(parts, AXES, split_axis=0, concat_axis=0, tiled=True)

    bands = banded(map_weight + none_16, map_bias + none_32[:-1])
    dist_gain = dist_gain + none_32[-1]

    return pair_call(
        place, gathered, dist_gain, bands, tile_rows, tile_cols
    )


def solution(mesh):
    placed = (P(AXES, None), P(), P(), P(), P(), P(), P(), P(), P())
    return jax.shard_map(
        on_device, mesh=mesh, in_specs=placed, out_specs=P(None, "rows", "cols"), check_vma=False
    )
```

```python
import functools
import math

import jax
import jax.numpy as jnp
from jax import lax
from jax.experimental import pallas as pl
from jax.experimental.pallas import tpu as pltpu
from jax.sharding import PartitionSpec as P

DMAX1 = 16
DMAX2 = 16
GROUP = 4
TAIL = 32
WIDE = 2
UNROLL = (6, 6, 4)
LANES = 256
PITCH = 40
FETCH_LIMIT = 50
CHUNK = 64
OUTSIDE = -1e30
AXES = ("rows", "cols")


def position_code(bin_index, start_pos, map_width):
    half_width = map_width // 2
    position = ((start_pos + bin_index) % 8192).astype(jnp.float32)
    rates = jnp.exp(-jnp.arange(half_width).astype(jnp.float32) * (math.log(1000.0) / half_width))
    phase_angle = position[:, None] * rates[None, :]
    return jnp.concatenate([jnp.cos(phase_angle), jnp.sin(phase_angle)], axis=1)


def fetch_kernel(far, near, arrived):
    copies = [
        pltpu.make_async_copy(far.at[which, tap], near.at[which, tap], arrived.at[which, tap])
        for which in range(far.shape[0])
        for tap in range(far.shape[1])
    ]
    for copy in copies:
        copy.start()
    for copy in copies:
        copy.wait()


def fetch_call(far):
    return pl.pallas_call(
        fetch_kernel,
        out_shape=jax.ShapeDtypeStruct(far.shape, far.dtype),
        in_specs=[pl.BlockSpec(memory_space=pltpu.HBM)],
        out_specs=pl.BlockSpec(memory_space=pltpu.VMEM),
        scratch_shapes=[pltpu.SemaphoreType.DMA(far.shape[:2])],
        compiler_params=pltpu.CompilerParams(vmem_limit_bytes=FETCH_LIMIT * 2**20),
        name="fetch",
    )(far)


def encode_kernel(
    total, place, both, outer, inner, proj, extra, weight, out, none_16, none_32, wide, mid,
):
    count = both.shape[0] // 2
    bias = extra[:2, :]
    chunks = wide.shape[0]

    def keep(ref, first, value):
        for k in range(chunks):
            ref[k, pl.ds(first, value.shape[0]), :] = value[:, k * 128 : (k + 1) * 128]

    def run(ref, first, span):
        return jnp.concatenate([ref[k, pl.ds(first, span), :] for k in range(chunks)], axis=1)

    def layer(which, ref, span):
        running = jnp.zeros((span, chunks * 128), jnp.float32)
        for tap in range(3):
            rows = run(ref, count + (tap - 1) * place[5 + which], span).astype(jnp.bfloat16)
            running += jnp.dot(rows, weight[which, tap], preferred_element_type=jnp.float32)
        return run(ref, count, span) + jnp.maximum(running + bias[which : which + 1, :], 0.0)

    odd = place[0] % 2
    for side, ref, half in ((2, both, 0), (3 - 2 * odd, both, 1), (1 + 2 * odd, outer, 0),
                            (4 * odd, outer, 1), (4 - 4 * odd, inner, 0)):
        first = side * count
        if ref is not both or half:
            first = pl.multiple_of(first, count)
        keep(wide, first, ref[half * count : (half + 1) * count, :].astype(jnp.float32))
    value = layer(0, wide, 3 * count).astype(jnp.bfloat16).astype(jnp.float32)
    index = (place[0] - 1) * count + lax.broadcasted_iota(jnp.int32, value.shape, 0)
    keep(mid, 0, jnp.where((index >= 0) & (index < total), value, 0.0))
    value = layer(1, mid, count)
    parts = lax.dot_general(
        value.astype(jnp.bfloat16),
        proj[...],
        (((1,), (1,)), ((), ())),
        preferred_element_type=jnp.float32,
    )
    parts = (parts + extra[2 : 2 + count, : proj.shape[0]]).astype(jnp.bfloat16)
    parts = parts[:, : proj.shape[0] // 2]
    parts = jnp.concatenate([parts[: count // 2], parts[count // 2 :]], axis=1)
    out[...] = jnp.broadcast_to(parts[None], out.shape)
    none_16[...] = jnp.zeros(none_16.shape, none_16.dtype)
    none_32[...] = jnp.zeros(none_32.shape, none_32.dtype)


def local_columns(rows):
    lane = lax.broadcasted_iota(jnp.int32, (rows, LANES), 1)
    return jnp.where(lane < LANES - 3 * DMAX2 - 8, lane, lane - LANES)


def pair_kernel(
    total_shards, first_dil, place, parts, gain, weight, out_far,
    row_turned, distance, field_a, field_b, final, held, out, sent,
):
    shard = 2 * parts.shape[1]
    chans = gain.shape[0]
    tile_rows = out.shape[1]
    margin = 3 * DMAX2
    reach = margin // shard
    row_place, col_place = place[1], place[2]
    last_row = place[3] - 1
    row_first = row_place * tile_rows
    col_first = col_place * 128
    dils = [place[first_dil + k] for k in range(3)]

    def pieces(first, count, wrap):
        taken = []
        for k in range(count):
            step = k - count if k >= wrap else k
            both = parts[jnp.clip(first + step, 0, total_shards - 1)]
            taken += [both[:, : 2 * chans], both[:, 2 * chans :]]
        return jnp.concatenate(taken, axis=0).astype(jnp.float32)

    col_glob = col_first + local_columns(1)
    inside = (col_glob >= 0) & (col_glob < total_shards * shard)
    inside_high = jnp.where(inside[:, 128:], 1.0, 0.0)
    inside_high = jnp.broadcast_to(inside_high, (chans, 128)).astype(jnp.bfloat16)

    cols = pieces(col_first // shard, LANES // shard, LANES // shard - reach)
    col_turned = jnp.transpose(cols)[chans : 2 * chans, :]
    col_turned = jnp.where(inside, col_turned, OUTSIDE)
    span0 = tile_rows + 2 * margin
    count = -(-span0 // shard)
    half = shard // 2
    rows = [
        parts[jnp.clip(row_first // shard - reach + k, 0, total_shards - 1)] for k in range(count)
    ]
    rows = jnp.transpose(jnp.concatenate(rows, axis=0).astype(jnp.float32))
    spot = lax.broadcasted_iota(jnp.int32, (1, count * half), 1)
    for side in range(2):
        row_glob = row_first - margin + spot // half * shard + side * half + spot % half
        valid = (row_glob >= 0) & (row_glob < total_shards * shard)
        turned = rows[side * 2 * chans : (side * 2 + 1) * chans, :]
        turned = jnp.where(valid, turned, OUTSIDE)
        row_turned[2 * side] = turned[:, :128]
        row_turned[2 * side + 1, :, : count * half - 128] = turned[:, 128:]

    row_local = lax.broadcasted_iota(jnp.int32, (span0, LANES), 0) - margin
    apart = jnp.abs(row_first + row_local - col_glob)
    distance[...] = jnp.log(1.0 + apart.astype(jnp.float32)) * 0.125
    gain_wide = jnp.broadcast_to(gain[...], (chans, LANES))
    lane16 = lax.broadcasted_iota(jnp.int16, (chans, 128), 1)

    def keep(field, d, masked, narrow=False):
        back = 128 - d
        at_left = lane16 < d.astype(jnp.int16)
        at_right = lane16 >= back.astype(jnp.int16)

        def store(i, low, high):
            low = low.astype(jnp.bfloat16)
            high = high.astype(jnp.bfloat16)
            if masked:
                high = high * inside_high
            field[i, chans : 2 * chans, :128] = low
            turned_low, turned_high = pltpu.roll(low, d, 1), pltpu.roll(high, d, 1)
            field[i, :chans, :128] = jnp.where(at_left, turned_high, turned_low)
            if not narrow:
                field[i, chans : 2 * chans, 128:] = high
                field[i, :chans, 128:] = jnp.where(at_left, turned_low, turned_high)
            turned_low, turned_high = pltpu.roll(low, back, 1), pltpu.roll(high, back, 1)
            field[i, 2 * chans :, :128] = jnp.where(at_right, turned_high, turned_low)
            if not narrow:
                field[i, 2 * chans :, 128:] = jnp.where(at_right, turned_low, turned_high)

        return store

    def clear(field, extra):
        @pl.when(row_place == 0)
        def _():
            @pl.loop(0, extra)
            def _(i):
                field[i] = jnp.zeros(field.shape[1:], field.dtype)

        @pl.when(row_place == last_row)
        def _():
            @pl.loop(0, extra)
            def _(i):
                field[extra + tile_rows + i] = jnp.zeros(field.shape[1:], field.dtype)

    need = dils[0] + dils[1] + dils[2]
    store_first = keep(field_a, dils[0], False)
    first_row, last_row_needed = margin - need, margin + tile_rows + need - 1

    @pl.loop(first_row // half, last_row_needed // half + 1)
    def _(block):
        first = pl.multiple_of(block * half, half)
        spot = block // 2 * half
        turned = row_turned[block % 2 * 2 + spot // 128]
        apart = distance[pl.ds(first, half), :]
        for k in range(half):
            pick = jnp.full((chans, 128), spot % 128 + k, jnp.int32)
            row_term = jnp.take_along_axis(turned, pick, axis=1)
            row_term = jnp.concatenate([row_term, row_term], axis=1)
            value = row_term + col_turned + gain_wide * apart[k : k + 1, :]
            value = jnp.maximum(value, 0.0)
            store_first(first + k, value[:, :128], value[:, 128:])

    tail = jnp.ones((TAIL, WIDE * LANES), jnp.bfloat16)

    def tower(layer, source, extra, need, store, first_in_step=None):
        d = dils[layer]
        span = GROUP * d
        first = extra - need
        count = tile_rows + 2 * need
        final_layer = layer == 2
        width = 128 if final_layer else LANES
        each = WIDE * LANES // width

        def product(bases):
            taps = []
            for k in range(GROUP + 2):
                at = [base + DMAX2 + (k - 1) * d for base in bases]
                taps.append(jnp.concatenate([source[i, :, :width] for i in at], axis=1))
            stack = jnp.concatenate(taps + [tail], axis=0)
            return jnp.dot(weight[layer], stack, preferred_element_type=jnp.float32)

        def finish(bases, sums):
            for n, base in enumerate(bases):
                for k in range(GROUP):
                    at = slice(n * width, (n + 1) * width)
                    center = source[base + DMAX2 + k * d, chans : 2 * chans, :width]
                    value = sums[k * chans : (k + 1) * chans, at]
                    if final_layer:
                        value = center.astype(jnp.float32) + jnp.maximum(value, 0.0)
                        store(base + k * d, value)
                    else:
                        value = center + jnp.maximum(value.astype(jnp.bfloat16), 0)
                        store(base + k * d, value[:, :128], value[:, 128:])

        def walk(start, phase):
            bases = []
            for _ in range(each):
                bases.append(first + jnp.minimum(start, count - span) + phase)
                wrap = phase + 1 >= d
                start = jnp.where(wrap, start + span, start)
                phase = jnp.where(wrap, 0, phase + 1)
            return bases, start, phase

        def step(index, carry):
            start, phase, bases = carry
            if first_in_step is not None:
                first_in_step(index)
            sums = held
            for _ in range(UNROLL[layer]):
                next_bases, start, phase = walk(start, phase)
                next_sums = product(next_bases)
                finish(bases, sums)
                bases, sums = next_bases, next_sums
            held[...] = sums
            return start, phase, bases

        zero = jnp.int32(0)
        total = (count + span - 1) // span * d
        together = UNROLL[layer] * each
        steps = (total + together - 1) // together
        carry = lax.fori_loop(0, steps, step, (zero, zero, walk(zero, zero)[0]))
        finish(carry[2], held)

    def keep_last(i, low):
        final[pl.ds(pl.multiple_of(i * PITCH, 8), chans), :] = low

    def turn(chunk):
        @functools.partial(lax.fori_loop, 0, CHUNK // 16, init_val=0, unroll=True)
        def _(block, carry):
            first = pl.multiple_of(chunk * CHUNK + block * 16, 16)
            for c in range(chans):
                taken = final[pl.ds(first * PITCH + c, 16, stride=PITCH), :]
                out[c, pl.ds(first, 16), :] = taken.astype(jnp.bfloat16)
            return carry

    def send(chunk):
        rows = pl.ds(chunk * CHUNK, CHUNK)
        return pltpu.make_async_copy(out.at[:, rows, :], out_far.at[:, rows, :], sent.at[chunk])

    early = 2

    def turn_early(step):
        turn(jnp.clip(step - 2, 0, early - 1))

    tower(0, field_a, 2 * DMAX2, dils[1] + dils[2], keep(field_b, dils[1], True))
    clear(field_b, 2 * DMAX2)
    tower(1, field_b, DMAX2, dils[2], keep(field_a, dils[2], True, True))
    clear(field_a, DMAX2)
    tower(2, field_a, 0, 0, keep_last, turn_early)

    for k in range(tile_rows // CHUNK):
        if k >= early:
            turn(k)
        send(k).start()
    for k in range(tile_rows // CHUNK):
        send(k).wait()


def banded(map_weight, map_bias):
    layers, _, _, outs, ins = map_weight.shape
    taps = jnp.transpose(map_weight, (0, 3, 1, 2, 4)).reshape(layers, outs, 9 * ins)
    left = map_bias
    split = []
    for _ in range(3):
        split.append(lax.reduce_precision(left, 8, 7))
        left = left - split[-1]
    split = jnp.stack(split, axis=2).astype(jnp.bfloat16)
    rows = []
    for k in range(GROUP):
        before, after = k * 3 * ins, (GROUP - 1 - k) * 3 * ins
        row = jnp.pad(taps, ((0, 0), (0, 0), (before, after)))
        rows.append(jnp.concatenate([row, jnp.pad(split, ((0, 0), (0, 0), (0, TAIL - 3)))], axis=2))
    return jnp.concatenate(rows, axis=1)


def pair_call(place, gathered, dist_gain, bands, tile_rows, tile_cols):
    chans = dist_gain.shape[0]
    smem = pl.BlockSpec(memory_space=pltpu.SMEM)
    vmem = pl.BlockSpec(memory_space=pltpu.VMEM)
    span = tile_rows + 6 * DMAX2
    return pl.pallas_call(
        functools.partial(pair_kernel, gathered.shape[0], place.shape[0] - 3),
        out_shape=jax.ShapeDtypeStruct((chans, tile_rows, tile_cols), jnp.bfloat16),
        in_specs=[smem] + [vmem] * 3,
        out_specs=pl.BlockSpec(memory_space=pltpu.HBM),
        scratch_shapes=[
            pltpu.VMEM((4, chans, 128), jnp.float32),
            pltpu.VMEM((span, LANES), jnp.float32),
            pltpu.VMEM((span, 3 * chans, LANES), jnp.bfloat16),
            pltpu.VMEM((span - 2 * DMAX2, 3 * chans, LANES), jnp.bfloat16),
            pltpu.VMEM((tile_rows * PITCH, 128), jnp.float32),
            pltpu.VMEM((GROUP * chans, WIDE * LANES), jnp.float32),
            pltpu.VMEM((chans, tile_rows, tile_cols), jnp.bfloat16),
            pltpu.SemaphoreType.DMA((tile_rows // CHUNK,)),
        ],
        compiler_params=pltpu.CompilerParams(vmem_limit_bytes=48 * 2**20),
        cost_estimate=pl.CostEstimate(
            flops=3 * 2 * tile_rows * 9 * chans * chans * LANES,
            bytes_accessed=tile_rows * tile_cols * chans * 2,
            transcendentals=0,
        ),
        name="pair_tower",
    )(
        place, gathered, dist_gain.reshape(chans, 1), bands,
    )


def on_device(
    features,
    tower_weight,
    tower_bias,
    pair_proj,
    dist_gain,
    map_weight,
    map_bias,
    dilations,
    start_bin,
):
    row_count = lax.axis_size("rows")
    col_count = lax.axis_size("cols")
    shards = row_count * col_count
    shard, width = features.shape
    total = shard * shards
    tile_rows = total // row_count
    tile_cols = total // col_count
    chans = map_weight.shape[-1]
    row_place = lax.axis_index("rows")
    col_place = lax.axis_index("cols")
    mine = row_place * col_count + col_place
    place = jnp.stack([mine, row_place, col_place, row_count, col_count]).astype(jnp.int32)
    place = jnp.concatenate([place, dilations])

    inner = [(i, i ^ 1) for i in range(shards)]
    outer = [(i, i + 1 if i % 2 else i - 1) for i in range(1, shards - 1)]
    brought = lax.ppermute(features, AXES, inner)
    brought, start_bin = lax.optimization_barrier((brought, start_bin))
    both = jnp.concatenate([features, brought], axis=0)
    from_outer = lax.ppermute(both, AXES, outer)
    code = position_code(mine * shard + jnp.arange(shard), start_bin[0], chans)
    code = jnp.pad(code, ((0, 0), (0, width - chans)))
    extra = jnp.concatenate([tower_bias, code], axis=0)
    proj = jnp.pad(pair_proj.T, ((0, 2 * chans), (0, 0)))
    weight = fetch_call(lax.optimization_barrier((tower_weight, both))[0])
    from_outer, extra, proj, place, weight = lax.optimization_barrier(
        (from_outer, extra, proj, place, weight)
    )
    from_inner = lax.ppermute(from_outer, AXES, inner)

    smem = pl.BlockSpec(memory_space=pltpu.SMEM)
    vmem = pl.BlockSpec(memory_space=pltpu.VMEM)
    parts, none_16, none_32 = pl.pallas_call(
        functools.partial(encode_kernel, total),
        out_shape=[
            jax.ShapeDtypeStruct((shards, shard // 2, 4 * chans), jnp.bfloat16),
            jax.ShapeDtypeStruct(map_weight.shape, map_weight.dtype),
            jax.ShapeDtypeStruct((map_bias.shape[0] + 1, chans), jnp.float32),
        ],
        in_specs=[smem] + [vmem] * 6,
        out_specs=[vmem] * 3,
        scratch_shapes=[
            pltpu.VMEM((width // 128, 5 * shard, 128), jnp.float32),
            pltpu.VMEM((width // 128, 3 * shard, 128), jnp.float32),
        ],
        compiler_params=pltpu.CompilerParams(vmem_limit_bytes=16 * 2**20),
        cost_estimate=pl.CostEstimate(
            flops=2 * 4 * shard * 3 * width * width,
            bytes_accessed=6 * width * width * 2,
            transcendentals=0,
        ),
        name="encode",
    )(
        place, both, from_outer, from_inner, proj, extra, weight,
    )

    gathered = lax.all_to_all(parts, AXES, split_axis=0, concat_axis=0, tiled=True)

    bands = banded(map_weight + none_16, map_bias + none_32[:-1])
    dist_gain = dist_gain + none_32[-1]

    return pair_call(
        place, gathered, dist_gain, bands, tile_rows, tile_cols
    )


def solution(mesh):
    placed = (P(AXES, None), P(), P(), P(), P(), P(), P(), P(), P())
    return jax.shard_map(
        on_device, mesh=mesh, in_specs=placed, out_specs=P(None, "rows", "cols"), check_vma=False
    )
```

```python
import functools
import math

import jax
import jax.numpy as jnp
from jax import lax
from jax.experimental import pallas as pl
from jax.experimental.pallas import tpu as pltpu
from jax.sharding import PartitionSpec as P

DMAX1 = 16
DMAX2 = 16
GROUP = 4
TAIL = 32
WIDE = 2
UNROLL = (8, 8, 4)
LANES = 256
PITCH = 40
FETCH_LIMIT = 50
CHUNK = 64
OUTSIDE = -1e30
AXES = ("rows", "cols")


def position_code(bin_index, start_pos, map_width):
    half_width = map_width // 2
    position = ((start_pos + bin_index) % 8192).astype(jnp.float32)
    rates = jnp.exp(-jnp.arange(half_width).astype(jnp.float32) * (math.log(1000.0) / half_width))
    phase_angle = position[:, None] * rates[None, :]
    return jnp.concatenate([jnp.cos(phase_angle), jnp.sin(phase_angle)], axis=1)


def fetch_kernel(far, near, arrived):
    copies = [
        pltpu.make_async_copy(far.at[which, tap], near.at[which, tap], arrived.at[which, tap])
        for which in range(far.shape[0])
        for tap in range(far.shape[1])
    ]
    for copy in copies:
        copy.start()
    for copy in copies:
        copy.wait()


def fetch_call(far):
    return pl.pallas_call(
        fetch_kernel,
        out_shape=jax.ShapeDtypeStruct(far.shape, far.dtype),
        in_specs=[pl.BlockSpec(memory_space=pltpu.HBM)],
        out_specs=pl.BlockSpec(memory_space=pltpu.VMEM),
        scratch_shapes=[pltpu.SemaphoreType.DMA(far.shape[:2])],
        compiler_params=pltpu.CompilerParams(vmem_limit_bytes=FETCH_LIMIT * 2**20),
        name="fetch",
    )(far)


def encode_kernel(
    total, place, both, outer, inner, proj, extra, weight, out, none_16, none_32, wide, mid,
):
    count = both.shape[0] // 2
    bias = extra[:2, :]
    chunks = wide.shape[0]

    def keep(ref, first, value):
        for k in range(chunks):
            ref[k, pl.ds(first, value.shape[0]), :] = value[:, k * 128 : (k + 1) * 128]

    def run(ref, first, span):
        return jnp.concatenate([ref[k, pl.ds(first, span), :] for k in range(chunks)], axis=1)

    def layer(which, ref, span):
        running = jnp.zeros((span, chunks * 128), jnp.float32)
        for tap in range(3):
            rows = run(ref, count + (tap - 1) * place[5 + which], span).astype(jnp.bfloat16)
            running += jnp.dot(rows, weight[which, tap], preferred_element_type=jnp.float32)
        return run(ref, count, span) + jnp.maximum(running + bias[which : which + 1, :], 0.0)

    odd = place[0] % 2
    for side, ref, half in ((2, both, 0), (3 - 2 * odd, both, 1), (1 + 2 * odd, outer, 0),
                            (4 * odd, outer, 1), (4 - 4 * odd, inner, 0)):
        first = side * count
        if ref is not both or half:
            first = pl.multiple_of(first, count)
        keep(wide, first, ref[half * count : (half + 1) * count, :].astype(jnp.float32))
    value = layer(0, wide, 3 * count).astype(jnp.bfloat16).astype(jnp.float32)
    index = (place[0] - 1) * count + lax.broadcasted_iota(jnp.int32, value.shape, 0)
    keep(mid, 0, jnp.where((index >= 0) & (index < total), value, 0.0))
    value = layer(1, mid, count)
    parts = lax.dot_general(
        value.astype(jnp.bfloat16),
        proj[...],
        (((1,), (1,)), ((), ())),
        preferred_element_type=jnp.float32,
    )
    parts = (parts + extra[2 : 2 + count, : proj.shape[0]]).astype(jnp.bfloat16)
    parts = parts[:, : proj.shape[0] // 2]
    parts = jnp.concatenate([parts[: count // 2], parts[count // 2 :]], axis=1)
    out[...] = jnp.broadcast_to(parts[None], out.shape)
    none_16[...] = jnp.zeros(none_16.shape, none_16.dtype)
    none_32[...] = jnp.zeros(none_32.shape, none_32.dtype)


def local_columns(rows):
    lane = lax.broadcasted_iota(jnp.int32, (rows, LANES), 1)
    return jnp.where(lane < LANES - 3 * DMAX2 - 8, lane, lane - LANES)


def pair_kernel(
    total_shards, first_dil, place, parts, gain, weight, out_far,
    row_turned, distance, field_a, field_b, final, held, out, sent,
):
    shard = 2 * parts.shape[1]
    chans = gain.shape[0]
    tile_rows = out.shape[1]
    margin = 3 * DMAX2
    reach = margin // shard
    row_place, col_place = place[1], place[2]
    last_row = place[3] - 1
    row_first = row_place * tile_rows
    col_first = col_place * 128
    dils = [place[first_dil + k] for k in range(3)]

    def pieces(first, count, wrap):
        taken = []
        for k in range(count):
            step = k - count if k >= wrap else k
            both = parts[jnp.clip(first + step, 0, total_shards - 1)]
            taken += [both[:, : 2 * chans], both[:, 2 * chans :]]
        return jnp.concatenate(taken, axis=0).astype(jnp.float32)

    col_glob = col_first + local_columns(1)
    inside = (col_glob >= 0) & (col_glob < total_shards * shard)
    inside_high = jnp.where(inside[:, 128:], 1.0, 0.0)
    inside_high = jnp.broadcast_to(inside_high, (chans, 128)).astype(jnp.bfloat16)

    cols = pieces(col_first // shard, LANES // shard, LANES // shard - reach)
    col_turned = jnp.transpose(cols)[chans : 2 * chans, :]
    col_turned = jnp.where(inside, col_turned, OUTSIDE)
    span0 = tile_rows + 2 * margin
    count = -(-span0 // shard)
    half = shard // 2
    rows = [
        parts[jnp.clip(row_first // shard - reach + k, 0, total_shards - 1)] for k in range(count)
    ]
    rows = jnp.transpose(jnp.concatenate(rows, axis=0).astype(jnp.float32))
    spot = lax.broadcasted_iota(jnp.int32, (1, count * half), 1)
    for side in range(2):
        row_glob = row_first - margin + spot // half * shard + side * half + spot % half
        valid = (row_glob >= 0) & (row_glob < total_shards * shard)
        turned = rows[side * 2 * chans : (side * 2 + 1) * chans, :]
        turned = jnp.where(valid, turned, OUTSIDE)
        row_turned[2 * side] = turned[:, :128]
        row_turned[2 * side + 1, :, : count * half - 128] = turned[:, 128:]

    row_local = lax.broadcasted_iota(jnp.int32, (span0, LANES), 0) - margin
    apart = jnp.abs(row_first + row_local - col_glob)
    distance[...] = jnp.log(1.0 + apart.astype(jnp.float32)) * 0.125
    gain_wide = jnp.broadcast_to(gain[...], (chans, LANES))
    lane16 = lax.broadcasted_iota(jnp.int16, (chans, 128), 1)

    def keep(field, d, masked, narrow=False):
        back = 128 - d
        at_left = lane16 < d.astype(jnp.int16)
        at_right = lane16 >= back.astype(jnp.int16)

        def store(i, low, high):
            low = low.astype(jnp.bfloat16)
            high = high.astype(jnp.bfloat16)
            if masked:
                high = high * inside_high
            field[i, chans : 2 * chans, :128] = low
            turned_low, turned_high = pltpu.roll(low, d, 1), pltpu.roll(high, d, 1)
            field[i, :chans, :128] = jnp.where(at_left, turned_high, turned_low)
            if not narrow:
                field[i, chans : 2 * chans, 128:] = high
                field[i, :chans, 128:] = jnp.where(at_left, turned_low, turned_high)
            turned_low, turned_high = pltpu.roll(low, back, 1), pltpu.roll(high, back, 1)
            field[i, 2 * chans :, :128] = jnp.where(at_right, turned_high, turned_low)
            if not narrow:
                field[i, 2 * chans :, 128:] = jnp.where(at_right, turned_low, turned_high)

        return store

    def clear(field, extra):
        @pl.when(row_place == 0)
        def _():
            @pl.loop(0, extra)
            def _(i):
                field[i] = jnp.zeros(field.shape[1:], field.dtype)

        @pl.when(row_place == last_row)
        def _():
            @pl.loop(0, extra)
            def _(i):
                field[extra + tile_rows + i] = jnp.zeros(field.shape[1:], field.dtype)

    need = dils[0] + dils[1] + dils[2]
    store_first = keep(field_a, dils[0], False)
    first_row, last_row_needed = margin - need, margin + tile_rows + need - 1

    @pl.loop(first_row // half, last_row_needed // half + 1)
    def _(block):
        first = pl.multiple_of(block * half, half)
        spot = block // 2 * half
        turned = row_turned[block % 2 * 2 + spot // 128]
        apart = distance[pl.ds(first, half), :]
        for k in range(half):
            pick = jnp.full((chans, 128), spot % 128 + k, jnp.int32)
            row_term = jnp.take_along_axis(turned, pick, axis=1)
            row_term = jnp.concatenate([row_term, row_term], axis=1)
            value = row_term + col_turned + gain_wide * apart[k : k + 1, :]
            value = jnp.maximum(value, 0.0)
            store_first(first + k, value[:, :128], value[:, 128:])

    tail = jnp.ones((TAIL, WIDE * LANES), jnp.bfloat16)

    def tower(layer, source, extra, need, store, first_in_step=None):
        d = dils[layer]
        span = GROUP * d
        first = extra - need
        count = tile_rows + 2 * need
        final_layer = layer == 2
        width = 128 if final_layer else LANES
        each = WIDE * LANES // width

        def product(bases):
            taps = []
            for k in range(GROUP + 2):
                at = [base + DMAX2 + (k - 1) * d for base in bases]
                taps.append(jnp.concatenate([source[i, :, :width] for i in at], axis=1))
            stack = jnp.concatenate(taps + [tail], axis=0)
            return jnp.dot(weight[layer], stack, preferred_element_type=jnp.float32)

        def finish(bases, sums):
            for n, base in enumerate(bases):
                for k in range(GROUP):
                    at = slice(n * width, (n + 1) * width)
                    center = source[base + DMAX2 + k * d, chans : 2 * chans, :width]
                    value = sums[k * chans : (k + 1) * chans, at]
                    if final_layer:
                        value = center.astype(jnp.float32) + jnp.maximum(value, 0.0)
                        store(base + k * d, value)
                    else:
                        value = center + jnp.maximum(value.astype(jnp.bfloat16), 0)
                        store(base + k * d, value[:, :128], value[:, 128:])

        def walk(start, phase):
            bases = []
            for _ in range(each):
                bases.append(first + jnp.minimum(start, count - span) + phase)
                wrap = phase + 1 >= d
                start = jnp.where(wrap, start + span, start)
                phase = jnp.where(wrap, 0, phase + 1)
            return bases, start, phase

        def step(index, carry):
            start, phase, bases = carry
            if first_in_step is not None:
                first_in_step(index)
            sums = held
            for _ in range(UNROLL[layer]):
                next_bases, start, phase = walk(start, phase)
                next_sums = product(next_bases)
                finish(bases, sums)
                bases, sums = next_bases, next_sums
            held[...] = sums
            return start, phase, bases

        zero = jnp.int32(0)
        total = (count + span - 1) // span * d
        together = UNROLL[layer] * each
        steps = (total + together - 1) // together
        carry = lax.fori_loop(0, steps, step, (zero, zero, walk(zero, zero)[0]))
        finish(carry[2], held)

    def keep_last(i, low):
        final[pl.ds(pl.multiple_of(i * PITCH, 8), chans), :] = low

    def turn(chunk):
        @functools.partial(lax.fori_loop, 0, CHUNK // 16, init_val=0, unroll=True)
        def _(block, carry):
            first = pl.multiple_of(chunk * CHUNK + block * 16, 16)
            for c in range(chans):
                taken = final[pl.ds(first * PITCH + c, 16, stride=PITCH), :]
                out[c, pl.ds(first, 16), :] = taken.astype(jnp.bfloat16)
            return carry

    def send(chunk):
        rows = pl.ds(chunk * CHUNK, CHUNK)
        return pltpu.make_async_copy(out.at[:, rows, :], out_far.at[:, rows, :], sent.at[chunk])

    early = 2

    def turn_early(step):
        turn(jnp.clip(step - 2, 0, early - 1))

    tower(0, field_a, 2 * DMAX2, dils[1] + dils[2], keep(field_b, dils[1], True))
    clear(field_b, 2 * DMAX2)
    tower(1, field_b, DMAX2, dils[2], keep(field_a, dils[2], True, True))
    clear(field_a, DMAX2)
    tower(2, field_a, 0, 0, keep_last, turn_early)

    for k in range(tile_rows // CHUNK):
        if k >= early:
            turn(k)
        send(k).start()
    for k in range(tile_rows // CHUNK):
        send(k).wait()


def banded(map_weight, map_bias):
    layers, _, _, outs, ins = map_weight.shape
    taps = jnp.transpose(map_weight, (0, 3, 1, 2, 4)).reshape(layers, outs, 9 * ins)
    left = map_bias
    split = []
    for _ in range(3):
        split.append(lax.reduce_precision(left, 8, 7))
        left = left - split[-1]
    split = jnp.stack(split, axis=2).astype(jnp.bfloat16)
    rows = []
    for k in range(GROUP):
        before, after = k * 3 * ins, (GROUP - 1 - k) * 3 * ins
        row = jnp.pad(taps, ((0, 0), (0, 0), (before, after)))
        rows.append(jnp.concatenate([row, jnp.pad(split, ((0, 0), (0, 0), (0, TAIL - 3)))], axis=2))
    return jnp.concatenate(rows, axis=1)


def pair_call(place, gathered, dist_gain, bands, tile_rows, tile_cols):
    chans = dist_gain.shape[0]
    smem = pl.BlockSpec(memory_space=pltpu.SMEM)
    vmem = pl.BlockSpec(memory_space=pltpu.VMEM)
    span = tile_rows + 6 * DMAX2
    return pl.pallas_call(
        functools.partial(pair_kernel, gathered.shape[0], place.shape[0] - 3),
        out_shape=jax.ShapeDtypeStruct((chans, tile_rows, tile_cols), jnp.bfloat16),
        in_specs=[smem] + [vmem] * 3,
        out_specs=pl.BlockSpec(memory_space=pltpu.HBM),
        scratch_shapes=[
            pltpu.VMEM((4, chans, 128), jnp.float32),
            pltpu.VMEM((span, LANES), jnp.float32),
            pltpu.VMEM((span, 3 * chans, LANES), jnp.bfloat16),
            pltpu.VMEM((span - 2 * DMAX2, 3 * chans, LANES), jnp.bfloat16),
            pltpu.VMEM((tile_rows * PITCH, 128), jnp.float32),
            pltpu.VMEM((GROUP * chans, WIDE * LANES), jnp.float32),
            pltpu.VMEM((chans, tile_rows, tile_cols), jnp.bfloat16),
            pltpu.SemaphoreType.DMA((tile_rows // CHUNK,)),
        ],
        compiler_params=pltpu.CompilerParams(vmem_limit_bytes=48 * 2**20),
        cost_estimate=pl.CostEstimate(
            flops=3 * 2 * tile_rows * 9 * chans * chans * LANES,
            bytes_accessed=tile_rows * tile_cols * chans * 2,
            transcendentals=0,
        ),
        name="pair_tower",
    )(
        place, gathered, dist_gain.reshape(chans, 1), bands,
    )


def on_device(
    features,
    tower_weight,
    tower_bias,
    pair_proj,
    dist_gain,
    map_weight,
    map_bias,
    dilations,
    start_bin,
):
    row_count = lax.axis_size("rows")
    col_count = lax.axis_size("cols")
    shards = row_count * col_count
    shard, width = features.shape
    total = shard * shards
    tile_rows = total // row_count
    tile_cols = total // col_count
    chans = map_weight.shape[-1]
    row_place = lax.axis_index("rows")
    col_place = lax.axis_index("cols")
    mine = row_place * col_count + col_place
    place = jnp.stack([mine, row_place, col_place, row_count, col_count]).astype(jnp.int32)
    place = jnp.concatenate([place, dilations])

    inner = [(i, i ^ 1) for i in range(shards)]
    outer = [(i, i + 1 if i % 2 else i - 1) for i in range(1, shards - 1)]
    brought = lax.ppermute(features, AXES, inner)
    brought, start_bin = lax.optimization_barrier((brought, start_bin))
    both = jnp.concatenate([features, brought], axis=0)
    from_outer = lax.ppermute(both, AXES, outer)
    code = position_code(mine * shard + jnp.arange(shard), start_bin[0], chans)
    code = jnp.pad(code, ((0, 0), (0, width - chans)))
    extra = jnp.concatenate([tower_bias, code], axis=0)
    proj = jnp.pad(pair_proj.T, ((0, 2 * chans), (0, 0)))
    weight = fetch_call(lax.optimization_barrier((tower_weight, both))[0])
    from_outer, extra, proj, place, weight = lax.optimization_barrier(
        (from_outer, extra, proj, place, weight)
    )
    from_inner = lax.ppermute(from_outer, AXES, inner)

    smem = pl.BlockSpec(memory_space=pltpu.SMEM)
    vmem = pl.BlockSpec(memory_space=pltpu.VMEM)
    parts, none_16, none_32 = pl.pallas_call(
        functools.partial(encode_kernel, total),
        out_shape=[
            jax.ShapeDtypeStruct((shards, shard // 2, 4 * chans), jnp.bfloat16),
            jax.ShapeDtypeStruct(map_weight.shape, map_weight.dtype),
            jax.ShapeDtypeStruct((map_bias.shape[0] + 1, chans), jnp.float32),
        ],
        in_specs=[smem] + [vmem] * 6,
        out_specs=[vmem] * 3,
        scratch_shapes=[
            pltpu.VMEM((width // 128, 5 * shard, 128), jnp.float32),
            pltpu.VMEM((width // 128, 3 * shard, 128), jnp.float32),
        ],
        compiler_params=pltpu.CompilerParams(vmem_limit_bytes=16 * 2**20),
        cost_estimate=pl.CostEstimate(
            flops=2 * 4 * shard * 3 * width * width,
            bytes_accessed=6 * width * width * 2,
            transcendentals=0,
        ),
        name="encode",
    )(
        place, both, from_outer, from_inner, proj, extra, weight,
    )

    gathered = lax.all_to_all(parts, AXES, split_axis=0, concat_axis=0, tiled=True)

    bands = banded(map_weight + none_16, map_bias + none_32[:-1])
    dist_gain = dist_gain + none_32[-1]

    return pair_call(
        place, gathered, dist_gain, bands, tile_rows, tile_cols
    )


def solution(mesh):
    placed = (P(AXES, None), P(), P(), P(), P(), P(), P(), P(), P())
    return jax.shard_map(
        on_device, mesh=mesh, in_specs=placed, out_specs=P(None, "rows", "cols"), check_vma=False
    )
```

```python
import functools
import math

import jax
import jax.numpy as jnp
from jax import lax
from jax.experimental import pallas as pl
from jax.experimental.pallas import tpu as pltpu
from jax.sharding import PartitionSpec as P

DMAX1 = 16
DMAX2 = 16
GROUP = 4
TAIL = 32
WIDE = 2
UNROLL = (6, 6, 4)
LANES = 256
PITCH = 40
FETCH_LIMIT = 50
CHUNK = 64
OUTSIDE = -1e30
AXES = ("rows", "cols")


def position_code(bin_index, start_pos, map_width):
    half_width = map_width // 2
    position = ((start_pos + bin_index) % 8192).astype(jnp.float32)
    rates = jnp.exp(-jnp.arange(half_width).astype(jnp.float32) * (math.log(1000.0) / half_width))
    phase_angle = position[:, None] * rates[None, :]
    return jnp.concatenate([jnp.cos(phase_angle), jnp.sin(phase_angle)], axis=1)


def fetch_kernel(far, near, arrived):
    copies = [
        pltpu.make_async_copy(far.at[which, tap], near.at[which, tap], arrived.at[which, tap])
        for which in range(far.shape[0])
        for tap in range(far.shape[1])
    ]
    for copy in copies:
        copy.start()
    for copy in copies:
        copy.wait()


def fetch_call(far):
    return pl.pallas_call(
        fetch_kernel,
        out_shape=jax.ShapeDtypeStruct(far.shape, far.dtype),
        in_specs=[pl.BlockSpec(memory_space=pltpu.HBM)],
        out_specs=pl.BlockSpec(memory_space=pltpu.VMEM),
        scratch_shapes=[pltpu.SemaphoreType.DMA(far.shape[:2])],
        compiler_params=pltpu.CompilerParams(vmem_limit_bytes=FETCH_LIMIT * 2**20),
        name="fetch",
    )(far)


def encode_kernel(
    total, place, both, outer, inner, proj, extra, weight, out, none_16, none_32, wide, mid,
):
    count = both.shape[0] // 2
    bias = extra[:2, :]
    chunks = wide.shape[0]

    def keep(ref, first, value):
        for k in range(chunks):
            ref[k, pl.ds(first, value.shape[0]), :] = value[:, k * 128 : (k + 1) * 128]

    def run(ref, first, span):
        return jnp.concatenate([ref[k, pl.ds(first, span), :] for k in range(chunks)], axis=1)

    def layer(which, ref, span):
        running = jnp.zeros((span, chunks * 128), jnp.float32)
        for tap in range(3):
            rows = run(ref, count + (tap - 1) * place[5 + which], span).astype(jnp.bfloat16)
            running += jnp.dot(rows, weight[which, tap], preferred_element_type=jnp.float32)
        return run(ref, count, span) + jnp.maximum(running + bias[which : which + 1, :], 0.0)

    odd = place[0] % 2
    for side, ref, half in ((2, both, 0), (3 - 2 * odd, both, 1), (1 + 2 * odd, outer, 0),
                            (4 * odd, outer, 1), (4 - 4 * odd, inner, 0)):
        first = side * count
        if ref is not both or half:
            first = pl.multiple_of(first, count)
        keep(wide, first, ref[half * count : (half + 1) * count, :].astype(jnp.float32))
    value = layer(0, wide, 3 * count).astype(jnp.bfloat16).astype(jnp.float32)
    index = (place[0] - 1) * count + lax.broadcasted_iota(jnp.int32, value.shape, 0)
    keep(mid, 0, jnp.where((index >= 0) & (index < total), value, 0.0))
    value = layer(1, mid, count)
    parts = lax.dot_general(
        value.astype(jnp.bfloat16),
        proj[...],
        (((1,), (1,)), ((), ())),
        preferred_element_type=jnp.float32,
    )
    parts = (parts + extra[2 : 2 + count, : proj.shape[0]]).astype(jnp.bfloat16)
    parts = parts[:, : proj.shape[0] // 2]
    parts = jnp.concatenate([parts[: count // 2], parts[count // 2 :]], axis=1)
    out[...] = jnp.broadcast_to(parts[None], out.shape)
    none_16[...] = jnp.zeros(none_16.shape, none_16.dtype)
    none_32[...] = jnp.zeros(none_32.shape, none_32.dtype)


def local_columns(rows):
    lane = lax.broadcasted_iota(jnp.int32, (rows, LANES), 1)
    return jnp.where(lane < LANES - 3 * DMAX2 - 8, lane, lane - LANES)


def pair_kernel(
    total_shards, first_dil, place, parts, gain, weight, out_far,
    row_turned, distance, field_a, field_b, final, held, out, sent,
):
    shard = 2 * parts.shape[1]
    chans = gain.shape[0]
    tile_rows = out.shape[1]
    margin = 3 * DMAX2
    reach = margin // shard
    row_place, col_place = place[1], place[2]
    last_row = place[3] - 1
    row_first = row_place * tile_rows
    col_first = col_place * 128
    dils = [place[first_dil + k] for k in range(3)]

    def pieces(first, count, wrap):
        taken = []
        for k in range(count):
            step = k - count if k >= wrap else k
            both = parts[jnp.clip(first + step, 0, total_shards - 1)]
            taken += [both[:, : 2 * chans], both[:, 2 * chans :]]
        return jnp.concatenate(taken, axis=0).astype(jnp.float32)

    col_glob = col_first + local_columns(1)
    inside = (col_glob >= 0) & (col_glob < total_shards * shard)
    inside_high = jnp.where(inside[:, 128:], 1.0, 0.0)
    inside_high = jnp.broadcast_to(inside_high, (chans, 128)).astype(jnp.bfloat16)

    cols = pieces(col_first // shard, LANES // shard, LANES // shard - reach)
    col_turned = jnp.transpose(cols)[chans : 2 * chans, :]
    col_turned = jnp.where(inside, col_turned, OUTSIDE)
    span0 = tile_rows + 2 * margin
    count = -(-span0 // shard)
    half = shard // 2
    rows = [
        parts[jnp.clip(row_first // shard - reach + k, 0, total_shards - 1)] for k in range(count)
    ]
    rows = jnp.transpose(jnp.concatenate(rows, axis=0).astype(jnp.float32))
    spot = lax.broadcasted_iota(jnp.int32, (1, count * half), 1)
    for side in range(2):
        row_glob = row_first - margin + spot // half * shard + side * half + spot % half
        valid = (row_glob >= 0) & (row_glob < total_shards * shard)
        turned = rows[side * 2 * chans : (side * 2 + 1) * chans, :]
        turned = jnp.where(valid, turned, OUTSIDE)
        row_turned[2 * side] = turned[:, :128]
        row_turned[2 * side + 1, :, : count * half - 128] = turned[:, 128:]

    row_local = lax.broadcasted_iota(jnp.int32, (span0, LANES), 0) - margin
    apart = jnp.abs(row_first + row_local - col_glob)
    distance[...] = jnp.log(1.0 + apart.astype(jnp.float32)) * 0.125
    gain_wide = jnp.broadcast_to(gain[...], (chans, LANES))
    lane16 = lax.broadcasted_iota(jnp.int16, (chans, 128), 1)

    def keep(field, d, masked, narrow=False):
        back = 128 - d
        at_left = lane16 < d.astype(jnp.int16)
        at_right = lane16 >= back.astype(jnp.int16)

        def store(i, low, high):
            low = low.astype(jnp.bfloat16)
            high = high.astype(jnp.bfloat16)
            if masked:
                high = high * inside_high
            field[i, chans : 2 * chans, :128] = low
            turned_low, turned_high = pltpu.roll(low, d, 1), pltpu.roll(high, d, 1)
            field[i, :chans, :128] = jnp.where(at_left, turned_high, turned_low)
            if not narrow:
                field[i, chans : 2 * chans, 128:] = high
                field[i, :chans, 128:] = jnp.where(at_left, turned_low, turned_high)
            turned_low, turned_high = pltpu.roll(low, back, 1), pltpu.roll(high, back, 1)
            field[i, 2 * chans :, :128] = jnp.where(at_right, turned_high, turned_low)
            if not narrow:
                field[i, 2 * chans :, 128:] = jnp.where(at_right, turned_low, turned_high)

        return store

    def clear(field, extra):
        @pl.when(row_place == 0)
        def _():
            @pl.loop(0, extra)
            def _(i):
                field[i] = jnp.zeros(field.shape[1:], field.dtype)

        @pl.when(row_place == last_row)
        def _():
            @pl.loop(0, extra)
            def _(i):
                field[extra + tile_rows + i] = jnp.zeros(field.shape[1:], field.dtype)

    need = dils[0] + dils[1] + dils[2]
    store_first = keep(field_a, dils[0], False)
    first_row, last_row_needed = margin - need, margin + tile_rows + need - 1

    @pl.loop(first_row // shard, last_row_needed // shard + 1)
    def _(block):
        first = pl.multiple_of(block * shard, shard)
        spot = block * half
        apart = distance[pl.ds(first, shard), :]
        for k in range(shard):
            turned = row_turned[k // half * 2 + spot // 128]
            pick = jnp.full((chans, 128), spot % 128 + k % half, jnp.int32)
            row_term = jnp.take_along_axis(turned, pick, axis=1)
            row_term = jnp.concatenate([row_term, row_term], axis=1)
            value = row_term + col_turned + gain_wide * apart[k : k + 1, :]
            value = jnp.maximum(value, 0.0)
            store_first(first + k, value[:, :128], value[:, 128:])

    tail = jnp.ones((TAIL, WIDE * LANES), jnp.bfloat16)

    def tower(layer, source, extra, need, store, first_in_step=None):
        d = dils[layer]
        span = GROUP * d
        first = extra - need
        count = tile_rows + 2 * need
        final_layer = layer == 2
        width = 128 if final_layer else LANES
        each = WIDE * LANES // width

        def product(bases):
            taps = []
            for k in range(GROUP + 2):
                at = [base + DMAX2 + (k - 1) * d for base in bases]
                taps.append(jnp.concatenate([source[i, :, :width] for i in at], axis=1))
            stack = jnp.concatenate(taps + [tail], axis=0)
            return jnp.dot(weight[layer], stack, preferred_element_type=jnp.float32)

        def finish(bases, sums):
            for n, base in enumerate(bases):
                for k in range(GROUP):
                    at = slice(n * width, (n + 1) * width)
                    center = source[base + DMAX2 + k * d, chans : 2 * chans, :width]
                    value = sums[k * chans : (k + 1) * chans, at]
                    if final_layer:
                        value = center.astype(jnp.float32) + jnp.maximum(value, 0.0)
                        store(base + k * d, value)
                    else:
                        value = center + jnp.maximum(value.astype(jnp.bfloat16), 0)
                        store(base + k * d, value[:, :128], value[:, 128:])

        def walk(start, phase):
            bases = []
            for _ in range(each):
                bases.append(first + jnp.minimum(start, count - span) + phase)
                wrap = phase + 1 >= d
                start = jnp.where(wrap, start + span, start)
                phase = jnp.where(wrap, 0, phase + 1)
            return bases, start, phase

        def step(index, carry):
            start, phase, bases = carry
            if first_in_step is not None:
                first_in_step(index)
            sums = held
            for _ in range(UNROLL[layer]):
                next_bases, start, phase = walk(start, phase)
                next_sums = product(next_bases)
                finish(bases, sums)
                bases, sums = next_bases, next_sums
            held[...] = sums
            return start, phase, bases

        zero = jnp.int32(0)
        total = (count + span - 1) // span * d
        together = UNROLL[layer] * each
        steps = (total + together - 1) // together
        carry = lax.fori_loop(0, steps, step, (zero, zero, walk(zero, zero)[0]))
        finish(carry[2], held)

    def keep_last(i, low):
        final[pl.ds(pl.multiple_of(i * PITCH, 8), chans), :] = low

    def turn(chunk):
        @functools.partial(lax.fori_loop, 0, CHUNK // 16, init_val=0, unroll=True)
        def _(block, carry):
            first = pl.multiple_of(chunk * CHUNK + block * 16, 16)
            for c in range(chans):
                taken = final[pl.ds(first * PITCH + c, 16, stride=PITCH), :]
                out[c, pl.ds(first, 16), :] = taken.astype(jnp.bfloat16)
            return carry

    def send(chunk):
        rows = pl.ds(chunk * CHUNK, CHUNK)
        return pltpu.make_async_copy(out.at[:, rows, :], out_far.at[:, rows, :], sent.at[chunk])

    early = 2

    def turn_early(step):
        turn(jnp.clip(step - 2, 0, early - 1))

    tower(0, field_a, 2 * DMAX2, dils[1] + dils[2], keep(field_b, dils[1], True))
    clear(field_b, 2 * DMAX2)
    tower(1, field_b, DMAX2, dils[2], keep(field_a, dils[2], True, True))
    clear(field_a, DMAX2)
    tower(2, field_a, 0, 0, keep_last, turn_early)

    for k in range(tile_rows // CHUNK):
        if k >= early:
            turn(k)
        send(k).start()
    for k in range(tile_rows // CHUNK):
        send(k).wait()


def banded(map_weight, map_bias):
    layers, _, _, outs, ins = map_weight.shape
    taps = jnp.transpose(map_weight, (0, 3, 1, 2, 4)).reshape(layers, outs, 9 * ins)
    left = map_bias
    split = []
    for _ in range(3):
        split.append(lax.reduce_precision(left, 8, 7))
        left = left - split[-1]
    split = jnp.stack(split, axis=2).astype(jnp.bfloat16)
    rows = []
    for k in range(GROUP):
        before, after = k * 3 * ins, (GROUP - 1 - k) * 3 * ins
        row = jnp.pad(taps, ((0, 0), (0, 0), (before, after)))
        rows.append(jnp.concatenate([row, jnp.pad(split, ((0, 0), (0, 0), (0, TAIL - 3)))], axis=2))
    return jnp.concatenate(rows, axis=1)


def pair_call(place, gathered, dist_gain, bands, tile_rows, tile_cols):
    chans = dist_gain.shape[0]
    smem = pl.BlockSpec(memory_space=pltpu.SMEM)
    vmem = pl.BlockSpec(memory_space=pltpu.VMEM)
    span = tile_rows + 6 * DMAX2
    return pl.pallas_call(
        functools.partial(pair_kernel, gathered.shape[0], place.shape[0] - 3),
        out_shape=jax.ShapeDtypeStruct((chans, tile_rows, tile_cols), jnp.bfloat16),
        in_specs=[smem] + [vmem] * 3,
        out_specs=pl.BlockSpec(memory_space=pltpu.HBM),
        scratch_shapes=[
            pltpu.VMEM((4, chans, 128), jnp.float32),
            pltpu.VMEM((span, LANES), jnp.float32),
            pltpu.VMEM((span, 3 * chans, LANES), jnp.bfloat16),
            pltpu.VMEM((span - 2 * DMAX2, 3 * chans, LANES), jnp.bfloat16),
            pltpu.VMEM((tile_rows * PITCH, 128), jnp.float32),
            pltpu.VMEM((GROUP * chans, WIDE * LANES), jnp.float32),
            pltpu.VMEM((chans, tile_rows, tile_cols), jnp.bfloat16),
            pltpu.SemaphoreType.DMA((tile_rows // CHUNK,)),
        ],
        compiler_params=pltpu.CompilerParams(vmem_limit_bytes=48 * 2**20),
        cost_estimate=pl.CostEstimate(
            flops=3 * 2 * tile_rows * 9 * chans * chans * LANES,
            bytes_accessed=tile_rows * tile_cols * chans * 2,
            transcendentals=0,
        ),
        name="pair_tower",
    )(
        place, gathered, dist_gain.reshape(chans, 1), bands,
    )


def on_device(
    features,
    tower_weight,
    tower_bias,
    pair_proj,
    dist_gain,
    map_weight,
    map_bias,
    dilations,
    start_bin,
):
    row_count = lax.axis_size("rows")
    col_count = lax.axis_size("cols")
    shards = row_count * col_count
    shard, width = features.shape
    total = shard * shards
    tile_rows = total // row_count
    tile_cols = total // col_count
    chans = map_weight.shape[-1]
    row_place = lax.axis_index("rows")
    col_place = lax.axis_index("cols")
    mine = row_place * col_count + col_place
    place = jnp.stack([mine, row_place, col_place, row_count, col_count]).astype(jnp.int32)
    place = jnp.concatenate([place, dilations])

    inner = [(i, i ^ 1) for i in range(shards)]
    outer = [(i, i + 1 if i % 2 else i - 1) for i in range(1, shards - 1)]
    brought = lax.ppermute(features, AXES, inner)
    brought, start_bin = lax.optimization_barrier((brought, start_bin))
    both = jnp.concatenate([features, brought], axis=0)
    from_outer = lax.ppermute(both, AXES, outer)
    code = position_code(mine * shard + jnp.arange(shard), start_bin[0], chans)
    code = jnp.pad(code, ((0, 0), (0, width - chans)))
    extra = jnp.concatenate([tower_bias, code], axis=0)
    proj = jnp.pad(pair_proj.T, ((0, 2 * chans), (0, 0)))
    weight = fetch_call(lax.optimization_barrier((tower_weight, both))[0])
    from_outer, extra, proj, place, weight = lax.optimization_barrier(
        (from_outer, extra, proj, place, weight)
    )
    from_inner = lax.ppermute(from_outer, AXES, inner)

    smem = pl.BlockSpec(memory_space=pltpu.SMEM)
    vmem = pl.BlockSpec(memory_space=pltpu.VMEM)
    parts, none_16, none_32 = pl.pallas_call(
        functools.partial(encode_kernel, total),
        out_shape=[
            jax.ShapeDtypeStruct((shards, shard // 2, 4 * chans), jnp.bfloat16),
            jax.ShapeDtypeStruct(map_weight.shape, map_weight.dtype),
            jax.ShapeDtypeStruct((map_bias.shape[0] + 1, chans), jnp.float32),
        ],
        in_specs=[smem] + [vmem] * 6,
        out_specs=[vmem] * 3,
        scratch_shapes=[
            pltpu.VMEM((width // 128, 5 * shard, 128), jnp.float32),
            pltpu.VMEM((width // 128, 3 * shard, 128), jnp.float32),
        ],
        compiler_params=pltpu.CompilerParams(vmem_limit_bytes=16 * 2**20),
        cost_estimate=pl.CostEstimate(
            flops=2 * 4 * shard * 3 * width * width,
            bytes_accessed=6 * width * width * 2,
            transcendentals=0,
        ),
        name="encode",
    )(
        place, both, from_outer, from_inner, proj, extra, weight,
    )

    gathered = lax.all_to_all(parts, AXES, split_axis=0, concat_axis=0, tiled=True)

    bands = banded(map_weight + none_16, map_bias + none_32[:-1])
    dist_gain = dist_gain + none_32[-1]

    return pair_call(
        place, gathered, dist_gain, bands, tile_rows, tile_cols
    )


def solution(mesh):
    placed = (P(AXES, None), P(), P(), P(), P(), P(), P(), P(), P())
    return jax.shard_map(
        on_device, mesh=mesh, in_specs=placed, out_specs=P(None, "rows", "cols"), check_vma=False
    )
```

```python
import functools
import math

import jax
import jax.numpy as jnp
from jax import lax
from jax.experimental import pallas as pl
from jax.experimental.pallas import tpu as pltpu
from jax.sharding import PartitionSpec as P

DMAX1 = 16
DMAX2 = 16
GROUP = 4
TAIL = 32
WIDE = 2
UNROLL = (6, 6, 4)
LANES = 256
PITCH = 40
FETCH_LIMIT = 50
CHUNK = 64
OUTSIDE = -1e30
AXES = ("rows", "cols")


def position_code(bin_index, start_pos, map_width):
    half_width = map_width // 2
    position = ((start_pos + bin_index) % 8192).astype(jnp.float32)
    rates = jnp.exp(-jnp.arange(half_width).astype(jnp.float32) * (math.log(1000.0) / half_width))
    phase_angle = position[:, None] * rates[None, :]
    return jnp.concatenate([jnp.cos(phase_angle), jnp.sin(phase_angle)], axis=1)


def fetch_kernel(far, near, arrived):
    copies = [
        pltpu.make_async_copy(far.at[which, tap], near.at[which, tap], arrived.at[which, tap])
        for which in range(far.shape[0])
        for tap in range(far.shape[1])
    ]
    for copy in copies:
        copy.start()
    for copy in copies:
        copy.wait()


def fetch_call(far):
    return pl.pallas_call(
        fetch_kernel,
        out_shape=jax.ShapeDtypeStruct(far.shape, far.dtype),
        in_specs=[pl.BlockSpec(memory_space=pltpu.HBM)],
        out_specs=pl.BlockSpec(memory_space=pltpu.VMEM),
        scratch_shapes=[pltpu.SemaphoreType.DMA(far.shape[:2])],
        compiler_params=pltpu.CompilerParams(vmem_limit_bytes=FETCH_LIMIT * 2**20),
        name="fetch",
    )(far)


def encode_kernel(
    total, place, both, outer, inner, proj, extra, weight, out, none_16, none_32, wide, mid,
):
    count = both.shape[0] // 2
    bias = extra[:2, :]
    chunks = wide.shape[0]

    def keep(ref, first, value):
        for k in range(chunks):
            ref[k, pl.ds(first, value.shape[0]), :] = value[:, k * 128 : (k + 1) * 128]

    def run(ref, first, span):
        return jnp.concatenate([ref[k, pl.ds(first, span), :] for k in range(chunks)], axis=1)

    def layer(which, ref, span):
        running = jnp.zeros((span, chunks * 128), jnp.float32)
        for tap in range(3):
            rows = run(ref, count + (tap - 1) * place[5 + which], span).astype(jnp.bfloat16)
            running += jnp.dot(rows, weight[which, tap], preferred_element_type=jnp.float32)
        return run(ref, count, span) + jnp.maximum(running + bias[which : which + 1, :], 0.0)

    odd = place[0] % 2
    for side, ref, half in ((2, both, 0), (3 - 2 * odd, both, 1), (1 + 2 * odd, outer, 0),
                            (4 * odd, outer, 1), (4 - 4 * odd, inner, 0)):
        first = side * count
        if ref is not both or half:
            first = pl.multiple_of(first, count)
        keep(wide, first, ref[half * count : (half + 1) * count, :].astype(jnp.float32))
    value = layer(0, wide, 3 * count).astype(jnp.bfloat16).astype(jnp.float32)
    index = (place[0] - 1) * count + lax.broadcasted_iota(jnp.int32, value.shape, 0)
    keep(mid, 0, jnp.where((index >= 0) & (index < total), value, 0.0))
    value = layer(1, mid, count)
    parts = lax.dot_general(
        value.astype(jnp.bfloat16),
        proj[...],
        (((1,), (1,)), ((), ())),
        preferred_element_type=jnp.float32,
    )
    parts = (parts + extra[2 : 2 + count, : proj.shape[0]]).astype(jnp.bfloat16)
    parts = parts[:, : proj.shape[0] // 2]
    parts = jnp.concatenate([parts[: count // 2], parts[count // 2 :]], axis=1)
    out[...] = jnp.broadcast_to(parts[None], out.shape)
    none_16[...] = jnp.zeros(none_16.shape, none_16.dtype)
    none_32[...] = jnp.zeros(none_32.shape, none_32.dtype)


def local_columns(rows):
    lane = lax.broadcasted_iota(jnp.int32, (rows, LANES), 1)
    return jnp.where(lane < LANES - 3 * DMAX2 - 8, lane, lane - LANES)


def pair_kernel(
    total_shards, first_dil, place, parts, gain, weight, out_far,
    row_turned, distance, field_a, field_b, final, held, out, sent,
):
    shard = 2 * parts.shape[1]
    chans = gain.shape[0]
    tile_rows = out.shape[1]
    margin = 3 * DMAX2
    reach = margin // shard
    row_place, col_place = place[1], place[2]
    last_row = place[3] - 1
    row_first = row_place * tile_rows
    col_first = col_place * 128
    dils = [place[first_dil + k] for k in range(3)]

    def pieces(first, count, wrap):
        taken = []
        for k in range(count):
            step = k - count if k >= wrap else k
            both = parts[jnp.clip(first + step, 0, total_shards - 1)]
            taken += [both[:, : 2 * chans], both[:, 2 * chans :]]
        return jnp.concatenate(taken, axis=0).astype(jnp.float32)

    col_glob = col_first + local_columns(1)
    inside = (col_glob >= 0) & (col_glob < total_shards * shard)
    inside_high = jnp.where(inside[:, 128:], 1.0, 0.0)
    inside_high = jnp.broadcast_to(inside_high, (chans, 128)).astype(jnp.bfloat16)

    cols = pieces(col_first // shard, LANES // shard, LANES // shard - reach)
    col_turned = jnp.transpose(cols)[chans : 2 * chans, :]
    col_turned = jnp.where(inside, col_turned, OUTSIDE)
    span0 = tile_rows + 2 * margin
    count = -(-span0 // shard)
    half = shard // 2
    rows = [
        parts[jnp.clip(row_first // shard - reach + k, 0, total_shards - 1)] for k in range(count)
    ]
    rows = jnp.transpose(jnp.concatenate(rows, axis=0).astype(jnp.float32))
    spot = lax.broadcasted_iota(jnp.int32, (1, count * half), 1)
    for side in range(2):
        row_glob = row_first - margin + spot // half * shard + side * half + spot % half
        valid = (row_glob >= 0) & (row_glob < total_shards * shard)
        turned = rows[side * 2 * chans : (side * 2 + 1) * chans, :]
        turned = jnp.where(valid, turned, OUTSIDE)
        row_turned[2 * side] = turned[:, :128]
        row_turned[2 * side + 1, :, : count * half - 128] = turned[:, 128:]

    row_local = lax.broadcasted_iota(jnp.int32, (span0, LANES), 0) - margin
    apart = jnp.abs(row_first + row_local - col_glob)
    distance[...] = jnp.log(1.0 + apart.astype(jnp.float32)) * 0.125
    gain_wide = jnp.broadcast_to(gain[...], (chans, LANES))
    lane16 = lax.broadcasted_iota(jnp.int16, (chans, 128), 1)

    def keep(field, d, masked, narrow=False):
        back = 128 - d
        at_left = lane16 < d.astype(jnp.int16)
        at_right = lane16 >= back.astype(jnp.int16)

        def store(i, low, high):
            low = low.astype(jnp.bfloat16)
            high = high.astype(jnp.bfloat16)
            if masked:
                high = high * inside_high
            field[i, chans : 2 * chans, :128] = low
            turned_low, turned_high = pltpu.roll(low, d, 1), pltpu.roll(high, d, 1)
            field[i, :chans, :128] = jnp.where(at_left, turned_high, turned_low)
            if not narrow:
                field[i, chans : 2 * chans, 128:] = high
                field[i, :chans, 128:] = jnp.where(at_left, turned_low, turned_high)
            turned_low, turned_high = pltpu.roll(low, back, 1), pltpu.roll(high, back, 1)
            field[i, 2 * chans :, :128] = jnp.where(at_right, turned_high, turned_low)
            if not narrow:
                field[i, 2 * chans :, 128:] = jnp.where(at_right, turned_low, turned_high)

        return store

    def clear(field, extra):
        @pl.when(row_place == 0)
        def _():
            @pl.loop(0, extra)
            def _(i):
                field[i] = jnp.zeros(field.shape[1:], field.dtype)

        @pl.when(row_place == last_row)
        def _():
            @pl.loop(0, extra)
            def _(i):
                field[extra + tile_rows + i] = jnp.zeros(field.shape[1:], field.dtype)

    need = dils[0] + dils[1] + dils[2]
    store_first = keep(field_a, dils[0], False)
    first_row, last_row_needed = margin - need, margin + tile_rows + need - 1

    @pl.loop(first_row // 4, last_row_needed // 4 + 1)
    def _(block):
        first = block * 4
        spot = block // 4 * half + block % 2 * 4
        turned = row_turned[block // 2 % 2 * 2 + spot // 128]
        for k in range(4):
            pick = jnp.full((chans, 128), spot % 128 + k, jnp.int32)
            row_term = jnp.take_along_axis(turned, pick, axis=1)
            row_term = jnp.concatenate([row_term, row_term], axis=1)
            value = row_term + col_turned + gain_wide * distance[pl.ds(first + k, 1), :]
            value = jnp.maximum(value, 0.0)
            store_first(first + k, value[:, :128], value[:, 128:])

    tail = jnp.ones((TAIL, WIDE * LANES), jnp.bfloat16)

    def tower(layer, source, extra, need, store, first_in_step=None):
        d = dils[layer]
        span = GROUP * d
        first = extra - need
        count = tile_rows + 2 * need
        final_layer = layer == 2
        width = 128 if final_layer else LANES
        each = WIDE * LANES // width

        def product(bases):
            taps = []
            for k in range(GROUP + 2):
                at = [base + DMAX2 + (k - 1) * d for base in bases]
                taps.append(jnp.concatenate([source[i, :, :width] for i in at], axis=1))
            stack = jnp.concatenate(taps + [tail], axis=0)
            return jnp.dot(weight[layer], stack, preferred_element_type=jnp.float32)

        def finish(bases, sums):
            for n, base in enumerate(bases):
                for k in range(GROUP):
                    at = slice(n * width, (n + 1) * width)
                    center = source[base + DMAX2 + k * d, chans : 2 * chans, :width]
                    value = sums[k * chans : (k + 1) * chans, at]
                    if final_layer:
                        value = center.astype(jnp.float32) + jnp.maximum(value, 0.0)
                        store(base + k * d, value)
                    else:
                        value = center + jnp.maximum(value.astype(jnp.bfloat16), 0)
                        store(base + k * d, value[:, :128], value[:, 128:])

        def walk(start, phase):
            bases = []
            for _ in range(each):
                bases.append(first + jnp.minimum(start, count - span) + phase)
                wrap = phase + 1 >= d
                start = jnp.where(wrap, start + span, start)
                phase = jnp.where(wrap, 0, phase + 1)
            return bases, start, phase

        def step(index, carry):
            start, phase, bases = carry
            if first_in_step is not None:
                first_in_step(index)
            sums = held
            for _ in range(UNROLL[layer]):
                next_bases, start, phase = walk(start, phase)
                next_sums = product(next_bases)
                finish(bases, sums)
                bases, sums = next_bases, next_sums
            held[...] = sums
            return start, phase, bases

        zero = jnp.int32(0)
        total = (count + span - 1) // span * d
        together = UNROLL[layer] * each
        steps = (total + together - 1) // together
        carry = lax.fori_loop(0, steps, step, (zero, zero, walk(zero, zero)[0]))
        finish(carry[2], held)

    def keep_last(i, low):
        final[pl.ds(pl.multiple_of(i * PITCH, 8), chans), :] = low

    def turn(chunk):
        @functools.partial(lax.fori_loop, 0, CHUNK // 16, init_val=0, unroll=True)
        def _(block, carry):
            first = pl.multiple_of(chunk * CHUNK + block * 16, 16)
            for c in range(chans):
                taken = final[pl.ds(first * PITCH + c, 16, stride=PITCH), :]
                out[c, pl.ds(first, 16), :] = taken.astype(jnp.bfloat16)
            return carry

    def send(chunk):
        rows = pl.ds(chunk * CHUNK, CHUNK)
        return pltpu.make_async_copy(out.at[:, rows, :], out_far.at[:, rows, :], sent.at[chunk])

    early = 2

    def turn_early(step):
        turn(jnp.clip(step - 2, 0, early - 1))

    tower(0, field_a, 2 * DMAX2, dils[1] + dils[2], keep(field_b, dils[1], True))
    clear(field_b, 2 * DMAX2)
    tower(1, field_b, DMAX2, dils[2], keep(field_a, dils[2], True, True))
    clear(field_a, DMAX2)
    tower(2, field_a, 0, 0, keep_last, turn_early)

    for k in range(tile_rows // CHUNK):
        if k >= early:
            turn(k)
        send(k).start()
    for k in range(tile_rows // CHUNK):
        send(k).wait()


def banded(map_weight, map_bias):
    layers, _, _, outs, ins = map_weight.shape
    taps = jnp.transpose(map_weight, (0, 3, 1, 2, 4)).reshape(layers, outs, 9 * ins)
    left = map_bias
    split = []
    for _ in range(3):
        split.append(lax.reduce_precision(left, 8, 7))
        left = left - split[-1]
    split = jnp.stack(split, axis=2).astype(jnp.bfloat16)
    rows = []
    for k in range(GROUP):
        before, after = k * 3 * ins, (GROUP - 1 - k) * 3 * ins
        row = jnp.pad(taps, ((0, 0), (0, 0), (before, after)))
        rows.append(jnp.concatenate([row, jnp.pad(split, ((0, 0), (0, 0), (0, TAIL - 3)))], axis=2))
    return jnp.concatenate(rows, axis=1)


def pair_call(place, gathered, dist_gain, bands, tile_rows, tile_cols):
    chans = dist_gain.shape[0]
    smem = pl.BlockSpec(memory_space=pltpu.SMEM)
    vmem = pl.BlockSpec(memory_space=pltpu.VMEM)
    span = tile_rows + 6 * DMAX2
    return pl.pallas_call(
        functools.partial(pair_kernel, gathered.shape[0], place.shape[0] - 3),
        out_shape=jax.ShapeDtypeStruct((chans, tile_rows, tile_cols), jnp.bfloat16),
        in_specs=[smem] + [vmem] * 3,
        out_specs=pl.BlockSpec(memory_space=pltpu.HBM),
        scratch_shapes=[
            pltpu.VMEM((4, chans, 128), jnp.float32),
            pltpu.VMEM((span, LANES), jnp.float32),
            pltpu.VMEM((span, 3 * chans, LANES), jnp.bfloat16),
            pltpu.VMEM((span - 2 * DMAX2, 3 * chans, LANES), jnp.bfloat16),
            pltpu.VMEM((tile_rows * PITCH, 128), jnp.float32),
            pltpu.VMEM((GROUP * chans, WIDE * LANES), jnp.float32),
            pltpu.VMEM((chans, tile_rows, tile_cols), jnp.bfloat16),
            pltpu.SemaphoreType.DMA((tile_rows // CHUNK,)),
        ],
        compiler_params=pltpu.CompilerParams(vmem_limit_bytes=48 * 2**20),
        cost_estimate=pl.CostEstimate(
            flops=3 * 2 * tile_rows * 9 * chans * chans * LANES,
            bytes_accessed=tile_rows * tile_cols * chans * 2,
            transcendentals=0,
        ),
        name="pair_tower",
    )(
        place, gathered, dist_gain.reshape(chans, 1), bands,
    )


def on_device(
    features,
    tower_weight,
    tower_bias,
    pair_proj,
    dist_gain,
    map_weight,
    map_bias,
    dilations,
    start_bin,
):
    row_count = lax.axis_size("rows")
    col_count = lax.axis_size("cols")
    shards = row_count * col_count
    shard, width = features.shape
    total = shard * shards
    tile_rows = total // row_count
    tile_cols = total // col_count
    chans = map_weight.shape[-1]
    row_place = lax.axis_index("rows")
    col_place = lax.axis_index("cols")
    mine = row_place * col_count + col_place
    place = jnp.stack([mine, row_place, col_place, row_count, col_count]).astype(jnp.int32)
    place = jnp.concatenate([place, dilations])

    inner = [(i, i ^ 1) for i in range(shards)]
    outer = [(i, i + 1 if i % 2 else i - 1) for i in range(1, shards - 1)]
    brought = lax.ppermute(features, AXES, inner)
    brought, start_bin = lax.optimization_barrier((brought, start_bin))
    both = jnp.concatenate([features, brought], axis=0)
    from_outer = lax.ppermute(both, AXES, outer)
    code = position_code(mine * shard + jnp.arange(shard), start_bin[0], chans)
    code = jnp.pad(code, ((0, 0), (0, width - chans)))
    extra = jnp.concatenate([tower_bias, code], axis=0)
    proj = jnp.pad(pair_proj.T, ((0, 2 * chans), (0, 0)))
    weight = fetch_call(lax.optimization_barrier((tower_weight, both))[0])
    from_outer, extra, proj, place, weight = lax.optimization_barrier(
        (from_outer, extra, proj, place, weight)
    )
    from_inner = lax.ppermute(from_outer, AXES, inner)

    smem = pl.BlockSpec(memory_space=pltpu.SMEM)
    vmem = pl.BlockSpec(memory_space=pltpu.VMEM)
    parts, none_16, none_32 = pl.pallas_call(
        functools.partial(encode_kernel, total),
        out_shape=[
            jax.ShapeDtypeStruct((shards, shard // 2, 4 * chans), jnp.bfloat16),
            jax.ShapeDtypeStruct(map_weight.shape, map_weight.dtype),
            jax.ShapeDtypeStruct((map_bias.shape[0] + 1, chans), jnp.float32),
        ],
        in_specs=[smem] + [vmem] * 6,
        out_specs=[vmem] * 3,
        scratch_shapes=[
            pltpu.VMEM((width // 128, 5 * shard, 128), jnp.float32),
            pltpu.VMEM((width // 128, 3 * shard, 128), jnp.float32),
        ],
        compiler_params=pltpu.CompilerParams(vmem_limit_bytes=16 * 2**20),
        cost_estimate=pl.CostEstimate(
            flops=2 * 4 * shard * 3 * width * width,
            bytes_accessed=6 * width * width * 2,
            transcendentals=0,
        ),
        name="encode",
    )(
        place, both, from_outer, from_inner, proj, extra, weight,
    )

    gathered = lax.all_to_all(parts, AXES, split_axis=0, concat_axis=0, tiled=True)

    bands = banded(map_weight + none_16, map_bias + none_32[:-1])
    dist_gain = dist_gain + none_32[-1]

    return pair_call(
        place, gathered, dist_gain, bands, tile_rows, tile_cols
    )


def solution(mesh):
    placed = (P(AXES, None), P(), P(), P(), P(), P(), P(), P(), P())
    return jax.shard_map(
        on_device, mesh=mesh, in_specs=placed, out_specs=P(None, "rows", "cols"), check_vma=False
    )
```
